32 devices in a mesh: ctx: 8 (over y, x, core), kv: 4 (over z).
Axes of the slice: x: 2, y: 2, z: 4, core: 2. Of those that a mesh axis runs over, the one named last changes fastest.
Arguments:
- new_tokens: float32 [2, 16384], P(None, 'ctx'), may hold values from -3 to 3
- ctx_hidden: bfloat16 [1, 2560, 16384], P(None, 'ctx'), may hold values from -200 to 200
- norm_gain: float32 [1, 16384], replicated, may hold values from 0.1 to 1.9
- query_weight: bfloat16 [1, 16384, 4096], P(None, 'ctx', 'kv'), may hold values from -9 to 9
- key_weight: bfloat16 [1, 16384, 512], P(None, 'ctx', 'kv'), may hold values from -9 to 9
- value_weight: bfloat16 [1, 16384, 512], P(None, 'ctx', 'kv'), may hold values from -0.046875 to 0.046875
- out_weight: bfloat16 [1, 4096, 16384], P(None, 'kv', 'ctx'), may hold values from -0.09375 to 0.09375
- lengths: int32 [2], replicated, may hold values from 320 to 1280, as said below
- positions: int32 [2], replicated, may hold values from 320 to 2559, as said below
Outputs:
- hidden_out: float32 [2, 16384], P(None, 'ctx')
The draws below stay inside these ranges and needn't reach their ends.
Inputs may be any that keep to these rules, and one draw needn't show every extreme that they name: `lengths`: one request's length equals 1280. lengths[r] <= positions[r] < lengths[r] + 1280 for every request.
All inputs are finite; a program needn't handle non-finite values.
Results may differ from the reference program's by a relative error of at most 0.0045.
The reference program's roundings to bfloat16 on the way (of `normed`, `queries`, `self_key`, `ctx_normed`, `ctx_keys`, `weights` and `attended`) count: a program that leaves them out, or rounds other values in their place, can miss the bound.
Values may be sent and summed in bfloat16 or wider, within the bound.
No kernel may reach another device: no remote copies, remote signals or barrier semaphores. Data moves between devices by JAX's collectives and lax.ppermute only.
A program may use at most 128 MiB of HBM per device.

```python
import math
import jax
import jax.numpy as jnp
from jax import lax

D = 16384
HEAD = 128
GROUP = 8
LAYERS = 1
REQS = 2
KV_HEADS = 4
HEADS = 32
CONTEXT = 2560
SLOTS = 1280


def request_lengths(key):
    key = jax.random.fold_in(key, 3)
    first_key, second_key = jax.random.split(key)
    drawn = jax.random.randint(first_key, (REQS,), SLOTS // 4, SLOTS + 1)
    full_one = jax.random.randint(second_key, (), 0, REQS)
    return jnp.where(jnp.arange(REQS, dtype=jnp.int32) == full_one, SLOTS, drawn).astype(jnp.int32)


def shared_parts(key):
    base = jnp.clip(jax.random.normal(jax.random.fold_in(key, 7), (LAYERS, D, KV_HEADS * HEAD), jnp.float32), -4.0, 4.0)
    column = jnp.exp(jax.random.uniform(jax.random.fold_in(key, 13), (LAYERS, 1, D), jnp.float32) * math.log(10.0))
    return (base, column)


def draw_lengths(key, part):
    return request_lengths(key)


def draw_positions(key, part):
    lengths = request_lengths(key)
    key = jax.random.fold_in(key, 5)
    gaps = jax.random.randint(key, (REQS,), 0, SLOTS)
    gaps = jnp.where(lengths == SLOTS, SLOTS - 1, gaps)
    return (lengths + gaps).astype(jnp.int32)


def draw_new_tokens(key, part):
    key = jax.random.fold_in(key, 41)
    values = jnp.clip(jax.random.normal(key, (REQS, D), jnp.float32), -6.0, 6.0) * 0.3
    return values


def draw_ctx_hidden(key, part):
    base, column = shared_parts(key)
    key = jax.random.fold_in(key, 11)
    row_key, main_key = jax.random.split(key, 2)
    row_scale = jnp.exp(jax.random.uniform(row_key, (LAYERS, CONTEXT, 1), jnp.float32) * math.log(10.0))
    values = jnp.clip(jax.random.normal(main_key, (LAYERS, CONTEXT, D), jnp.float32), -5.0, 5.0) * row_scale * column
    return (values / 3.0).astype(jnp.bfloat16)


def draw_query_weight(key, part):
    key = jax.random.fold_in(key, 21)
    fresh = jnp.clip(jax.random.normal(key, (LAYERS, D, KV_HEADS, GROUP, HEAD), jnp.float32), -6.0, 6.0)
    return (fresh * D ** (-0.5)).reshape(LAYERS, D, HEADS * HEAD).astype(jnp.bfloat16)


def draw_key_weight(key, part):
    base, column = shared_parts(key)
    return (base * D ** (-0.5)).astype(jnp.bfloat16)


def steps_of(rng, dims, shards, low, top_value):
    factor_of = 1.0
    for position, shards_of in shards:
        steps = jax.random.uniform(jax.random.fold_in(jax.random.fold_in(rng, 6), position), (shards_of,), jnp.float32, low / len(shards), top_value / len(shards))
        factor_of = factor_of * jnp.repeat(jnp.exp(steps), dims[position] // shards_of).reshape((-1,) + (1,) * (len(dims) - 1 - position))
    return factor_of


def noise(own_key, dims, deviation, reach, pieces=(), kind=jnp.bfloat16):
    gain = steps_of(own_key, dims, pieces, -0.22, 0.18) if pieces else 1.0
    values = jax.random.normal(own_key, dims, jnp.float32) * deviation * gain
    return jnp.minimum(jnp.maximum(values, -reach), reach).astype(kind)


def setup_inputs(seed: int = 0) -> dict:
    keys = jax.random.split(jax.random.key(seed), 10)
    return {
        "new_tokens": draw_new_tokens(jax.random.fold_in(keys[9], 71), 0),
        "ctx_hidden": draw_ctx_hidden(jax.random.fold_in(keys[9], 71), 0),
        "norm_gain": jnp.clip(1.0 + 0.18 * jax.random.normal(keys[2], (LAYERS, D), jnp.float32), 0.1, 1.9),
        "query_weight": draw_query_weight(jax.random.fold_in(keys[9], 71), 0),
        "key_weight": draw_key_weight(jax.random.fold_in(keys[9], 71), 0),
        "value_weight": noise(keys[5], (LAYERS, D, KV_HEADS * HEAD), D ** -0.5, 0.046875, ((1, 8), (2, 4))),
        "out_weight": noise(keys[6], (LAYERS, HEADS * HEAD, D), (HEADS * HEAD) ** -0.5, 0.09375, ((1, 4), (2, 8))),
        "lengths": draw_lengths(jax.random.fold_in(keys[9], 71), 0),
        "positions": draw_positions(jax.random.fold_in(keys[9], 71), 0),
    }


ROPE_BASE = 500000.0
EPSILON = 1e-05
FLOOR = -1e+30

def rms_scaled(row_block, gain_row):
    values = row_block.astype(jnp.float32)
    factor = lax.rsqrt(lax.optimization_barrier(jnp.mean(values * values, axis=-1, keepdims=True)) + EPSILON)
    return (values * factor * gain_row).astype(jnp.bfloat16)

def rotary(values, placed):
    half_size = values.shape[-1] // 2
    frequency = jnp.exp(jnp.arange(half_size, dtype=jnp.float32) * (-2.0 * math.log(ROPE_BASE) / values.shape[-1]))
    angles = placed[..., None] * frequency
    cosine = jnp.cos(angles)
    sine_part = jnp.sin(angles)
    leading = values[..., :half_size]
    trailing = values[..., half_size:]
    return jnp.concatenate((leading * cosine - trailing * sine_part, trailing * cosine + leading * sine_part), axis=-1)

def reference(new_tokens, ctx_hidden, norm_gain, query_weight, key_weight, value_weight, out_weight, lengths, positions):
    row_ids = jnp.arange(CONTEXT, dtype=jnp.int32)
    owners = row_ids // SLOTS
    within = row_ids % SLOTS
    request_ids = jnp.arange(REQS, dtype=jnp.int32)
    valid = (owners[None, :] == request_ids[:, None]) & (within[None, :] < lengths[:, None])
    key_places = within.astype(jnp.float32)
    new_places = positions.astype(jnp.float32)
    scale = 1.0 / math.sqrt(HEAD)
    state = new_tokens
    for layer_index in range(LAYERS):
        gain_row = norm_gain[layer_index]
        normed = rms_scaled(state, gain_row)
        queries = jnp.dot(normed, query_weight[layer_index], preferred_element_type=jnp.float32)
        queries = rotary(queries.reshape(REQS, KV_HEADS, GROUP, HEAD), new_places[:, None, None]).astype(jnp.bfloat16)
        self_key = jnp.dot(normed, key_weight[layer_index], preferred_element_type=jnp.float32)
        self_key = rotary(self_key.reshape(REQS, KV_HEADS, HEAD), new_places[:, None]).astype(jnp.bfloat16)
        self_value = jnp.dot(normed, value_weight[layer_index], preferred_element_type=jnp.float32)
        self_value = self_value.reshape(REQS, KV_HEADS, HEAD).astype(jnp.bfloat16)
        ctx_normed = rms_scaled(ctx_hidden[layer_index], gain_row)
        ctx_keys = jnp.dot(ctx_normed, key_weight[layer_index], preferred_element_type=jnp.float32)
        ctx_keys = rotary(ctx_keys.reshape(CONTEXT, KV_HEADS, HEAD), key_places[:, None]).astype(jnp.bfloat16)
        ctx_values = jnp.dot(ctx_normed, value_weight[layer_index], preferred_element_type=jnp.float32)
        ctx_values = ctx_values.reshape(CONTEXT, KV_HEADS, HEAD).astype(jnp.bfloat16)
        scores = jnp.einsum('rkgh,nkh->rkgn', queries.astype(jnp.float32), ctx_keys.astype(jnp.float32)) * scale
        masked = jnp.where(valid[:, None, None, :], scores, FLOOR)
        self_scores = jnp.einsum('rkgh,rkh->rkg', queries.astype(jnp.float32), self_key.astype(jnp.float32)) * scale
        highest = jnp.maximum(lax.optimization_barrier(jnp.max(masked, axis=-1)), self_scores)
        weights = jnp.where(valid[:, None, None, :], jnp.exp(masked - highest[..., None]), 0.0).astype(jnp.bfloat16)
        self_weight = jnp.exp(self_scores - highest).astype(jnp.bfloat16).astype(jnp.float32)
        total_mass = lax.optimization_barrier(jnp.sum(weights.astype(jnp.float32), axis=-1)) + self_weight
        accum = jnp.einsum('rkgn,nkh->rkgh', weights.astype(jnp.float32), ctx_values.astype(jnp.float32))
        accum = accum + self_weight[..., None] * self_value.astype(jnp.float32)[:, :, None, :]
        attended = (accum / total_mass[..., None]).reshape(REQS, HEADS * HEAD).astype(jnp.bfloat16)
        state = state + jnp.dot(attended, out_weight[layer_index], preferred_element_type=jnp.float32)
    return state
```

```python
import math

import jax
import jax.numpy as jnp
from jax import lax
from jax.sharding import PartitionSpec as P

ROPE_BASE = 500000.0
EPSILON = 1e-05
FLOOR = -1e30


def swap(value, axis, distance):
    count = lax.axis_size(axis)
    return lax.ppermute(value, axis, [(i, i ^ distance) for i in range(count)])


def tree(parts, join):
    while len(parts) > 1:
        parts = [join(parts[i], parts[i + 1]) for i in range(0, len(parts), 2)]
    return parts[0]


def pick(values, index):
    return lax.dynamic_index_in_dim(values, index, 0, keepdims=False)


def exchange_all(value, axis, count):
    return [value] + [swap(value, axis, d) for d in range(1, count)]


def rotary(values, placed):
    half_size = values.shape[-1] // 2
    frequency = jnp.exp(
        jnp.arange(half_size, dtype=jnp.float32) * (-2.0 * math.log(ROPE_BASE) / values.shape[-1])
    )
    angles = placed[..., None] * frequency
    cosine = jnp.cos(angles)
    sine_part = jnp.sin(angles)
    leading = values[..., :half_size]
    trailing = values[..., half_size:]
    return jnp.concatenate(
        (leading * cosine - trailing * sine_part, trailing * cosine + leading * sine_part), axis=-1
    )


def gather_blocks(own):
    count = lax.axis_size("ctx")
    rows = own.shape[0]
    held = [[(0, 0, own[: rows // 2])], [(0, rows // 2, own[rows // 2 :])]]
    bits = [1 << b for b in range(1, count.bit_length() - 1)]
    orders = [bits, bits[::-1]]
    for step in range(len(bits)):
        for part in range(2):
            bit = orders[part][step]
            held[part] = held[part] + [
                (d ^ bit, first, swap(block, "ctx", bit)) for d, first, block in held[part]
            ]
    blocks = held[0] + held[1]
    return blocks + [(d ^ 1, first, swap(block, "ctx", 1)) for d, first, block in blocks]


def project(rows_in, blocks, place, width):
    total = None
    for distance, first, block in blocks:
        columns = lax.dynamic_slice_in_dim(
            rows_in, (place ^ distance) * width + first, block.shape[0], 1
        )
        part = jnp.dot(columns, block, preferred_element_type=jnp.float32)
        total = part if total is None else total + part
    return total


def shards(
    new_tokens,
    ctx_hidden,
    norm_gain,
    query_weight,
    key_weight,
    value_weight,
    out_weight,
    lengths,
    positions,
):
    ctx_count = lax.axis_size("ctx")
    kv_count = lax.axis_size("kv")
    place = lax.axis_index("ctx")
    row_count, features = ctx_hidden.shape[1:]
    head_size = key_weight.shape[2]
    heads = query_weight.shape[2] // head_size
    requests, width = new_tokens.shape
    slot_count = row_count * ctx_count // requests
    team = slot_count // row_count
    request = place // team
    scale = 1.0 / math.sqrt(head_size)
    gain_row = norm_gain[0]

    key_blocks = gather_blocks(key_weight[0])
    value_blocks = gather_blocks(value_weight[0])

    squares = jnp.sum(new_tokens * new_tokens, axis=-1)
    squares = tree(exchange_all(squares, "ctx", ctx_count), jnp.add)
    factor = lax.rsqrt(squares / features + EPSILON)[:, None]
    own_gain = lax.dynamic_slice_in_dim(gain_row, place * width, width, 0)
    normed = (new_tokens * factor * own_gain).astype(jnp.bfloat16)
    parts = jnp.concatenate(
        [
            jnp.dot(normed, weight[0], preferred_element_type=jnp.float32)
            for weight in (query_weight, key_weight, value_weight)
        ],
        axis=1,
    ).reshape(requests, heads + 2, head_size)
    summed = tree(
        [pick(parts, request)]
        + [swap(pick(parts, (place ^ d) // team), "ctx", d) for d in range(1, ctx_count)],
        jnp.add,
    )
    new_place = pick(positions, request).astype(jnp.float32)
    turned = rotary(summed[: heads + 1], new_place[None]).astype(jnp.bfloat16)
    queries = turned[:heads]
    self_key = turned[heads]
    self_value = summed[heads + 1].astype(jnp.bfloat16).astype(jnp.float32)
    self_scores = (
        jnp.sum(queries.astype(jnp.float32) * self_key.astype(jnp.float32), axis=-1) * scale
    )

    hidden = ctx_hidden[0].astype(jnp.float32)
    row_factor = lax.rsqrt(jnp.mean(hidden * hidden, axis=-1, keepdims=True) + EPSILON)
    ctx_normed = (hidden * row_factor * gain_row).astype(jnp.bfloat16)
    within = (place % team) * row_count + jnp.arange(row_count, dtype=jnp.int32)
    live = within < pick(lengths, request)
    ctx_keys = rotary(
        project(ctx_normed, key_blocks, place, width), within.astype(jnp.float32)
    ).astype(jnp.bfloat16)
    scores = jnp.einsum("gh,nh->gn", queries, ctx_keys, preferred_element_type=jnp.float32) * scale
    masked = jnp.where(live[None, :], scores, FLOOR)
    top = jnp.maximum(jnp.max(masked, axis=-1), self_scores)
    top = tree(exchange_all(top, "ctx", team), jnp.maximum)
    weights = jnp.where(live[None, :], jnp.exp(masked - top[:, None]), 0.0).astype(jnp.bfloat16)
    self_weight = jnp.exp(self_scores - top).astype(jnp.bfloat16).astype(jnp.float32)
    self_weight = jnp.where(place % team == 0, self_weight, 0.0)
    mass = jnp.sum(weights.astype(jnp.float32), axis=-1) + self_weight
    ctx_values = project(ctx_normed, value_blocks, place, width).astype(jnp.bfloat16)
    accum = jnp.dot(weights, ctx_values, preferred_element_type=jnp.float32)
    accum = accum + self_weight[:, None] * self_value

    packed = jnp.concatenate((accum, jnp.broadcast_to(mass[:, None], accum.shape)), axis=1)
    packed = exchange_all(packed, "ctx", ctx_count)
    sums = jnp.stack(
        [tree(packed[j * team : (j + 1) * team], jnp.add) for j in range(requests)]
    )
    sums = sums[jnp.arange(requests) ^ request]
    attended = (sums[..., :head_size] / sums[..., head_size:]).astype(jnp.bfloat16)
    update = jnp.dot(
        attended.reshape(requests, heads * head_size),
        out_weight[0],
        preferred_element_type=jnp.float32,
    )
    return new_tokens + tree(exchange_all(update, "kv", kv_count), jnp.add)


def solution(mesh):
    in_specs = (
        P(None, "ctx"),
        P(None, "ctx", None),
        P(),
        P(None, "ctx", "kv"),
        P(None, "ctx", "kv"),
        P(None, "ctx", "kv"),
        P(None, "kv", "ctx"),
        P(),
        P(),
    )
    out_specs = P(None, "ctx")
    return jax.shard_map(shards, mesh=mesh, in_specs=in_specs, out_specs=out_specs, check_vma=False)
```

```python
import functools
import math

import jax
import jax.numpy as jnp
from jax import lax
from jax.experimental import pallas as pl
from jax.experimental.pallas import tpu as pltpu
from jax.sharding import PartitionSpec as P

ROPE_BASE = 500000.0
EPSILON = 1e-05
FLOOR = -1e30
VMEM_BYTES = 16 * 1024 * 1024
CHEAP = pl.CostEstimate(flops=1000, bytes_accessed=1000, transcendentals=0)
IN_VMEM = pl.BlockSpec(memory_space=pltpu.VMEM)
IN_SMEM = pl.BlockSpec(memory_space=pltpu.SMEM)
IN_HBM = pl.BlockSpec(memory_space=pltpu.HBM)


def params():
    return pltpu.CompilerParams(vmem_limit_bytes=VMEM_BYTES)


def swap(value, axis, distance):
    count = lax.axis_size(axis)
    return lax.ppermute(value, axis, [(i, i ^ distance) for i in range(count)])


def pick(values, index):
    return lax.dynamic_index_in_dim(values, index, 0, keepdims=False)


def spread(value, axis):
    count = lax.axis_size(axis)
    return lax.all_to_all(jnp.broadcast_to(value[None], (count,) + value.shape), axis, 0, 0)


def rotary(values, placed):
    half_size = values.shape[-1] // 2
    frequency = jnp.exp(
        jnp.arange(half_size, dtype=jnp.float32) * (-2.0 * math.log(ROPE_BASE) / values.shape[-1])
    )
    angles = placed[..., None] * frequency
    cosine = jnp.cos(angles)
    sine_part = jnp.sin(angles)
    leading = values[..., :half_size]
    trailing = values[..., half_size:]
    return jnp.concatenate(
        (leading * cosine - trailing * sine_part, trailing * cosine + leading * sine_part), axis=-1
    )


def norm_kernel(chunk, x_ref, gain_ref, out_ref, sems):
    blocks, rows, width = out_ref.shape
    copies = []
    for c in range(rows // chunk):
        part = pl.ds(c * chunk, chunk)
        copies.append(
            [
                pltpu.make_async_copy(
                    x_ref.at[part, pl.ds(b * width, width)], out_ref.at[b, part, :], sems.at[c, b]
                )
                for b in range(blocks)
            ]
        )
        for copy in copies[-1]:
            copy.start()
    for c in range(rows // chunk):
        part = pl.ds(c * chunk, chunk)
        for copy in copies[c]:
            copy.wait()

        def add_squares(b, total):
            values = out_ref[b, part, :].astype(jnp.float32)
            squares = values * values
            for j in range(width // 128):
                total = total + squares[:, j * 128 : (j + 1) * 128]
            return total

        total = lax.fori_loop(0, blocks, add_squares, jnp.zeros((chunk, 128), jnp.float32))
        mean = jnp.sum(total, axis=-1, keepdims=True) / (blocks * width)
        factor = lax.rsqrt(mean + EPSILON)

        def scale(b, _):
            values = out_ref[b, part, :].astype(jnp.float32)
            out_ref[b, part, :] = (values * factor * gain_ref[b]).astype(jnp.bfloat16)
            return 0

        lax.fori_loop(0, blocks, scale, 0)


def normalise(hidden, gain_row, blocks):
    rows, features = hidden.shape
    width = features // blocks
    chunk = 32
    return pl.pallas_call(
        functools.partial(norm_kernel, chunk),
        in_specs=[IN_HBM, IN_VMEM],
        out_specs=IN_VMEM,
        out_shape=jax.ShapeDtypeStruct((blocks, rows, width), jnp.bfloat16),
        scratch_shapes=[pltpu.SemaphoreType.DMA((rows // chunk, blocks))],
        compiler_params=params(),
        cost_estimate=CHEAP,
        name="normalise",
    )(hidden, gain_row.reshape(blocks, 1, width))


def project_kernel(pieces, has_total, place_ref, rows_ref, *refs):
    place = place_ref[0]
    out_ref = refs[-1]
    total = refs[len(pieces)][...] if has_total else None
    for (distance, first), block_ref in zip(pieces, refs):
        depth = block_ref.shape[0]
        part = jnp.dot(
            rows_ref[place ^ distance, :, first : first + depth],
            block_ref[...],
            preferred_element_type=jnp.float32,
        )
        total = part if total is None else total + part
    out_ref[...] = total


def project(place, rows_in, blocks, total):
    extra = [] if total is None else [total]
    pieces = [(distance, first) for distance, first, _ in blocks]
    return pl.pallas_call(
        functools.partial(project_kernel, pieces, total is not None),
        in_specs=[IN_SMEM] + [IN_VMEM] * (1 + len(blocks) + len(extra)),
        out_specs=IN_VMEM,
        out_shape=jax.ShapeDtypeStruct((rows_in.shape[1], blocks[0][2].shape[1]), jnp.float32),
        compiler_params=params(),
        cost_estimate=CHEAP,
        name="project",
    )(place, rows_in, *[block for _, _, block in blocks], *extra)


def gather_rounds(own):
    count = lax.axis_size("ctx")
    rows = own.shape[0]
    bits = [1 << b for b in range(1, count.bit_length() - 1)]
    rounds = [[(0, 0, own)]] + [[] for _ in bits]
    halves = {}
    for bit in bits:
        block = swap(own, "ctx", bit)
        rounds[1].append((bit, 0, block))
        halves[bit] = (block[: rows // 2], block[rows // 2 :])
    for distance in sorted(range(2, count, 2), key=lambda d: bin(d).count("1")):
        hops = bin(distance).count("1")
        if hops < 2:
            continue
        low = distance & -distance
        high = 1 << (distance.bit_length() - 1)
        halves[distance] = (
            swap(halves[distance ^ high][0], "ctx", high),
            swap(halves[distance ^ low][1], "ctx", low),
        )
        rounds[hops].append((distance, 0, halves[distance][0]))
        rounds[hops].append((distance, rows // 2, halves[distance][1]))
    return [r + [(d ^ 1, first, swap(block, "ctx", 1)) for d, first, block in r] for r in rounds]


def project_all(place, rows_in, rounds):
    total = None
    for blocks in rounds:
        total = project(place, rows_in, blocks, total)
    return total


def shards(
    new_tokens,
    ctx_hidden,
    norm_gain,
    query_weight,
    key_weight,
    value_weight,
    out_weight,
    lengths,
    positions,
):
    ctx_count = lax.axis_size("ctx")
    place = lax.axis_index("ctx")
    places = place.astype(jnp.int32).reshape(1)
    row_count, features = ctx_hidden.shape[1:]
    head_size = key_weight.shape[2]
    heads = query_weight.shape[2] // head_size
    requests, width = new_tokens.shape
    slot_count = row_count * ctx_count // requests
    team = slot_count // row_count
    request = place // team
    scale = 1.0 / math.sqrt(head_size)
    gain_row = norm_gain[0]

    key_rounds = gather_rounds(key_weight[0])
    first_hop = [block for distance, _, block in key_rounds[1] if distance % 2 == 0]
    own_values = lax.optimization_barrier((value_weight[0], *first_hop))[0]
    value_rounds = gather_rounds(own_values)

    squares = jnp.sum(new_tokens * new_tokens, axis=-1)
    squares = spread(jnp.broadcast_to(squares[:, None], (requests, 128)), "ctx")
    factor = lax.rsqrt(jnp.sum(squares, axis=0)[:, :1] / features + EPSILON)
    own_gain = lax.dynamic_slice_in_dim(gain_row, place * width, width, 0)
    normed = (new_tokens * factor * own_gain).astype(jnp.bfloat16)
    parts = jnp.concatenate(
        [
            jnp.dot(normed, weight[0], preferred_element_type=jnp.float32)
            for weight in (query_weight, key_weight, value_weight)
        ],
        axis=1,
    ).reshape(requests, heads + 2, head_size)
    summed = jnp.sum(
        lax.all_to_all(jnp.repeat(parts, team, axis=0), "ctx", 0, 0), axis=0
    )
    new_place = pick(positions, request).astype(jnp.float32)
    turned = rotary(summed[: heads + 1], new_place[None]).astype(jnp.bfloat16)
    queries = turned[:heads]
    self_key = turned[heads]
    self_value = summed[heads + 1].astype(jnp.bfloat16).astype(jnp.float32)
    self_scores = (
        jnp.sum(queries.astype(jnp.float32) * self_key.astype(jnp.float32), axis=-1) * scale
    )

    ctx_normed = normalise(ctx_hidden[0], gain_row, ctx_count)
    within = (place % team) * row_count + jnp.arange(row_count, dtype=jnp.int32)
    live = within < pick(lengths, request)
    keys_raw = project_all(places, ctx_normed, key_rounds)
    ctx_keys = rotary(keys_raw, within.astype(jnp.float32)).astype(jnp.bfloat16)
    scores = jnp.einsum("gh,nh->gn", queries, ctx_keys, preferred_element_type=jnp.float32) * scale
    masked = jnp.where(live[None, :], scores, FLOOR)
    top = jnp.maximum(jnp.max(masked, axis=-1), self_scores)
    tops = spread(jnp.broadcast_to(top[:, None], (heads, 128)), "ctx")
    tops = tops.reshape(requests, team, heads, 128)[:, :, :, 0]
    top = jnp.max(pick(tops, request), axis=0)
    weights = jnp.where(live[None, :], jnp.exp(masked - top[:, None]), 0.0).astype(jnp.bfloat16)
    self_weight = jnp.exp(self_scores - top).astype(jnp.bfloat16).astype(jnp.float32)
    self_weight = jnp.where(place % team == 0, self_weight, 0.0)
    mass = jnp.sum(weights.astype(jnp.float32), axis=-1) + self_weight
    ctx_values = project_all(places, ctx_normed, value_rounds).astype(jnp.bfloat16)
    accum = jnp.dot(weights, ctx_values, preferred_element_type=jnp.float32)
    accum = accum + self_weight[:, None] * self_value

    packed = jnp.concatenate((accum, jnp.broadcast_to(mass[:, None], accum.shape)), axis=1)
    packed = spread(packed, "ctx")
    sums = jnp.sum(packed.reshape((requests, team) + packed.shape[1:]), axis=1)
    attended = (sums[..., :head_size] / sums[..., head_size:]).astype(jnp.bfloat16)
    update = jnp.dot(
        attended.reshape(requests, heads * head_size),
        out_weight[0],
        preferred_element_type=jnp.float32,
    )
    return new_tokens + jnp.sum(spread(update, "kv"), axis=0)


def solution(mesh):
    in_specs = (
        P(None, "ctx"),
        P(None, "ctx", None),
        P(),
        P(None, "ctx", "kv"),
        P(None, "ctx", "kv"),
        P(None, "ctx", "kv"),
        P(None, "kv", "ctx"),
        P(),
        P(),
    )
    out_specs = P(None, "ctx")
    return jax.shard_map(shards, mesh=mesh, in_specs=in_specs, out_specs=out_specs, check_vma=False)
```

```python
import functools
import math

import jax
import jax.numpy as jnp
from jax import lax
from jax.experimental import pallas as pl
from jax.experimental.pallas import tpu as pltpu
from jax.sharding import PartitionSpec as P

ROPE_BASE = 500000.0
EPSILON = 1e-05
FLOOR = -1e30
LANES = 128
NORM_ROWS = 64
VMEM_BYTES = 16 * 1024 * 1024
CHEAP = pl.CostEstimate(flops=1000, bytes_accessed=1000, transcendentals=0)
IN_VMEM = pl.BlockSpec(memory_space=pltpu.VMEM)
IN_SMEM = pl.BlockSpec(memory_space=pltpu.SMEM)
IN_HBM = pl.BlockSpec(memory_space=pltpu.HBM)


def call(kernel, name, in_specs, out_shape, scratch_shapes=()):
    return pl.pallas_call(
        kernel,
        in_specs=in_specs,
        out_specs=jax.tree.map(lambda _: IN_VMEM, out_shape),
        out_shape=out_shape,
        scratch_shapes=scratch_shapes,
        compiler_params=pltpu.CompilerParams(vmem_limit_bytes=VMEM_BYTES),
        cost_estimate=CHEAP,
        name=name,
    )


def shape(dims, dtype=jnp.float32):
    return jax.ShapeDtypeStruct(dims, dtype)


def swap(value, axis, distance):
    count = lax.axis_size(axis)
    return lax.ppermute(value, axis, [(i, i ^ distance) for i in range(count)])


def after(value, *others):
    return lax.optimization_barrier((value, *others))[0]


def bits_below(count):
    return [1 << b for b in range(count.bit_length() - 1)]


def tables(placed, head_size):
    half_size = head_size // 2
    frequency = jnp.exp(
        jnp.arange(half_size, dtype=jnp.float32) * (-2.0 * math.log(ROPE_BASE) / head_size)
    )
    angles = placed[..., None] * frequency
    cosine = jnp.cos(angles)
    sine_part = jnp.sin(angles)
    return (
        jnp.concatenate((cosine, cosine), axis=-1),
        jnp.concatenate((-sine_part, sine_part), axis=-1),
    )


def turn(values, cosine, signed_sine):
    half_size = values.shape[-1] // 2
    swapped = jnp.concatenate((values[:, half_size:], values[:, :half_size]), axis=-1)
    return values * cosine + swapped * signed_sine


def squares_kernel(tokens_ref, out_ref):
    values = tokens_ref[...]
    total = jnp.sum(values * values, axis=-1, keepdims=True)
    out_ref[...] = jnp.broadcast_to(total, out_ref.shape)


def norm_kernel(first, x_ref, gain_ref, out_ref, sems):
    blocks, rows, width = out_ref.shape
    step = 16
    copies = []
    for c in range(rows // step):
        copies.append(
            [
                pltpu.make_async_copy(
                    x_ref.at[pl.ds(first + c * step, step), pl.ds(b * width, width)],
                    out_ref.at[b, pl.ds(c * step, step), :],
                    sems.at[c, b],
                )
                for b in range(blocks)
            ]
        )
        for copy in copies[-1]:
            copy.start()
    for c in range(rows // step):
        part = pl.ds(c * step, step)
        for copy in copies[c]:
            copy.wait()

        def add_squares(b, totals):
            totals = list(totals)
            for j in range(width // LANES):
                values = out_ref[b, part, j * LANES : (j + 1) * LANES].astype(jnp.float32)
                totals[j % 4] = totals[j % 4] + values * values
            return tuple(totals)

        zero = jnp.zeros((step, LANES), jnp.float32)
        totals = lax.fori_loop(0, blocks, add_squares, (zero,) * 4)
        total = (totals[0] + totals[1]) + (totals[2] + totals[3])
        mean = jnp.sum(total, axis=-1, keepdims=True) / (blocks * width)
        factor = jnp.broadcast_to(lax.rsqrt(mean + EPSILON), (step, LANES))

        def scale(b, _):
            for j in range(width // LANES):
                lanes = slice(j * LANES, (j + 1) * LANES)
                values = out_ref[b, part, lanes].astype(jnp.float32)
                out_ref[b, part, lanes] = (values * factor * gain_ref[b, :, lanes]).astype(
                    jnp.bfloat16
                )
            return 0

        lax.fori_loop(0, blocks, scale, 0)


def normalise(hidden, gains, first):
    blocks, _, width = gains.shape
    return call(
        functools.partial(norm_kernel, first),
        "normalise",
        [IN_HBM, IN_VMEM],
        shape((blocks, NORM_ROWS, width), jnp.bfloat16),
        [pltpu.SemaphoreType.DMA((NORM_ROWS // 16, blocks))],
    )(pltpu.with_memory_space_constraint(hidden, pltpu.HBM), gains)


def query_kernel(
    features, place_ref, squares_ref, tokens_ref, gains_ref, query_ref, key_ref, value_ref, out_ref
):
    requests = tokens_ref.shape[0]
    factor = lax.rsqrt(squares_ref[:, :1] / features + EPSILON)
    normed = (tokens_ref[...] * factor * gains_ref[place_ref[0]]).astype(jnp.bfloat16)
    row = 0
    for weight_ref in (query_ref, key_ref, value_ref):
        part = jnp.dot(normed, weight_ref[...], preferred_element_type=jnp.float32)
        for h in range(weight_ref.shape[1] // LANES):
            for r in range(requests):
                out_ref[r, row : row + 1, :] = part[r : r + 1, h * LANES : (h + 1) * LANES]
            row += 1


def blocks_dot(pieces, place, row_refs, block_refs, total):
    for (distance, first), block_ref in zip(pieces, block_refs):
        depth = block_ref.shape[0]
        rows = jnp.concatenate(
            [ref[place ^ distance, :, first : first + depth] for ref in row_refs], axis=0
        )
        part = jnp.dot(rows, block_ref[...], preferred_element_type=jnp.float32)
        total = part if total is None else total + part
    return total


def project_kernel(pieces, row_count, has_total, place_ref, *refs):
    rows, refs = refs[:row_count], refs[row_count:]
    total = refs[len(pieces)][...] if has_total else None
    refs[-1][...] = blocks_dot(pieces, place_ref[0], rows, refs, total)


def project(place, rows, blocks, total):
    extra = [] if total is None else [total]
    pieces = [(distance, first) for distance, first, _ in blocks]
    row_count = sum(r.shape[1] for r in rows)
    return call(
        functools.partial(project_kernel, pieces, len(rows), total is not None),
        "project",
        [IN_SMEM] + [IN_VMEM] * (len(rows) + len(blocks) + len(extra)),
        shape((row_count, blocks[0][2].shape[1])),
    )(place, *rows, *[block for _, _, block in blocks], *extra)


def live_rows(dims, team, place, lengths_ref):
    rows = dims[1]
    within = lax.rem(place, team) * rows + lax.broadcasted_iota(jnp.int32, dims, 1)
    return within < lengths_ref[lax.div(place, team)]


def score_kernel(pieces, row_count, team, place_ref, lengths_ref, *refs):
    rows, refs = refs[:row_count], refs[row_count:]
    blocks, refs = refs[: len(pieces)], refs[len(pieces) :]
    total_ref, cos_ref, sin_ref, new_cos_ref, new_sin_ref, summed_ref = refs[:6]
    masked_ref, top_ref, self_ref = refs[6:]
    place = place_ref[0]
    request = lax.div(place, team)
    heads = masked_ref.shape[0]
    scale = 1.0 / math.sqrt(LANES)
    turned = turn(
        summed_ref[...], new_cos_ref[pl.ds(request, 1), :], new_sin_ref[pl.ds(request, 1), :]
    ).astype(jnp.bfloat16)
    queries = turned[:heads]
    self_key = turned[heads : heads + 1].astype(jnp.float32)
    self_scores = (
        jnp.sum(queries.astype(jnp.float32) * self_key, axis=-1, keepdims=True) * scale
    )
    keys = blocks_dot(pieces, place, rows, blocks, total_ref[...])
    keys = turn(keys, cos_ref[...], sin_ref[...]).astype(jnp.bfloat16)
    scores = (
        lax.dot_general(
            queries, keys, (((1,), (1,)), ((), ())), preferred_element_type=jnp.float32
        )
        * scale
    )
    masked = jnp.where(live_rows(scores.shape, team, place, lengths_ref), scores, FLOOR)
    masked_ref[...] = masked
    top = jnp.maximum(jnp.max(masked, axis=-1, keepdims=True), self_scores)
    top_ref[...] = jnp.broadcast_to(top, top_ref.shape)
    self_ref[...] = jnp.broadcast_to(self_scores, self_ref.shape)


def weigh_kernel(pieces, row_count, team, place_ref, lengths_ref, *refs):
    rows, refs = refs[:row_count], refs[row_count:]
    blocks, refs = refs[: len(pieces)], refs[len(pieces) :]
    total_ref, masked_ref, top_ref, self_ref, summed_ref, out_ref = refs
    place = place_ref[0]
    heads = masked_ref.shape[0]
    masked = masked_ref[...]
    top = top_ref[:, :1]
    live = live_rows(masked.shape, team, place, lengths_ref)
    weights = jnp.where(live, jnp.exp(masked - top), 0.0).astype(jnp.bfloat16)
    self_weight = jnp.exp(self_ref[...] - top_ref[...]).astype(jnp.bfloat16).astype(jnp.float32)
    self_weight = jnp.where(lax.rem(place, team) == 0, self_weight, 0.0)
    self_value = summed_ref[heads + 1 : heads + 2, :].astype(jnp.bfloat16).astype(jnp.float32)
    mass = jnp.sum(weights.astype(jnp.float32), axis=-1, keepdims=True) + self_weight
    values = blocks_dot(pieces, place, rows, blocks, total_ref[...]).astype(jnp.bfloat16)
    accum = jnp.dot(weights, values, preferred_element_type=jnp.float32)
    out_ref[:, :LANES] = accum + self_weight * self_value
    out_ref[:, LANES:] = mass


def output_kernel(team, place_ref, mine_ref, other_ref, weight_ref, out_ref):
    request = lax.div(place_ref[0], team)
    heads = mine_ref.shape[0]
    attended = []
    for ref in (mine_ref, other_ref):
        attended.append(ref[:, :LANES] / ref[:, LANES:])
    first = jnp.where(request == 0, attended[0], attended[1]).astype(jnp.bfloat16)
    second = jnp.where(request == 0, attended[1], attended[0]).astype(jnp.bfloat16)
    both = jnp.concatenate(
        [
            jnp.concatenate((first[h : h + 1], second[h : h + 1]), axis=0)
            for h in range(heads)
        ],
        axis=1,
    )
    out_ref[...] = jnp.dot(both, weight_ref[...], preferred_element_type=jnp.float32)


def gather_rounds(own):
    count = lax.axis_size("ctx")
    rows = own.shape[0]
    bits = [1 << b for b in range(1, count.bit_length() - 1)]
    rounds = [[(0, 0, own)]] + [[] for _ in bits]
    halves = {}
    for bit in bits:
        block = swap(own, "ctx", bit)
        rounds[1].append((bit, 0, block))
        halves[bit] = (block[: rows // 2], block[rows // 2 :])
    for distance in sorted(range(2, count, 2), key=lambda d: bin(d).count("1")):
        hops = bin(distance).count("1")
        if hops < 2:
            continue
        low = distance & -distance
        high = 1 << (distance.bit_length() - 1)
        halves[distance] = (
            swap(halves[distance ^ high][0], "ctx", high),
            swap(halves[distance ^ low][1], "ctx", low),
        )
        rounds[hops].append((distance, 0, halves[distance][0]))
        rounds[hops].append((distance, rows // 2, halves[distance][1]))
    return [r + [(d ^ 1, first, swap(block, "ctx", 1)) for d, first, block in r] for r in rounds]


def shards(
    new_tokens,
    ctx_hidden,
    norm_gain,
    query_weight,
    key_weight,
    value_weight,
    out_weight,
    lengths,
    positions,
):
    ctx_count = lax.axis_size("ctx")
    kv_count = lax.axis_size("kv")
    place = lax.axis_index("ctx").astype(jnp.int32)
    places = place.reshape(1)
    row_count, features = ctx_hidden.shape[1:]
    head_size = key_weight.shape[2]
    heads = query_weight.shape[2] // head_size
    requests, width = new_tokens.shape
    slot_count = row_count * ctx_count // requests
    team = slot_count // row_count
    assert requests == 2 and slot_count % row_count == 0 and row_count % NORM_ROWS == 0
    assert head_size == LANES
    gains = norm_gain.reshape(ctx_count, 1, width)
    steps = row_count // NORM_ROWS

    key_rounds = gather_rounds(key_weight[0])

    rows = []

    def normalise_beside(sent, received):
        if len(rows) == steps:
            return received
        rows.append(normalise(after(ctx_hidden[0], sent), gains, len(rows) * NORM_ROWS))
        return after(received, rows[-1])

    squares = call(squares_kernel, "squares", [IN_VMEM], shape((requests, LANES)))(new_tokens)
    for distance in bits_below(ctx_count):
        received = normalise_beside(squares, swap(squares, "ctx", distance))
        squares = squares + received
    parts = call(
        functools.partial(query_kernel, features),
        "query_products",
        [IN_SMEM] + [IN_VMEM] * 6,
        shape((requests, heads + 2, head_size)),
    )(places, squares, new_tokens, gains, query_weight[0], key_weight[0], value_weight[0])
    request = place // team
    own_part = jnp.where(request == 0, parts[0], parts[1])
    sent = jnp.where(request == 0, parts[1], parts[0])
    summed = own_part + normalise_beside(sent, swap(sent, "ctx", team))
    for distance in bits_below(team):
        received = normalise_beside(summed, swap(summed, "ctx", distance))
        summed = summed + received
    while len(rows) < steps:
        normalise_beside(summed, summed)

    within = (place % team) * row_count + jnp.arange(row_count, dtype=jnp.int32)
    cosine, sine_part = tables(within.astype(jnp.float32), head_size)
    new_cosine, new_sine = tables(positions.astype(jnp.float32), head_size)
    key_total = None
    for blocks in key_rounds[:-1]:
        key_total = project(places, rows, blocks, key_total)
    blocks = key_rounds[-1]
    masked, top, self_scores = call(
        functools.partial(
            score_kernel, [(d, first) for d, first, _ in blocks], len(rows), team
        ),
        "scores",
        [IN_SMEM] * 2 + [IN_VMEM] * (len(rows) + len(blocks) + 6),
        (shape((heads, row_count)), shape((heads, LANES)), shape((heads, LANES))),
    )(
        places,
        lengths,
        *rows,
        *[block for _, _, block in blocks],
        key_total,
        cosine,
        sine_part,
        new_cosine,
        new_sine,
        summed,
    )
    for distance in bits_below(team):
        top = jnp.maximum(top, swap(top, "ctx", distance))

    value_rounds = gather_rounds(after(value_weight[0], key_total))
    value_total = None
    for blocks in value_rounds[:-1]:
        value_total = project(places, rows, blocks, value_total)
    blocks = value_rounds[-1]
    packed = call(
        functools.partial(
            weigh_kernel, [(d, first) for d, first, _ in blocks], len(rows), team
        ),
        "weighted_values",
        [IN_SMEM] * 2 + [IN_VMEM] * (len(rows) + len(blocks) + 5),
        shape((heads, 2 * head_size)),
    )(
        places,
        lengths,
        *rows,
        *[block for _, _, block in blocks],
        value_total,
        masked,
        top,
        self_scores,
        summed,
    )
    for distance in bits_below(team):
        packed = packed + swap(packed, "ctx", distance)
    other = swap(packed, "ctx", team)
    update = call(
        functools.partial(output_kernel, team),
        "output_products",
        [IN_SMEM] + [IN_VMEM] * 3,
        shape((requests, out_weight.shape[2])),
    )(places, packed, other, out_weight[0])
    for distance in bits_below(kv_count):
        update = update + swap(update, "kv", distance)
    return new_tokens + update


def solution(mesh):
    in_specs = (
        P(None, "ctx"),
        P(None, "ctx", None),
        P(),
        P(None, "ctx", "kv"),
        P(None, "ctx", "kv"),
        P(None, "ctx", "kv"),
        P(None, "kv", "ctx"),
        P(),
        P(),
    )
    out_specs = P(None, "ctx")
    return jax.shard_map(shards, mesh=mesh, in_specs=in_specs, out_specs=out_specs, check_vma=False)
```

```python
import functools
import math

import jax
import jax.numpy as jnp
from jax import lax
from jax.experimental import pallas as pl
from jax.experimental.pallas import tpu as pltpu
from jax.sharding import PartitionSpec as P

ROPE_BASE = 500000.0
EPSILON = 1e-05
FLOOR = -1e30
LANES = 128
NORM_ROWS = 160
GROUP_ROWS = 16
VMEM_BYTES = 16 * 1024 * 1024
CHEAP = pl.CostEstimate(flops=1000, bytes_accessed=1000, transcendentals=0)
IN_VMEM = pl.BlockSpec(memory_space=pltpu.VMEM)
IN_SMEM = pl.BlockSpec(memory_space=pltpu.SMEM)
IN_HBM = pl.BlockSpec(memory_space=pltpu.HBM)


def call(kernel, name, in_specs, out_shape, scratch_shapes=()):
    return pl.pallas_call(
        kernel,
        in_specs=in_specs,
        out_specs=jax.tree.map(lambda _: IN_VMEM, out_shape),
        out_shape=out_shape,
        scratch_shapes=scratch_shapes,
        compiler_params=pltpu.CompilerParams(vmem_limit_bytes=VMEM_BYTES),
        cost_estimate=CHEAP,
        name=name,
    )


def shape(dims, dtype=jnp.float32):
    return jax.ShapeDtypeStruct(dims, dtype)


def swap(value, axis, distance):
    count = lax.axis_size(axis)
    return lax.ppermute(value, axis, [(i, i ^ distance) for i in range(count)])


def after(value, *others):
    return lax.optimization_barrier((value, *others))[0]


def bits_below(count):
    return [1 << b for b in range(count.bit_length() - 1)]


def others(bits):
    found = [0]
    for bit in bits:
        found += [d | bit for d in found]
    return sorted(found[1:], key=lambda d: (-bin(d).count("1"), -d))


def combine(value, axis, bits, join):
    if len(bits) > 2:
        return combine(join(value, swap(value, axis, bits[0])), axis, bits[1:], join)
    parts = {d: swap(value, axis, d) for d in others(bits)}
    parts[0] = value
    for bit in bits:
        parts = {d: join(parts[d], parts[d | bit]) for d in sorted(parts) if not d & bit}
    return parts[0]


def tables(placed, head_size):
    half_size = head_size // 2
    frequency = jnp.exp(
        jnp.arange(half_size, dtype=jnp.float32) * (-2.0 * math.log(ROPE_BASE) / head_size)
    )
    angles = placed[..., None] * frequency
    cosine = jnp.cos(angles)
    sine_part = jnp.sin(angles)
    return (
        jnp.concatenate((cosine, cosine), axis=-1),
        jnp.concatenate((-sine_part, sine_part), axis=-1),
    )


def turn(values, cosine, signed_sine):
    half_size = values.shape[-1] // 2
    swapped = jnp.concatenate((values[:, half_size:], values[:, :half_size]), axis=-1)
    return values * cosine + swapped * signed_sine


def squares_kernel(tokens_ref, out_ref):
    values = tokens_ref[...]
    total = jnp.sum(values * values, axis=-1, keepdims=True)
    out_ref[...] = jnp.broadcast_to(total, out_ref.shape)


def norm_kernel(first, x_ref, gain_ref, out_ref, held_ref, sems):
    blocks, rows, width = out_ref.shape
    features = blocks * width
    groups = rows // GROUP_ROWS
    tiles = width // LANES

    def copy(g):
        return pltpu.make_async_copy(
            x_ref.at[pl.ds(first + g * GROUP_ROWS, GROUP_ROWS), :], held_ref.at[g], sems.at[g]
        )

    def factor_of(g):
        totals = [jnp.zeros((GROUP_ROWS, LANES), jnp.float32) for _ in range(4)]
        for j in range(blocks * tiles):
            values = held_ref[g, :, j * LANES : (j + 1) * LANES].astype(jnp.float32)
            totals[j % 4] = totals[j % 4] + values * values
        total = (totals[0] + totals[1]) + (totals[2] + totals[3])
        mean = jnp.sum(total, axis=-1, keepdims=True) / features
        return jnp.broadcast_to(lax.rsqrt(mean + EPSILON), (GROUP_ROWS, LANES))

    def scale(g, factor):
        part = pl.ds(pl.multiple_of(g * GROUP_ROWS, GROUP_ROWS), GROUP_ROWS)
        for b in range(blocks):
            for j in range(tiles):
                lanes = slice(j * LANES, (j + 1) * LANES)
                from_lane = b * width + j * LANES
                values = held_ref[g, :, from_lane : from_lane + LANES].astype(jnp.float32)
                out_ref[b, part, lanes] = (values * factor * gain_ref[b, :, lanes]).astype(
                    jnp.bfloat16
                )

    for g in range(groups):
        copy(g).start()
    copy(0).wait()

    def step(g, factor):
        copy(g + 1).wait()
        following = factor_of(g + 1)
        scale(g, factor)
        return following

    scale(groups - 1, lax.fori_loop(0, groups - 1, step, factor_of(0)))


def normalise(hidden, gains, first):
    blocks, _, width = gains.shape
    groups = NORM_ROWS // GROUP_ROWS
    return call(
        functools.partial(norm_kernel, first),
        "normalise",
        [IN_HBM, IN_VMEM],
        shape((blocks, NORM_ROWS, width), jnp.bfloat16),
        [
            pltpu.VMEM((groups, GROUP_ROWS, blocks * width), jnp.bfloat16),
            pltpu.SemaphoreType.DMA((groups,)),
        ],
    )(pltpu.with_memory_space_constraint(hidden, pltpu.HBM), gains)


def query_kernel(
    features, place_ref, squares_ref, tokens_ref, gains_ref, query_ref, key_ref, value_ref, out_ref
):
    requests = tokens_ref.shape[0]
    factor = lax.rsqrt(squares_ref[:, :1] / features + EPSILON)
    normed = (tokens_ref[...] * factor * gains_ref[place_ref[0]]).astype(jnp.bfloat16)
    row = 0
    for weight_ref in (query_ref, key_ref, value_ref):
        part = jnp.dot(normed, weight_ref[...], preferred_element_type=jnp.float32)
        for h in range(weight_ref.shape[1] // LANES):
            for r in range(requests):
                out_ref[r, row : row + 1, :] = part[r : r + 1, h * LANES : (h + 1) * LANES]
            row += 1


def blocks_dot(pieces, place, row_refs, block_refs, total):
    for (distance, first), block_ref in zip(pieces, block_refs):
        depth = block_ref.shape[0]
        rows = jnp.concatenate(
            [ref[place ^ distance, :, first : first + depth] for ref in row_refs], axis=0
        )
        part = jnp.dot(rows, block_ref[...], preferred_element_type=jnp.float32)
        total = part if total is None else total + part
    return total


def project_kernel(pieces, row_count, has_total, place_ref, *refs):
    rows, refs = refs[:row_count], refs[row_count:]
    total = refs[len(pieces)][...] if has_total else None
    refs[-1][...] = blocks_dot(pieces, place_ref[0], rows, refs, total)


def project(place, rows, blocks, total):
    extra = [] if total is None else [total]
    pieces = [(distance, first) for distance, first, _ in blocks]
    row_count = sum(r.shape[1] for r in rows)
    return call(
        functools.partial(project_kernel, pieces, len(rows), total is not None),
        "project",
        [IN_SMEM] + [IN_VMEM] * (len(rows) + len(blocks) + len(extra)),
        shape((row_count, blocks[0][2].shape[1])),
    )(place, *rows, *[block for _, _, block in blocks], *extra)


def live_rows(dims, team, place, lengths_ref):
    rows = dims[1]
    within = lax.rem(place, team) * rows + lax.broadcasted_iota(jnp.int32, dims, 1)
    return within < lengths_ref[lax.div(place, team)]


def score_kernel(pieces, row_count, team, place_ref, lengths_ref, *refs):
    rows, refs = refs[:row_count], refs[row_count:]
    blocks, refs = refs[: len(pieces)], refs[len(pieces) :]
    total_ref, cos_ref, sin_ref, new_cos_ref, new_sin_ref, summed_ref = refs[:6]
    masked_ref, top_ref, self_ref = refs[6:]
    place = place_ref[0]
    request = lax.div(place, team)
    heads = masked_ref.shape[0]
    scale = 1.0 / math.sqrt(LANES)
    turned = turn(
        summed_ref[...], new_cos_ref[pl.ds(request, 1), :], new_sin_ref[pl.ds(request, 1), :]
    ).astype(jnp.bfloat16)
    queries = turned[:heads]
    self_key = turned[heads : heads + 1].astype(jnp.float32)
    self_scores = (
        jnp.sum(queries.astype(jnp.float32) * self_key, axis=-1, keepdims=True) * scale
    )
    keys = blocks_dot(pieces, place, rows, blocks, total_ref[...])
    keys = turn(keys, cos_ref[...], sin_ref[...]).astype(jnp.bfloat16)
    scores = (
        lax.dot_general(
            queries, keys, (((1,), (1,)), ((), ())), preferred_element_type=jnp.float32
        )
        * scale
    )
    masked = jnp.where(live_rows(scores.shape, team, place, lengths_ref), scores, FLOOR)
    masked_ref[...] = masked
    top = jnp.maximum(jnp.max(masked, axis=-1, keepdims=True), self_scores)
    top_ref[...] = jnp.broadcast_to(top, top_ref.shape)
    self_ref[...] = jnp.broadcast_to(self_scores, self_ref.shape)


def weigh_kernel(pieces, row_count, team, place_ref, lengths_ref, *refs):
    rows, refs = refs[:row_count], refs[row_count:]
    blocks, refs = refs[: len(pieces)], refs[len(pieces) :]
    total_ref, masked_ref, top_ref, self_ref, summed_ref, out_ref = refs
    place = place_ref[0]
    heads = masked_ref.shape[0]
    masked = masked_ref[...]
    top = top_ref[:, :1]
    live = live_rows(masked.shape, team, place, lengths_ref)
    weights = jnp.where(live, jnp.exp(masked - top), 0.0).astype(jnp.bfloat16)
    self_weight = jnp.exp(self_ref[...] - top_ref[...]).astype(jnp.bfloat16).astype(jnp.float32)
    self_weight = jnp.where(lax.rem(place, team) == 0, self_weight, 0.0)
    self_value = summed_ref[heads + 1 : heads + 2, :].astype(jnp.bfloat16).astype(jnp.float32)
    mass = jnp.sum(weights.astype(jnp.float32), axis=-1, keepdims=True) + self_weight
    values = blocks_dot(pieces, place, rows, blocks, total_ref[...]).astype(jnp.bfloat16)
    accum = jnp.dot(weights, values, preferred_element_type=jnp.float32)
    out_ref[:, :LANES] = accum + self_weight * self_value
    out_ref[:, LANES:] = mass


def output_kernel(team, place_ref, mine_ref, other_ref, weight_ref, out_ref):
    request = lax.div(place_ref[0], team)
    heads = mine_ref.shape[0]
    attended = []
    for ref in (mine_ref, other_ref):
        attended.append(ref[:, :LANES] / ref[:, LANES:])
    first = jnp.where(request == 0, attended[0], attended[1]).astype(jnp.bfloat16)
    second = jnp.where(request == 0, attended[1], attended[0]).astype(jnp.bfloat16)
    both = jnp.concatenate(
        [
            jnp.concatenate((first[h : h + 1], second[h : h + 1]), axis=0)
            for h in range(heads)
        ],
        axis=1,
    )
    out_ref[...] = jnp.dot(both, weight_ref[...], preferred_element_type=jnp.float32)


def gather_rounds(own, far):
    count = lax.axis_size("ctx")
    rows = own.shape[0]
    bits = bits_below(count)[1:]
    rounds = [[(0, 0, own)]] + [[] for _ in bits]
    halves = {}
    for bit in bits:
        block = swap(far, "ctx", bit)
        rounds[1].append((bit, 0, block))
        halves[bit] = (block[: rows // 2], block[rows // 2 :])
    for distance in sorted(range(2, count, 2), key=lambda d: bin(d).count("1")):
        hops = bin(distance).count("1")
        if hops < 2:
            continue
        low = distance & -distance
        high = 1 << (distance.bit_length() - 1)
        halves[distance] = (
            swap(halves[distance ^ high][0], "ctx", high),
            swap(halves[distance ^ low][1], "ctx", low),
        )
        rounds[hops].append((distance, 0, halves[distance][0]))
        rounds[hops].append((distance, rows // 2, halves[distance][1]))
    return rounds


def shared(blocks, *before):
    passed = [
        (d ^ 1, first, swap(after(block, *before) if before else block, "ctx", 1))
        for d, first, block in blocks
    ]
    return blocks + passed


def project_all(place, rows, rounds):
    total = None
    for blocks in rounds[:-1]:
        total = project(place, rows, shared(blocks), total)
    return total, shared(rounds[-1], total)


def shards(
    new_tokens,
    ctx_hidden,
    norm_gain,
    query_weight,
    key_weight,
    value_weight,
    out_weight,
    lengths,
    positions,
):
    ctx_count = lax.axis_size("ctx")
    kv_count = lax.axis_size("kv")
    place = lax.axis_index("ctx").astype(jnp.int32)
    places = place.reshape(1)
    row_count, features = ctx_hidden.shape[1:]
    head_size = key_weight.shape[2]
    heads = query_weight.shape[2] // head_size
    requests, width = new_tokens.shape
    slot_count = row_count * ctx_count // requests
    team = slot_count // row_count
    assert requests == 2 and slot_count % row_count == 0 and row_count % NORM_ROWS == 0
    assert head_size == LANES
    gains = norm_gain.reshape(ctx_count, 1, width)

    key_rounds = gather_rounds(key_weight[0], key_weight[0])

    chip_bits = bits_below(ctx_count)[1:]
    first_hop = [block for _, _, block in key_rounds[1]]
    squares = call(squares_kernel, "squares", [IN_VMEM], shape((requests, LANES)))(new_tokens)
    squares = combine(squares, "ctx", [1], jnp.add)
    rows = [
        normalise(after(ctx_hidden[0], squares), gains, first)
        for first in range(0, row_count, NORM_ROWS)
    ]
    squares = combine(squares, "ctx", chip_bits, jnp.add)
    squares = after(squares, *rows, *first_hop)
    parts = call(
        functools.partial(query_kernel, features),
        "query_products",
        [IN_SMEM] + [IN_VMEM] * 6,
        shape((requests, heads + 2, head_size)),
    )(places, squares, new_tokens, gains, query_weight[0], key_weight[0], value_weight[0])
    parts = combine(parts, "ctx", [1], jnp.add)
    request = place // team
    own_part = jnp.where(request == 0, parts[0], parts[1])
    other_part = jnp.where(request == 0, parts[1], parts[0])
    if len(chip_bits) > 2:
        summed = combine(own_part + swap(other_part, "ctx", team), "ctx", chip_bits[:-1], jnp.add)
    else:
        received = {
            d: swap(other_part if d & team else own_part, "ctx", d) for d in others(chip_bits)
        }
        received[0] = own_part
        for bit in chip_bits:
            received = {
                d: received[d] + received[d | bit] for d in sorted(received) if not d & bit
            }
        summed = received[0]

    within = (place % team) * row_count + jnp.arange(row_count, dtype=jnp.int32)
    cosine, sine_part = tables(within.astype(jnp.float32), head_size)
    new_cosine, new_sine = tables(positions.astype(jnp.float32), head_size)
    key_total, blocks = project_all(places, rows, key_rounds)
    masked, top, self_scores = call(
        functools.partial(
            score_kernel, [(d, first) for d, first, _ in blocks], len(rows), team
        ),
        "scores",
        [IN_SMEM] * 2 + [IN_VMEM] * (len(rows) + len(blocks) + 6),
        (shape((heads, row_count)), shape((heads, LANES)), shape((heads, LANES))),
    )(
        places,
        lengths,
        *rows,
        *[block for _, _, block in blocks],
        key_total,
        cosine,
        sine_part,
        new_cosine,
        new_sine,
        summed,
    )
    top = combine(top, "ctx", [1], jnp.maximum)
    top = combine(top, "ctx", bits_below(team)[1:], jnp.maximum)

    value_rounds = gather_rounds(value_weight[0], after(value_weight[0], parts))
    value_total, blocks = project_all(places, rows, value_rounds)
    packed = call(
        functools.partial(
            weigh_kernel, [(d, first) for d, first, _ in blocks], len(rows), team
        ),
        "weighted_values",
        [IN_SMEM] * 2 + [IN_VMEM] * (len(rows) + len(blocks) + 5),
        shape((heads, 2 * head_size)),
    )(
        places,
        lengths,
        *rows,
        *[block for _, _, block in blocks],
        value_total,
        masked,
        top,
        self_scores,
        summed,
    )
    packed = combine(packed, "ctx", [1], jnp.add)
    if len(chip_bits) > 2:
        packed = combine(packed, "ctx", chip_bits[:-1], jnp.add)
        other = swap(packed, "ctx", team)
    else:
        received = {d: swap(packed, "ctx", d) for d in others(chip_bits)}
        received[0] = packed
        for bit in chip_bits[:-1]:
            received = {
                d: received[d] + received[d | bit] for d in sorted(received) if not d & bit
            }
        packed, other = received[0], received[team]
    update = call(
        functools.partial(output_kernel, team),
        "output_products",
        [IN_SMEM] + [IN_VMEM] * 3,
        shape((requests, out_weight.shape[2])),
    )(places, packed, other, out_weight[0])
    return new_tokens + combine(update, "kv", bits_below(kv_count), jnp.add)


def solution(mesh):
    in_specs = (
        P(None, "ctx"),
        P(None, "ctx", None),
        P(),
        P(None, "ctx", "kv"),
        P(None, "ctx", "kv"),
        P(None, "ctx", "kv"),
        P(None, "kv", "ctx"),
        P(),
        P(),
    )
    out_specs = P(None, "ctx")
    return jax.shard_map(shards, mesh=mesh, in_specs=in_specs, out_specs=out_specs, check_vma=False)
```

```python
import functools
import math

import jax
import jax.numpy as jnp
from jax import lax
from jax.experimental import pallas as pl
from jax.experimental.pallas import tpu as pltpu
from jax.sharding import PartitionSpec as P

ROPE_BASE = 500000.0
EPSILON = 1e-05
FLOOR = -1e30
LANES = 128
NORM_ROWS = 64
GROUP_ROWS = 16
VMEM_BYTES = 16 * 1024 * 1024
CHEAP = pl.CostEstimate(flops=1000, bytes_accessed=1000, transcendentals=0)
IN_VMEM = pl.BlockSpec(memory_space=pltpu.VMEM)
IN_SMEM = pl.BlockSpec(memory_space=pltpu.SMEM)
IN_HBM = pl.BlockSpec(memory_space=pltpu.HBM)


def call(kernel, name, in_specs, out_shape, scratch_shapes=()):
    return pl.pallas_call(
        kernel,
        in_specs=in_specs,
        out_specs=jax.tree.map(lambda _: IN_VMEM, out_shape),
        out_shape=out_shape,
        scratch_shapes=scratch_shapes,
        compiler_params=pltpu.CompilerParams(vmem_limit_bytes=VMEM_BYTES),
        cost_estimate=CHEAP,
        name=name,
    )


def shape(dims, dtype=jnp.float32):
    return jax.ShapeDtypeStruct(dims, dtype)


def swap(value, axis, distance):
    count = lax.axis_size(axis)
    return lax.ppermute(value, axis, [(i, i ^ distance) for i in range(count)])


def after(value, *others):
    return lax.optimization_barrier((value, *others))[0]


def bits_below(count):
    return [1 << b for b in range(count.bit_length() - 1)]


def butterfly(value, axis, bits, join):
    for bit in bits:
        value = join(value, swap(value, axis, bit))
    return value


def by_core(value, bit_0, bit_1):
    count = lax.axis_size("ctx")
    bits = (bit_0, bit_1)
    pairs = [(i, i ^ bits[i % 2]) for i in range(count) if bits[i % 2]]
    return lax.ppermute(value, "ctx", pairs)


def on_core(core):
    return lax.axis_index("ctx") % 2 == core


def send_first(own, partner):
    count = lax.axis_size("ctx")
    if count != 8:
        return [((d, d), swap(own, "ctx", d)) for d in range(2, count // 2)]
    return [((2, 4), by_core(own, 2, 4)), ((3, 5), by_core(partner, 2, 4))]


def share(blocks, *before):
    count = lax.axis_size("ctx")
    if count != 8:
        return []
    return [
        ((odd ^ 1, even ^ 1), swap(after(block, *before) if before else block, "ctx", 1))
        for (even, odd), block in blocks
    ]


def send_last(own, received):
    count = lax.axis_size("ctx")
    if count != 8:
        return [((d, d), swap(own, "ctx", d)) for d in range(count // 2, count)]
    return [((7, 7), by_core(received[0][1], 2, 4))]


def tables(placed, head_size):
    half_size = head_size // 2
    frequency = jnp.exp(
        jnp.arange(half_size, dtype=jnp.float32) * (-2.0 * math.log(ROPE_BASE) / head_size)
    )
    angles = placed[..., None] * frequency
    cosine = jnp.cos(angles)
    sine_part = jnp.sin(angles)
    return (
        jnp.concatenate((cosine, cosine), axis=-1),
        jnp.concatenate((-sine_part, sine_part), axis=-1),
    )


def turn(values, cosine, signed_sine):
    half_size = values.shape[-1] // 2
    swapped = jnp.concatenate((values[:, half_size:], values[:, :half_size]), axis=-1)
    return values * cosine + swapped * signed_sine


def squares_kernel(tokens_ref, out_ref):
    values = tokens_ref[...]
    total = jnp.sum(values * values, axis=-1, keepdims=True)
    out_ref[...] = jnp.broadcast_to(total, out_ref.shape)


def norm_kernel(first, x_ref, gain_ref, *refs):
    out_refs, (held_ref, sems) = refs[:-2], refs[-2:]
    blocks, rows, width = out_refs[0].shape
    features = blocks * width
    groups = len(out_refs) * rows // GROUP_ROWS
    tiles = width // LANES

    def copy(g):
        return pltpu.make_async_copy(
            x_ref.at[pl.ds(first + g * GROUP_ROWS, GROUP_ROWS), :], held_ref.at[g], sems.at[g]
        )

    def factor_of(g):
        totals = [jnp.zeros((GROUP_ROWS, LANES), jnp.float32) for _ in range(4)]
        for j in range(blocks * tiles):
            values = held_ref[g, :, j * LANES : (j + 1) * LANES].astype(jnp.float32)
            totals[j % 4] = totals[j % 4] + values * values
        total = (totals[0] + totals[1]) + (totals[2] + totals[3])
        mean = jnp.sum(total, axis=-1, keepdims=True) / features
        return jnp.broadcast_to(lax.rsqrt(mean + EPSILON), (GROUP_ROWS, LANES))

    def scale(g, factor, out_ref, row):
        part = pl.ds(pl.multiple_of(row, GROUP_ROWS), GROUP_ROWS)
        for b in range(blocks):
            for j in range(tiles):
                lanes = slice(j * LANES, (j + 1) * LANES)
                from_lane = b * width + j * LANES
                values = held_ref[g, :, from_lane : from_lane + LANES].astype(jnp.float32)
                out_ref[b, part, lanes] = (values * factor * gain_ref[b, :, lanes]).astype(
                    jnp.bfloat16
                )

    for g in range(groups):
        copy(g).start()
    copy(0).wait()

    factor = factor_of(0)
    for i, out_ref in enumerate(out_refs):
        start = i * rows // GROUP_ROWS
        stop = min(start + rows // GROUP_ROWS, groups - 1)

        def step(g, factor, out_ref=out_ref, start=start):
            copy(g + 1).wait()
            following = factor_of(g + 1)
            scale(g, factor, out_ref, (g - start) * GROUP_ROWS)
            return following

        factor = lax.fori_loop(start, stop, step, factor)
    scale(groups - 1, factor, out_refs[-1], rows - GROUP_ROWS)


def normalise(hidden, gains, first, parts):
    blocks, _, width = gains.shape
    groups = parts * NORM_ROWS // GROUP_ROWS
    return call(
        functools.partial(norm_kernel, first),
        "normalise",
        [IN_HBM, IN_VMEM],
        (shape((blocks, NORM_ROWS, width), jnp.bfloat16),) * parts,
        [
            pltpu.VMEM((groups, GROUP_ROWS, blocks * width), jnp.bfloat16),
            pltpu.SemaphoreType.DMA((groups,)),
        ],
    )(pltpu.with_memory_space_constraint(hidden, pltpu.HBM), gains)


def query_kernel(
    features, place_ref, squares_ref, tokens_ref, gains_ref, query_ref, key_ref, value_ref, out_ref
):
    requests = tokens_ref.shape[0]
    factor = lax.rsqrt(squares_ref[:, :1] / features + EPSILON)
    normed = (tokens_ref[...] * factor * gains_ref[place_ref[0]]).astype(jnp.bfloat16)
    row = 0
    for weight_ref in (query_ref, key_ref, value_ref):
        part = jnp.dot(normed, weight_ref[...], preferred_element_type=jnp.float32)
        for h in range(weight_ref.shape[1] // LANES):
            for r in range(requests):
                out_ref[r, row : row + 1, :] = part[r : r + 1, h * LANES : (h + 1) * LANES]
            row += 1


def blocks_dot(distances, place, row_refs, block_refs, total):
    for (even, odd), block_ref in zip(distances, block_refs):
        distance = jnp.where(lax.rem(place, 2) == 0, even, odd)
        rows = jnp.concatenate([ref[place ^ distance] for ref in row_refs], axis=0)
        part = jnp.dot(rows, block_ref[...], preferred_element_type=jnp.float32)
        total = part if total is None else total + part
    return total


def project_kernel(distances, row_count, has_total, place_ref, *refs):
    rows, refs = refs[:row_count], refs[row_count:]
    total = refs[len(distances)][...] if has_total else None
    refs[-1][...] = blocks_dot(distances, place_ref[0], rows, refs, total)


def project(place, rows, blocks, total=None):
    extra = [] if total is None else [total]
    row_count = sum(r.shape[1] for r in rows)
    return call(
        functools.partial(project_kernel, [d for d, _ in blocks], len(rows), total is not None),
        "project",
        [IN_SMEM] + [IN_VMEM] * (len(rows) + len(blocks) + len(extra)),
        shape((row_count, LANES)),
    )(place, *rows, *[block for _, block in blocks], *extra)


def live_rows(dims, team, place, lengths_ref):
    rows = dims[1]
    within = lax.rem(place, team) * rows + lax.broadcasted_iota(jnp.int32, dims, 1)
    return within < lengths_ref[lax.div(place, team)]


def score_kernel(team, place_ref, lengths_ref, *refs):
    keys_ref, cos_ref, sin_ref, new_cos_ref, new_sin_ref, summed_ref = refs[:6]
    masked_ref, top_ref, self_ref = refs[6:]
    place = place_ref[0]
    request = lax.div(place, team)
    heads = masked_ref.shape[0]
    scale = 1.0 / math.sqrt(LANES)
    turned = turn(
        summed_ref[...], new_cos_ref[pl.ds(request, 1), :], new_sin_ref[pl.ds(request, 1), :]
    ).astype(jnp.bfloat16)
    queries = turned[:heads]
    self_key = turned[heads : heads + 1].astype(jnp.float32)
    self_scores = (
        jnp.sum(queries.astype(jnp.float32) * self_key, axis=-1, keepdims=True) * scale
    )
    keys = turn(keys_ref[...], cos_ref[...], sin_ref[...]).astype(jnp.bfloat16)
    scores = (
        lax.dot_general(
            queries, keys, (((1,), (1,)), ((), ())), preferred_element_type=jnp.float32
        )
        * scale
    )
    masked = jnp.where(live_rows(scores.shape, team, place, lengths_ref), scores, FLOOR)
    masked_ref[...] = masked
    top = jnp.maximum(jnp.max(masked, axis=-1, keepdims=True), self_scores)
    top_ref[...] = jnp.broadcast_to(top, top_ref.shape)
    self_ref[...] = jnp.broadcast_to(self_scores, self_ref.shape)


def weigh_kernel(distances, row_count, team, place_ref, lengths_ref, *refs):
    rows, refs = refs[:row_count], refs[row_count:]
    blocks, refs = refs[: len(distances)], refs[len(distances) :]
    total_ref, masked_ref, top_ref, self_ref, summed_ref, out_ref = refs
    place = place_ref[0]
    heads = masked_ref.shape[0]
    masked = masked_ref[...]
    top = top_ref[:, :1]
    live = live_rows(masked.shape, team, place, lengths_ref)
    weights = jnp.where(live, jnp.exp(masked - top), 0.0).astype(jnp.bfloat16)
    self_weight = jnp.exp(self_ref[...] - top_ref[...]).astype(jnp.bfloat16).astype(jnp.float32)
    self_weight = jnp.where(lax.rem(place, team) == 0, self_weight, 0.0)
    self_value = summed_ref[heads + 1 : heads + 2, :].astype(jnp.bfloat16).astype(jnp.float32)
    mass = jnp.sum(weights.astype(jnp.float32), axis=-1, keepdims=True) + self_weight
    values = blocks_dot(distances, place, rows, blocks, total_ref[...]).astype(jnp.bfloat16)
    accum = jnp.dot(weights, values, preferred_element_type=jnp.float32)
    out_ref[:, :LANES] = accum + self_weight * self_value
    out_ref[:, LANES:] = mass


def output_kernel(team, place_ref, mine_ref, other_ref, weight_ref, out_ref):
    request = lax.div(place_ref[0], team)
    heads = mine_ref.shape[0]
    attended = []
    for ref in (mine_ref, other_ref):
        attended.append(ref[:, :LANES] / ref[:, LANES:])
    first = jnp.where(request == 0, attended[0], attended[1]).astype(jnp.bfloat16)
    second = jnp.where(request == 0, attended[1], attended[0]).astype(jnp.bfloat16)
    both = jnp.concatenate(
        [
            jnp.concatenate((first[h : h + 1], second[h : h + 1]), axis=0)
            for h in range(heads)
        ],
        axis=1,
    )
    out_ref[...] = jnp.dot(both, weight_ref[...], preferred_element_type=jnp.float32)


def shards(
    new_tokens,
    ctx_hidden,
    norm_gain,
    query_weight,
    key_weight,
    value_weight,
    out_weight,
    lengths,
    positions,
):
    ctx_count = lax.axis_size("ctx")
    kv_count = lax.axis_size("kv")
    place = lax.axis_index("ctx").astype(jnp.int32)
    places = place.reshape(1)
    row_count, features = ctx_hidden.shape[1:]
    head_size = key_weight.shape[2]
    heads = query_weight.shape[2] // head_size
    requests, width = new_tokens.shape
    slot_count = row_count * ctx_count // requests
    team = slot_count // row_count
    assert requests == 2 and slot_count % row_count == 0 and row_count % NORM_ROWS == 0
    assert head_size == LANES
    gains = norm_gain.reshape(ctx_count, 1, width)

    split = ctx_count == 8
    chip_bits = bits_below(ctx_count)[1:]
    rows = []

    def beside(received, sent):
        if len(rows) * NORM_ROWS == row_count:
            return received
        rows.extend(
            normalise(after(ctx_hidden[0], sent), gains, len(rows) * NORM_ROWS, 1)
        )
        return after(received, rows[-1])

    def over_x(value, join):
        value = join(value, beside(by_core(value, 0, 2), value))
        return jnp.where(on_core(0), beside(swap(value, "ctx", 1), value), value)

    def over_y(sent, value, join):
        value = join(value, beside(by_core(sent, 4, 0), sent))
        return jnp.where(on_core(1), beside(swap(value, "ctx", 1), value), value)

    key_partner = swap(key_weight[0], "ctx", 1)
    value_partner = swap(value_weight[0], "ctx", 1)
    key_near = [((0, 0), key_weight[0]), ((1, 1), key_partner)]
    value_near = [((0, 0), value_weight[0]), ((1, 1), value_partner)]
    key_far = send_first(key_weight[0], key_partner)

    squares = call(squares_kernel, "squares", [IN_VMEM], shape((requests, LANES)))(new_tokens)
    squares = squares + swap(squares, "ctx", 1)
    squares = after(squares, key_partner, value_partner)
    if split:
        squares = over_x(squares, jnp.add)
        key_shared = share(key_far, squares)
        squares = over_y(squares, squares, jnp.add)
        squares = after(squares, key_far[1][1])
    else:
        key_shared = share(key_far)
        squares = butterfly(squares, "ctx", chip_bits, jnp.add)
    key_last = send_last(key_weight[0], key_shared)
    own_values = after(value_weight[0], *[block for _, block in key_shared[:1]])
    value_far = send_first(own_values, value_partner)

    parts = call(
        functools.partial(query_kernel, features),
        "query_products",
        [IN_SMEM] + [IN_VMEM] * 6,
        shape((requests, heads + 2, head_size)),
    )(places, squares, new_tokens, gains, query_weight[0], key_weight[0], value_weight[0])
    parts = parts + beside(swap(parts, "ctx", 1), parts)
    request = place // team
    if split:
        parts = over_x(parts, jnp.add)
    own_part = jnp.where(request == 0, parts[0], parts[1])
    other_part = jnp.where(request == 0, parts[1], parts[0])
    if split:
        summed = over_y(other_part, own_part, jnp.add)
    else:
        summed = own_part + swap(other_part, "ctx", team)
        summed = butterfly(summed, "ctx", chip_bits[:-1], jnp.add)
    while len(rows) * NORM_ROWS < row_count:
        summed = beside(summed, summed)

    key_total = project(places, rows, key_near)
    key_total = project(places, rows, key_far + key_shared, key_total)
    key_total = project(places, rows, key_last + share(key_last), key_total)
    value_total = project(places, rows, value_near)
    value_shared = share(value_far)
    value_last = send_last(own_values, value_shared)
    value_total = project(places, rows, value_far + value_shared, value_total)

    within = (place % team) * row_count + jnp.arange(row_count, dtype=jnp.int32)
    cosine, sine_part = tables(within.astype(jnp.float32), head_size)
    new_cosine, new_sine = tables(positions.astype(jnp.float32), head_size)
    masked, top, self_scores = call(
        functools.partial(score_kernel, team),
        "scores",
        [IN_SMEM] * 2 + [IN_VMEM] * 6,
        (shape((heads, row_count)), shape((heads, LANES)), shape((heads, LANES))),
    )(places, lengths, key_total, cosine, sine_part, new_cosine, new_sine, summed)
    if split:
        top = over_x(jnp.maximum(top, swap(top, "ctx", 1)), jnp.maximum)
    else:
        top = butterfly(top, "ctx", bits_below(team), jnp.maximum)

    blocks = value_last + share(value_last, value_total)
    packed = call(
        functools.partial(weigh_kernel, [d for d, _ in blocks], len(rows), team),
        "weighted_values",
        [IN_SMEM] * 2 + [IN_VMEM] * (len(rows) + len(blocks) + 5),
        shape((heads, 2 * head_size)),
    )(
        places,
        lengths,
        *rows,
        *[block for _, block in blocks],
        value_total,
        masked,
        top,
        self_scores,
        summed,
    )
    packed = butterfly(packed, "ctx", bits_below(team), jnp.add)
    other = swap(packed, "ctx", team)
    update = call(
        functools.partial(output_kernel, team),
        "output_products",
        [IN_SMEM] + [IN_VMEM] * 3,
        shape((requests, out_weight.shape[2])),
    )(places, packed, other, out_weight[0])
    return new_tokens + butterfly(update, "kv", bits_below(kv_count), jnp.add)


def solution(mesh):
    in_specs = (
        P(None, "ctx"),
        P(None, "ctx", None),
        P(),
        P(None, "ctx", "kv"),
        P(None, "ctx", "kv"),
        P(None, "ctx", "kv"),
        P(None, "kv", "ctx"),
        P(),
        P(),
    )
    out_specs = P(None, "ctx")
    return jax.shard_map(shards, mesh=mesh, in_specs=in_specs, out_specs=out_specs, check_vma=False)
```

```python
import functools
import math

import jax
import jax.numpy as jnp
from jax import lax
from jax.experimental import pallas as pl
from jax.experimental.pallas import tpu as pltpu
from jax.sharding import PartitionSpec as P

ROPE_BASE = 500000.0
EPSILON = 1e-05
FLOOR = -1e30
LANES = 128
NORM_ROWS = 64
GROUP_ROWS = 16
VMEM_BYTES = 16 * 1024 * 1024
CHEAP = pl.CostEstimate(flops=1000, bytes_accessed=1000, transcendentals=0)
IN_VMEM = pl.BlockSpec(memory_space=pltpu.VMEM)
IN_SMEM = pl.BlockSpec(memory_space=pltpu.SMEM)
IN_HBM = pl.BlockSpec(memory_space=pltpu.HBM)


def call(kernel, name, in_specs, out_shape, scratch_shapes=()):
    return pl.pallas_call(
        kernel,
        in_specs=in_specs,
        out_specs=jax.tree.map(lambda _: IN_VMEM, out_shape),
        out_shape=out_shape,
        scratch_shapes=scratch_shapes,
        compiler_params=pltpu.CompilerParams(vmem_limit_bytes=VMEM_BYTES),
        cost_estimate=CHEAP,
        name=name,
    )


def shape(dims, dtype=jnp.float32):
    return jax.ShapeDtypeStruct(dims, dtype)


def swap(value, axis, distance):
    count = lax.axis_size(axis)
    return lax.ppermute(value, axis, [(i, i ^ distance) for i in range(count)])


def after(value, *others):
    return lax.optimization_barrier((value, *others))[0]


def bits_below(count):
    return [1 << b for b in range(count.bit_length() - 1)]


def butterfly(value, axis, bits, join):
    for bit in bits:
        value = join(value, swap(value, axis, bit))
    return value


def by_core(value, bit_0, bit_1):
    count = lax.axis_size("ctx")
    bits = (bit_0, bit_1)
    pairs = [(i, i ^ bits[i % 2]) for i in range(count) if bits[i % 2]]
    return lax.ppermute(value, "ctx", pairs)


def send_first(own, partner):
    count = lax.axis_size("ctx")
    if count != 8:
        return [((d, d), swap(own, "ctx", d)) for d in range(2, count // 2)]
    return [((2, 4), by_core(own, 2, 4)), ((3, 5), by_core(partner, 2, 4))]


def share(blocks, *before):
    count = lax.axis_size("ctx")
    if count != 8:
        return []
    return [
        ((odd ^ 1, even ^ 1), swap(after(block, *before) if before else block, "ctx", 1))
        for (even, odd), block in blocks
    ]


def send_last(own, received):
    count = lax.axis_size("ctx")
    if count != 8:
        return [((d, d), swap(own, "ctx", d)) for d in range(count // 2, count)]
    return [((7, 7), by_core(received[0][1], 2, 4))]


def tables(placed, head_size):
    half_size = head_size // 2
    frequency = jnp.exp(
        jnp.arange(half_size, dtype=jnp.float32) * (-2.0 * math.log(ROPE_BASE) / head_size)
    )
    angles = placed[..., None] * frequency
    return jnp.cos(angles), jnp.sin(angles)


def turn(values, cosine, sine_part):
    half_size = values.shape[-1] // 2
    leading = values[:, :half_size]
    trailing = values[:, half_size:]
    return jnp.concatenate(
        (leading * cosine - trailing * sine_part, trailing * cosine + leading * sine_part), axis=-1
    )


def squares_kernel(team, row_count, place_ref, tokens_ref, out_ref, core_ref, request_ref, row_ref):
    values = tokens_ref[...]
    total = jnp.sum(values * values, axis=-1, keepdims=True)
    out_ref[...] = jnp.broadcast_to(total, out_ref.shape)
    place = place_ref[0]
    core_ref[...] = jnp.full(core_ref.shape, lax.rem(place, 2))
    request_ref[...] = jnp.full(request_ref.shape, lax.div(place, team))
    row_ref[...] = jnp.full(row_ref.shape, lax.rem(place, team) * row_count)


def norm_kernel(first, x_ref, gain_ref, *refs):
    out_refs, (held_ref, sems) = refs[:-2], refs[-2:]
    blocks, rows, width = out_refs[0].shape
    features = blocks * width
    groups = len(out_refs) * rows // GROUP_ROWS
    tiles = width // LANES

    def copy(g):
        return pltpu.make_async_copy(
            x_ref.at[pl.ds(first + g * GROUP_ROWS, GROUP_ROWS), :], held_ref.at[g], sems.at[g]
        )

    def factor_of(g):
        totals = [jnp.zeros((GROUP_ROWS, LANES), jnp.float32) for _ in range(4)]
        for j in range(blocks * tiles):
            values = held_ref[g, :, j * LANES : (j + 1) * LANES].astype(jnp.float32)
            totals[j % 4] = totals[j % 4] + values * values
        total = (totals[0] + totals[1]) + (totals[2] + totals[3])
        mean = jnp.sum(total, axis=-1, keepdims=True) / features
        return jnp.broadcast_to(lax.rsqrt(mean + EPSILON), (GROUP_ROWS, LANES))

    def scale(g, factor, out_ref, row):
        part = pl.ds(pl.multiple_of(row, GROUP_ROWS), GROUP_ROWS)
        for b in range(blocks):
            for j in range(tiles):
                lanes = slice(j * LANES, (j + 1) * LANES)
                from_lane = b * width + j * LANES
                values = held_ref[g, :, from_lane : from_lane + LANES].astype(jnp.float32)
                out_ref[b, part, lanes] = (values * factor * gain_ref[b, :, lanes]).astype(
                    jnp.bfloat16
                )

    for g in range(groups):
        copy(g).start()
    copy(0).wait()

    factor = factor_of(0)
    for i, out_ref in enumerate(out_refs):
        start = i * rows // GROUP_ROWS
        stop = min(start + rows // GROUP_ROWS, groups - 1)

        def step(g, factor, out_ref=out_ref, start=start):
            copy(g + 1).wait()
            following = factor_of(g + 1)
            scale(g, factor, out_ref, (g - start) * GROUP_ROWS)
            return following

        factor = lax.fori_loop(start, stop, step, factor)
    scale(groups - 1, factor, out_refs[-1], rows - GROUP_ROWS)


def normalise(hidden, gains, first, parts):
    blocks, _, width = gains.shape
    groups = parts * NORM_ROWS // GROUP_ROWS
    return call(
        functools.partial(norm_kernel, first),
        "normalise",
        [IN_HBM, IN_VMEM],
        (shape((blocks, NORM_ROWS, width), jnp.bfloat16),) * parts,
        [
            pltpu.VMEM((groups, GROUP_ROWS, blocks * width), jnp.bfloat16),
            pltpu.SemaphoreType.DMA((groups,)),
        ],
    )(pltpu.with_memory_space_constraint(hidden, pltpu.HBM), gains)


def query_kernel(
    features, place_ref, squares_ref, tokens_ref, gains_ref, query_ref, key_ref, value_ref, out_ref
):
    requests = tokens_ref.shape[0]
    factor = lax.rsqrt(squares_ref[:, :1] / features + EPSILON)
    normed = (tokens_ref[...] * factor * gains_ref[place_ref[0]]).astype(jnp.bfloat16)
    row = 0
    for weight_ref in (query_ref, key_ref, value_ref):
        part = jnp.dot(normed, weight_ref[...], preferred_element_type=jnp.float32)
        for h in range(weight_ref.shape[1] // LANES):
            for r in range(requests):
                out_ref[r, row : row + 1, :] = part[r : r + 1, h * LANES : (h + 1) * LANES]
            row += 1


def blocks_dot(distances, place, row_refs, block_refs, total):
    for (even, odd), block_ref in zip(distances, block_refs):
        distance = jnp.where(lax.rem(place, 2) == 0, even, odd)
        rows = jnp.concatenate([ref[place ^ distance] for ref in row_refs], axis=0)
        part = jnp.dot(rows, block_ref[...], preferred_element_type=jnp.float32)
        total = part if total is None else total + part
    return total


def project_kernel(distances, row_count, has_total, place_ref, *refs):
    rows, refs = refs[:row_count], refs[row_count:]
    total = refs[len(distances)][...] if has_total else None
    refs[-1][...] = blocks_dot(distances, place_ref[0], rows, refs, total)


def project(place, rows, blocks, total=None):
    extra = [] if total is None else [total]
    row_count = sum(r.shape[1] for r in rows)
    return call(
        functools.partial(project_kernel, [d for d, _ in blocks], len(rows), total is not None),
        "project",
        [IN_SMEM] + [IN_VMEM] * (len(rows) + len(blocks) + len(extra)),
        shape((row_count, LANES)),
    )(place, *rows, *[block for _, block in blocks], *extra)


def live_rows(dims, team, place, lengths_ref):
    rows = dims[1]
    within = lax.rem(place, team) * rows + lax.broadcasted_iota(jnp.int32, dims, 1)
    return within < lengths_ref[lax.div(place, team)]


def score_kernel(team, place_ref, lengths_ref, *refs):
    keys_ref, cos_ref, sin_ref, new_cos_ref, new_sin_ref, summed_ref = refs[:6]
    masked_ref, top_ref, self_ref = refs[6:]
    place = place_ref[0]
    request = lax.div(place, team)
    heads = masked_ref.shape[0]
    scale = 1.0 / math.sqrt(LANES)
    turned = turn(
        summed_ref[...], new_cos_ref[pl.ds(request, 1), :], new_sin_ref[pl.ds(request, 1), :]
    ).astype(jnp.bfloat16)
    queries = turned[:heads]
    self_key = turned[heads : heads + 1].astype(jnp.float32)
    self_scores = (
        jnp.sum(queries.astype(jnp.float32) * self_key, axis=-1, keepdims=True) * scale
    )
    keys = turn(keys_ref[...], cos_ref[...], sin_ref[...]).astype(jnp.bfloat16)
    scores = (
        lax.dot_general(
            queries, keys, (((1,), (1,)), ((), ())), preferred_element_type=jnp.float32
        )
        * scale
    )
    masked = jnp.where(live_rows(scores.shape, team, place, lengths_ref), scores, FLOOR)
    masked_ref[...] = masked
    top = jnp.maximum(jnp.max(masked, axis=-1, keepdims=True), self_scores)
    top_ref[...] = jnp.broadcast_to(top, top_ref.shape)
    self_ref[...] = jnp.broadcast_to(self_scores, self_ref.shape)


def weigh_kernel(distances, row_count, team, place_ref, lengths_ref, *refs):
    rows, refs = refs[:row_count], refs[row_count:]
    blocks, refs = refs[: len(distances)], refs[len(distances) :]
    total_ref, masked_ref, top_ref, self_ref, summed_ref, out_ref = refs
    place = place_ref[0]
    heads = masked_ref.shape[0]
    masked = masked_ref[...]
    top = top_ref[:, :1]
    live = live_rows(masked.shape, team, place, lengths_ref)
    weights = jnp.where(live, jnp.exp(masked - top), 0.0).astype(jnp.bfloat16)
    self_weight = jnp.exp(self_ref[...] - top_ref[...]).astype(jnp.bfloat16).astype(jnp.float32)
    self_weight = jnp.where(lax.rem(place, team) == 0, self_weight, 0.0)
    self_value = summed_ref[heads + 1 : heads + 2, :].astype(jnp.bfloat16).astype(jnp.float32)
    mass = jnp.sum(weights.astype(jnp.float32), axis=-1, keepdims=True) + self_weight
    values = blocks_dot(distances, place, rows, blocks, total_ref[...]).astype(jnp.bfloat16)
    accum = jnp.dot(weights, values, preferred_element_type=jnp.float32)
    out_ref[:, :LANES] = accum + self_weight * self_value
    out_ref[:, LANES:] = mass


def output_kernel(team, place_ref, mine_ref, other_ref, weight_ref, out_ref):
    request = lax.div(place_ref[0], team)
    heads = mine_ref.shape[0]
    attended = []
    for ref in (mine_ref, other_ref):
        attended.append(ref[:, :LANES] / ref[:, LANES:])
    first = jnp.where(request == 0, attended[0], attended[1]).astype(jnp.bfloat16)
    second = jnp.where(request == 0, attended[1], attended[0]).astype(jnp.bfloat16)
    both = jnp.concatenate(
        [
            jnp.concatenate((first[h : h + 1], second[h : h + 1]), axis=0)
            for h in range(heads)
        ],
        axis=1,
    )
    out_ref[...] = jnp.dot(both, weight_ref[...], preferred_element_type=jnp.float32)


def shards(
    new_tokens,
    ctx_hidden,
    norm_gain,
    query_weight,
    key_weight,
    value_weight,
    out_weight,
    lengths,
    positions,
):
    ctx_count = lax.axis_size("ctx")
    kv_count = lax.axis_size("kv")
    place = lax.axis_index("ctx").astype(jnp.int32)
    places = place.reshape(1)
    row_count, features = ctx_hidden.shape[1:]
    head_size = key_weight.shape[2]
    heads = query_weight.shape[2] // head_size
    requests, width = new_tokens.shape
    slot_count = row_count * ctx_count // requests
    team = slot_count // row_count
    assert requests == 2 and slot_count % row_count == 0 and row_count % NORM_ROWS == 0
    assert head_size == LANES
    gains = norm_gain.reshape(ctx_count, 1, width)

    split = ctx_count == 8
    chip_bits = bits_below(ctx_count)[1:]
    rows = []
    squares, core, own_request, first_row = call(
        functools.partial(squares_kernel, team, row_count),
        "squares",
        [IN_SMEM, IN_VMEM],
        (shape((requests, LANES)),) + (shape((1, LANES), jnp.int32),) * 3,
    )(places, new_tokens)

    def beside(received, sent, parts):
        first = len(rows) * NORM_ROWS
        rows.extend(normalise(after(ctx_hidden[0], sent), gains, first, parts))
        return after(received, rows[-1])

    def sum_chips(value, norm_parts=0):
        received = by_core(value, 4, 2)
        if norm_parts:
            received = beside(received, value, norm_parts)
        told = swap(received, "ctx", 1)
        opposite = by_core(told, 4, 2)
        if norm_parts:
            opposite = beside(opposite, told, row_count // NORM_ROWS - norm_parts)
        over_x = jnp.where(core == 0, told, received)
        over_y = jnp.where(core == 0, received, told)
        return (value + over_x) + (over_y + opposite), told

    key_partner = swap(key_weight[0], "ctx", 1)
    value_partner = swap(value_weight[0], "ctx", 1)
    key_near = [((0, 0), key_weight[0]), ((1, 1), key_partner)]
    value_near = [((0, 0), value_weight[0]), ((1, 1), value_partner)]
    key_far = send_first(key_weight[0], key_partner)

    squares = squares + swap(squares, "ctx", 1)
    squares = after(squares, key_partner, value_partner)
    if split:
        squares, told = sum_chips(squares, row_count // NORM_ROWS // 2)
        key_shared = share(key_far, told)
        squares = after(squares, key_far[1][1])
    else:
        key_shared = share(key_far)
        squares = beside(squares, squares, row_count // NORM_ROWS)
        squares = butterfly(squares, "ctx", chip_bits, jnp.add)
    key_last = send_last(key_weight[0], key_shared)
    own_values = after(value_weight[0], *[block for _, block in key_shared[:1]])
    value_far = send_first(own_values, value_partner)

    parts = call(
        functools.partial(query_kernel, features),
        "query_products",
        [IN_SMEM] + [IN_VMEM] * 6,
        shape((requests, heads + 2, head_size)),
    )(places, squares, new_tokens, gains, query_weight[0], key_weight[0], value_weight[0])
    parts = parts + swap(parts, "ctx", 1)
    parts_sent = parts
    if split:
        parts, _ = sum_chips(parts)
        summed = jnp.where(own_request == 0, parts[0], parts[1])
    else:
        own_part = jnp.where(own_request == 0, parts[0], parts[1])
        other_part = jnp.where(own_request == 0, parts[1], parts[0])
        summed = own_part + swap(other_part, "ctx", team)
        summed = butterfly(summed, "ctx", chip_bits[:-1], jnp.add)

    key_total = project(places, rows, key_near)
    key_total = project(places, rows, key_far + key_shared, key_total)
    key_total = project(places, rows, key_last + share(key_last), key_total)
    value_total = project(places, rows, value_near)
    value_shared = share(value_far, parts_sent)
    value_last = send_last(own_values, value_shared)
    value_total = project(places, rows, value_far + value_shared, value_total)

    within = first_row[0, :1] + jnp.arange(row_count, dtype=jnp.int32)
    cosine, sine_part = tables(within.astype(jnp.float32), head_size)
    new_cosine, new_sine = tables(positions.astype(jnp.float32), head_size)
    masked, top, self_scores = call(
        functools.partial(score_kernel, team),
        "scores",
        [IN_SMEM] * 2 + [IN_VMEM] * 6,
        (shape((heads, row_count)), shape((heads, LANES)), shape((heads, LANES))),
    )(places, lengths, key_total, cosine, sine_part, new_cosine, new_sine, summed)
    if split:
        top = jnp.maximum(top, swap(top, "ctx", 1))
        top = jnp.maximum(top, by_core(top, 0, 2))
        top = jnp.where(core == 0, swap(top, "ctx", 1), top)
    else:
        top = butterfly(top, "ctx", bits_below(team), jnp.maximum)

    blocks = value_last + share(value_last, value_total)
    packed = call(
        functools.partial(weigh_kernel, [d for d, _ in blocks], len(rows), team),
        "weighted_values",
        [IN_SMEM] * 2 + [IN_VMEM] * (len(rows) + len(blocks) + 5),
        shape((heads, 2 * head_size)),
    )(
        places,
        lengths,
        *rows,
        *[block for _, block in blocks],
        value_total,
        masked,
        top,
        self_scores,
        summed,
    )
    packed = butterfly(packed, "ctx", bits_below(team), jnp.add)
    other = swap(packed, "ctx", team)
    update = call(
        functools.partial(output_kernel, team),
        "output_products",
        [IN_SMEM] + [IN_VMEM] * 3,
        shape((requests, out_weight.shape[2])),
    )(places, packed, other, out_weight[0])
    return new_tokens + butterfly(update, "kv", bits_below(kv_count), jnp.add)


def solution(mesh):
    in_specs = (
        P(None, "ctx"),
        P(None, "ctx", None),
        P(),
        P(None, "ctx", "kv"),
        P(None, "ctx", "kv"),
        P(None, "ctx", "kv"),
        P(None, "kv", "ctx"),
        P(),
        P(),
    )
    out_specs = P(None, "ctx")
    return jax.shard_map(shards, mesh=mesh, in_specs=in_specs, out_specs=out_specs, check_vma=False)
```

```python
import functools
import math

import jax
import jax.numpy as jnp
from jax import lax
from jax.experimental import pallas as pl
from jax.experimental.pallas import tpu as pltpu
from jax.sharding import PartitionSpec as P

ROPE_BASE = 500000.0
EPSILON = 1e-05
FLOOR = -1e30
LANES = 128
NORM_ROWS = 64
GROUP_ROWS = 16
VMEM_BYTES = 16 * 1024 * 1024
CHEAP = pl.CostEstimate(flops=1000, bytes_accessed=1000, transcendentals=0)
IN_VMEM = pl.BlockSpec(memory_space=pltpu.VMEM)
IN_SMEM = pl.BlockSpec(memory_space=pltpu.SMEM)
IN_HBM = pl.BlockSpec(memory_space=pltpu.HBM)


def call(kernel, name, in_specs, out_shape, scratch_shapes=()):
    return pl.pallas_call(
        kernel,
        in_specs=in_specs,
        out_specs=jax.tree.map(lambda _: IN_VMEM, out_shape),
        out_shape=out_shape,
        scratch_shapes=scratch_shapes,
        compiler_params=pltpu.CompilerParams(vmem_limit_bytes=VMEM_BYTES),
        cost_estimate=CHEAP,
        name=name,
    )


def shape(dims, dtype=jnp.float32):
    return jax.ShapeDtypeStruct(dims, dtype)


def swap(value, axis, distance):
    count = lax.axis_size(axis)
    return lax.ppermute(value, axis, [(i, i ^ distance) for i in range(count)])


def after(value, *others):
    return lax.optimization_barrier((value, *others))[0]


def bits_below(count):
    return [1 << b for b in range(count.bit_length() - 1)]


def butterfly(value, axis, bits, join):
    for bit in bits:
        value = join(value, swap(value, axis, bit))
    return value


def by_core(value, bit_0, bit_1):
    count = lax.axis_size("ctx")
    bits = (bit_0, bit_1)
    pairs = [(i, i ^ bits[i % 2]) for i in range(count) if bits[i % 2]]
    return lax.ppermute(value, "ctx", pairs)


def send_first(own, partner):
    count = lax.axis_size("ctx")
    if count != 8:
        return [((d, d), swap(own, "ctx", d)) for d in range(2, count // 2)]
    return [((2, 4), by_core(own, 2, 4)), ((3, 5), by_core(partner, 2, 4))]


def share(blocks, *before):
    count = lax.axis_size("ctx")
    if count != 8:
        return []
    return [
        ((odd ^ 1, even ^ 1), swap(after(block, *before) if before else block, "ctx", 1))
        for (even, odd), block in blocks
    ]


def send_last(own, received):
    count = lax.axis_size("ctx")
    if count != 8:
        return [((d, d), swap(own, "ctx", d)) for d in range(count // 2, count)]
    return [((7, 7), by_core(received[0][1], 2, 4))]


def tables(placed, head_size):
    half_size = head_size // 2
    frequency = jnp.exp(
        jnp.arange(half_size, dtype=jnp.float32) * (-2.0 * math.log(ROPE_BASE) / head_size)
    )
    angles = placed[..., None] * frequency
    return jnp.cos(angles), jnp.sin(angles)


def turn(values, cosine, sine_part):
    half_size = values.shape[-1] // 2
    leading = values[:, :half_size]
    trailing = values[:, half_size:]
    return jnp.concatenate(
        (leading * cosine - trailing * sine_part, trailing * cosine + leading * sine_part), axis=-1
    )


def squares_kernel(team, row_count, place_ref, tokens_ref, out_ref, core_ref, request_ref, row_ref):
    values = tokens_ref[...]
    total = jnp.sum(values * values, axis=-1, keepdims=True)
    out_ref[...] = jnp.broadcast_to(total, out_ref.shape)
    place = place_ref[0]
    core_ref[...] = jnp.full(core_ref.shape, lax.rem(place, 2))
    request_ref[...] = jnp.full(request_ref.shape, lax.div(place, team))
    row_ref[...] = jnp.full(row_ref.shape, lax.rem(place, team) * row_count)


def norm_kernel(first, x_ref, gain_ref, *refs):
    out_refs, (held_ref, sems) = refs[:-2], refs[-2:]
    blocks, rows, width = out_refs[0].shape
    features = blocks * width
    groups = len(out_refs) * rows // GROUP_ROWS
    tiles = width // LANES

    def copy(g):
        return pltpu.make_async_copy(
            x_ref.at[pl.ds(first + g * GROUP_ROWS, GROUP_ROWS), :], held_ref.at[g], sems.at[g]
        )

    def factor_of(g):
        totals = [jnp.zeros((GROUP_ROWS, LANES), jnp.float32) for _ in range(4)]
        for j in range(blocks * tiles):
            values = held_ref[g, :, j * LANES : (j + 1) * LANES].astype(jnp.float32)
            totals[j % 4] = totals[j % 4] + values * values
        total = (totals[0] + totals[1]) + (totals[2] + totals[3])
        mean = jnp.sum(total, axis=-1, keepdims=True) / features
        return jnp.broadcast_to(lax.rsqrt(mean + EPSILON), (GROUP_ROWS, LANES))

    def scale(g, factor, out_ref, row):
        part = pl.ds(pl.multiple_of(row, GROUP_ROWS), GROUP_ROWS)
        for b in range(blocks):
            for j in range(tiles):
                lanes = slice(j * LANES, (j + 1) * LANES)
                from_lane = b * width + j * LANES
                values = held_ref[g, :, from_lane : from_lane + LANES].astype(jnp.float32)
                out_ref[b, part, lanes] = (values * factor * gain_ref[b, :, lanes]).astype(
                    jnp.bfloat16
                )

    for g in range(groups):
        copy(g).start()
    copy(0).wait()

    factor = factor_of(0)
    for i, out_ref in enumerate(out_refs):
        start = i * rows // GROUP_ROWS
        stop = min(start + rows // GROUP_ROWS, groups - 1)

        def step(g, factor, out_ref=out_ref, start=start):
            copy(g + 1).wait()
            following = factor_of(g + 1)
            scale(g, factor, out_ref, (g - start) * GROUP_ROWS)
            return following

        factor = lax.fori_loop(start, stop, step, factor)
    scale(groups - 1, factor, out_refs[-1], rows - GROUP_ROWS)


def normalise(hidden, gains, first, parts):
    blocks, _, width = gains.shape
    groups = parts * NORM_ROWS // GROUP_ROWS
    return call(
        functools.partial(norm_kernel, first),
        "normalise",
        [IN_HBM, IN_VMEM],
        (shape((blocks, NORM_ROWS, width), jnp.bfloat16),) * parts,
        [
            pltpu.VMEM((groups, GROUP_ROWS, blocks * width), jnp.bfloat16),
            pltpu.SemaphoreType.DMA((groups,)),
        ],
    )(pltpu.with_memory_space_constraint(hidden, pltpu.HBM), gains)


def query_kernel(
    features, place_ref, squares_ref, tokens_ref, gains_ref, query_ref, key_ref, value_ref, out_ref
):
    requests = tokens_ref.shape[0]
    factor = lax.rsqrt(squares_ref[:, :1] / features + EPSILON)
    normed = (tokens_ref[...] * factor * gains_ref[place_ref[0]]).astype(jnp.bfloat16)
    row = 0
    for weight_ref in (query_ref, key_ref, value_ref):
        part = jnp.dot(normed, weight_ref[...], preferred_element_type=jnp.float32)
        for h in range(weight_ref.shape[1] // LANES):
            for r in range(requests):
                out_ref[r, row : row + 1, :] = part[r : r + 1, h * LANES : (h + 1) * LANES]
            row += 1


def blocks_dot(distances, place, row_refs, block_refs, total):
    for (even, odd), block_ref in zip(distances, block_refs):
        distance = jnp.where(lax.rem(place, 2) == 0, even, odd)
        rows = jnp.concatenate([ref[place ^ distance] for ref in row_refs], axis=0)
        part = jnp.dot(rows, block_ref[...], preferred_element_type=jnp.float32)
        total = part if total is None else total + part
    return total


def project_kernel(distances, row_count, has_total, place_ref, *refs):
    rows, refs = refs[:row_count], refs[row_count:]
    total = refs[len(distances)][...] if has_total else None
    refs[-1][...] = blocks_dot(distances, place_ref[0], rows, refs, total)


def project(place, rows, blocks, total=None):
    extra = [] if total is None else [total]
    row_count = sum(r.shape[1] for r in rows)
    return call(
        functools.partial(project_kernel, [d for d, _ in blocks], len(rows), total is not None),
        "project",
        [IN_SMEM] + [IN_VMEM] * (len(rows) + len(blocks) + len(extra)),
        shape((row_count, LANES)),
    )(place, *rows, *[block for _, block in blocks], *extra)


def live_rows(dims, team, place, lengths_ref):
    rows = dims[1]
    within = lax.rem(place, team) * rows + lax.broadcasted_iota(jnp.int32, dims, 1)
    return within < lengths_ref[lax.div(place, team)]


def score_kernel(team, place_ref, lengths_ref, *refs):
    keys_ref, cos_ref, sin_ref, new_cos_ref, new_sin_ref, summed_ref = refs[:6]
    masked_ref, top_ref, self_ref = refs[6:]
    place = place_ref[0]
    request = lax.div(place, team)
    heads = masked_ref.shape[0]
    scale = 1.0 / math.sqrt(LANES)
    turned = turn(
        summed_ref[...], new_cos_ref[pl.ds(request, 1), :], new_sin_ref[pl.ds(request, 1), :]
    ).astype(jnp.bfloat16)
    queries = turned[:heads]
    self_key = turned[heads : heads + 1].astype(jnp.float32)
    self_scores = (
        jnp.sum(queries.astype(jnp.float32) * self_key, axis=-1, keepdims=True) * scale
    )
    keys = turn(keys_ref[...], cos_ref[...], sin_ref[...]).astype(jnp.bfloat16)
    scores = (
        lax.dot_general(
            queries, keys, (((1,), (1,)), ((), ())), preferred_element_type=jnp.float32
        )
        * scale
    )
    masked = jnp.where(live_rows(scores.shape, team, place, lengths_ref), scores, FLOOR)
    masked_ref[...] = masked
    top = jnp.maximum(jnp.max(masked, axis=-1, keepdims=True), self_scores)
    top_ref[...] = jnp.broadcast_to(top, top_ref.shape)
    self_ref[...] = jnp.broadcast_to(self_scores, self_ref.shape)


def weigh_kernel(distances, row_count, team, place_ref, lengths_ref, *refs):
    rows, refs = refs[:row_count], refs[row_count:]
    blocks, refs = refs[: len(distances)], refs[len(distances) :]
    total_ref, masked_ref, top_ref, self_ref, summed_ref, out_ref = refs
    place = place_ref[0]
    heads = masked_ref.shape[0]
    masked = masked_ref[...]
    top = top_ref[:, :1]
    live = live_rows(masked.shape, team, place, lengths_ref)
    weights = jnp.where(live, jnp.exp(masked - top), 0.0).astype(jnp.bfloat16)
    self_weight = jnp.exp(self_ref[...] - top_ref[...]).astype(jnp.bfloat16).astype(jnp.float32)
    self_weight = jnp.where(lax.rem(place, team) == 0, self_weight, 0.0)
    self_value = summed_ref[heads + 1 : heads + 2, :].astype(jnp.bfloat16).astype(jnp.float32)
    mass = jnp.sum(weights.astype(jnp.float32), axis=-1, keepdims=True) + self_weight
    values = blocks_dot(distances, place, rows, blocks, total_ref[...]).astype(jnp.bfloat16)
    accum = jnp.dot(weights, values, preferred_element_type=jnp.float32)
    out_ref[:, :LANES] = accum + self_weight * self_value
    out_ref[:, LANES:] = mass


def output_kernel(team, place_ref, mine_ref, other_ref, weight_ref, out_ref):
    request = lax.div(place_ref[0], team)
    heads = mine_ref.shape[0]
    attended = []
    for ref in (mine_ref, other_ref):
        attended.append(ref[:, :LANES] / ref[:, LANES:])
    first = jnp.where(request == 0, attended[0], attended[1]).astype(jnp.bfloat16)
    second = jnp.where(request == 0, attended[1], attended[0]).astype(jnp.bfloat16)
    both = jnp.concatenate(
        [
            jnp.concatenate((first[h : h + 1], second[h : h + 1]), axis=0)
            for h in range(heads)
        ],
        axis=1,
    )
    out_ref[...] = jnp.dot(both, weight_ref[...], preferred_element_type=jnp.float32)


def shards(
    new_tokens,
    ctx_hidden,
    norm_gain,
    query_weight,
    key_weight,
    value_weight,
    out_weight,
    lengths,
    positions,
):
    ctx_count = lax.axis_size("ctx")
    kv_count = lax.axis_size("kv")
    place = lax.axis_index("ctx").astype(jnp.int32)
    places = place.reshape(1)
    row_count, features = ctx_hidden.shape[1:]
    head_size = key_weight.shape[2]
    heads = query_weight.shape[2] // head_size
    requests, width = new_tokens.shape
    slot_count = row_count * ctx_count // requests
    team = slot_count // row_count
    assert requests == 2 and slot_count % row_count == 0 and row_count % NORM_ROWS == 0
    assert head_size == LANES
    gains = norm_gain.reshape(ctx_count, 1, width)

    split = ctx_count == 8
    chip_bits = bits_below(ctx_count)[1:]
    rows = []
    squares, core, own_request, first_row = call(
        functools.partial(squares_kernel, team, row_count),
        "squares",
        [IN_SMEM, IN_VMEM],
        (shape((requests, LANES)),) + (shape((1, LANES), jnp.int32),) * 3,
    )(places, new_tokens)

    def beside(received, sent, parts):
        first = len(rows) * NORM_ROWS
        rows.extend(normalise(after(ctx_hidden[0], sent), gains, first, parts))
        return after(received, rows[-1])

    def sum_chips(value, norm_parts=0):
        received = by_core(value, 4, 2)
        if norm_parts:
            received = beside(received, value, norm_parts)
        told = swap(received, "ctx", 1)
        opposite = by_core(told, 4, 2)
        if norm_parts:
            opposite = beside(opposite, told, row_count // NORM_ROWS - norm_parts)
        over_x = jnp.where(core == 0, told, received)
        over_y = jnp.where(core == 0, received, told)
        return (value + over_x) + (over_y + opposite), told

    key_partner = swap(key_weight[0], "ctx", 1)
    value_partner = swap(value_weight[0], "ctx", 1)
    key_near = [((0, 0), key_weight[0]), ((1, 1), key_partner)]
    value_near = [((0, 0), value_weight[0]), ((1, 1), value_partner)]
    key_far = send_first(key_weight[0], key_partner)

    squares = squares + swap(squares, "ctx", 1)
    squares = after(squares, key_partner, value_partner)
    if split:
        squares, told = sum_chips(squares, row_count // NORM_ROWS // 2)
        key_shared = share(key_far, told)
        squares = after(squares, key_far[1][1], key_shared[0][1])
    else:
        key_shared = share(key_far)
        squares = beside(squares, squares, row_count // NORM_ROWS)
        squares = butterfly(squares, "ctx", chip_bits, jnp.add)
    key_last = send_last(key_weight[0], key_shared)

    parts = call(
        functools.partial(query_kernel, features),
        "query_products",
        [IN_SMEM] + [IN_VMEM] * 6,
        shape((requests, heads + 2, head_size)),
    )(places, squares, new_tokens, gains, query_weight[0], key_weight[0], value_weight[0])
    parts = parts + swap(parts, "ctx", 1)
    parts_sent = parts
    value_far = send_first(value_weight[0], after(value_partner, parts))
    if split:
        parts, _ = sum_chips(parts)
        summed = jnp.where(own_request == 0, parts[0], parts[1])
    else:
        own_part = jnp.where(own_request == 0, parts[0], parts[1])
        other_part = jnp.where(own_request == 0, parts[1], parts[0])
        summed = own_part + swap(other_part, "ctx", team)
        summed = butterfly(summed, "ctx", chip_bits[:-1], jnp.add)

    key_total = project(places, rows, key_near)
    key_total = project(places, rows, key_far + key_shared, key_total)
    key_total = project(places, rows, key_last + share(key_last), key_total)

    within = first_row[0, :1] + jnp.arange(row_count, dtype=jnp.int32)
    cosine, sine_part = tables(within.astype(jnp.float32), head_size)
    new_cosine, new_sine = tables(positions.astype(jnp.float32), head_size)
    masked, top, self_scores = call(
        functools.partial(score_kernel, team),
        "scores",
        [IN_SMEM] * 2 + [IN_VMEM] * 6,
        (shape((heads, row_count)), shape((heads, LANES)), shape((heads, LANES))),
    )(places, lengths, key_total, cosine, sine_part, new_cosine, new_sine, summed)
    top = butterfly(top, "ctx", [1], jnp.maximum)
    near_top = top
    top = butterfly(top, "ctx", bits_below(team)[1:], jnp.maximum)

    value_shared = share(value_far, parts_sent)
    value_last = send_last(value_weight[0], value_shared)
    value_total = project(after(places, near_top), rows, value_near)
    value_total = project(after(places, top), rows, value_far + value_shared, value_total)

    blocks = value_last + share(value_last, value_total)
    packed = call(
        functools.partial(weigh_kernel, [d for d, _ in blocks], len(rows), team),
        "weighted_values",
        [IN_SMEM] * 2 + [IN_VMEM] * (len(rows) + len(blocks) + 5),
        shape((heads, 2 * head_size)),
    )(
        places,
        lengths,
        *rows,
        *[block for _, block in blocks],
        value_total,
        masked,
        top,
        self_scores,
        summed,
    )
    packed = butterfly(packed, "ctx", bits_below(team), jnp.add)
    other = swap(packed, "ctx", team)
    update = call(
        functools.partial(output_kernel, team),
        "output_products",
        [IN_SMEM] + [IN_VMEM] * 3,
        shape((requests, out_weight.shape[2])),
    )(places, packed, other, out_weight[0])
    return new_tokens + butterfly(update, "kv", bits_below(kv_count), jnp.add)


def solution(mesh):
    in_specs = (
        P(None, "ctx"),
        P(None, "ctx", None),
        P(),
        P(None, "ctx", "kv"),
        P(None, "ctx", "kv"),
        P(None, "ctx", "kv"),
        P(None, "kv", "ctx"),
        P(),
        P(),
    )
    out_specs = P(None, "ctx")
    return jax.shard_map(shards, mesh=mesh, in_specs=in_specs, out_specs=out_specs, check_vma=False)
```

```python
import functools
import math

import jax
import jax.numpy as jnp
from jax import lax
from jax.experimental import pallas as pl
from jax.experimental.pallas import tpu as pltpu
from jax.sharding import PartitionSpec as P

ROPE_BASE = 500000.0
EPSILON = 1e-05
FLOOR = -1e30
LANES = 128
NORM_ROWS = 64
GROUP_ROWS = 16
VMEM_BYTES = 16 * 1024 * 1024
CHEAP = pl.CostEstimate(flops=1000, bytes_accessed=1000, transcendentals=0)
IN_VMEM = pl.BlockSpec(memory_space=pltpu.VMEM)
IN_SMEM = pl.BlockSpec(memory_space=pltpu.SMEM)
IN_ANY = pl.BlockSpec(memory_space=pl.ANY)
IN_HBM = pl.BlockSpec(memory_space=pltpu.HBM)


def call(kernel, name, in_specs, out_shape, scratch_shapes=()):
    return pl.pallas_call(
        kernel,
        in_specs=in_specs,
        out_specs=jax.tree.map(lambda _: IN_VMEM, out_shape),
        out_shape=out_shape,
        scratch_shapes=scratch_shapes,
        compiler_params=pltpu.CompilerParams(vmem_limit_bytes=VMEM_BYTES),
        cost_estimate=CHEAP,
        name=name,
    )


def shape(dims, dtype=jnp.float32):
    return jax.ShapeDtypeStruct(dims, dtype)


def swap(value, axis, distance):
    count = lax.axis_size(axis)
    return lax.ppermute(value, axis, [(i, i ^ distance) for i in range(count)])


def after(value, *others):
    return lax.optimization_barrier((value, *others))[0]


def bits_below(count):
    return [1 << b for b in range(count.bit_length() - 1)]


def butterfly(value, axis, bits, join):
    for bit in bits:
        value = join(value, swap(value, axis, bit))
    return value


def by_core(value, bit_0, bit_1):
    count = lax.axis_size("ctx")
    bits = (bit_0, bit_1)
    pairs = [(i, i ^ bits[i % 2]) for i in range(count) if bits[i % 2]]
    return lax.ppermute(value, "ctx", pairs)


def tables(placed, head_size):
    half_size = head_size // 2
    frequency = jnp.exp(
        jnp.arange(half_size, dtype=jnp.float32) * (-2.0 * math.log(ROPE_BASE) / head_size)
    )
    angles = placed[..., None] * frequency
    return jnp.cos(angles), jnp.sin(angles)


def turn(values, cosine, sine_part):
    half_size = values.shape[-1] // 2
    leading = values[:, :half_size]
    trailing = values[:, half_size:]
    return jnp.concatenate(
        (leading * cosine - trailing * sine_part, trailing * cosine + leading * sine_part), axis=-1
    )


def squares_kernel(team, row_count, place_ref, tokens_ref, out_ref, core_ref, request_ref, row_ref):
    values = tokens_ref[...]
    total = jnp.sum(values * values, axis=-1, keepdims=True)
    out_ref[...] = jnp.broadcast_to(total, out_ref.shape)
    place = place_ref[0]
    core_ref[...] = jnp.full(core_ref.shape, lax.rem(place, 2))
    request_ref[...] = jnp.full(request_ref.shape, lax.div(place, team))
    row_ref[...] = jnp.full(row_ref.shape, lax.rem(place, team) * row_count)


def norm_kernel(first, x_ref, gain_ref, *refs):
    out_refs, (held_ref, sems) = refs[:-2], refs[-2:]
    blocks, rows, width = out_refs[0].shape
    features = blocks * width
    groups = len(out_refs) * rows // GROUP_ROWS
    tiles = width // LANES

    def copy(g):
        return pltpu.make_async_copy(
            x_ref.at[pl.ds(first + g * GROUP_ROWS, GROUP_ROWS), :], held_ref.at[g], sems.at[g]
        )

    def factor_of(g):
        totals = [jnp.zeros((GROUP_ROWS, LANES), jnp.float32) for _ in range(4)]
        for j in range(blocks * tiles):
            values = held_ref[g, :, j * LANES : (j + 1) * LANES].astype(jnp.float32)
            totals[j % 4] = totals[j % 4] + values * values
        total = (totals[0] + totals[1]) + (totals[2] + totals[3])
        mean = jnp.sum(total, axis=-1, keepdims=True) / features
        return jnp.broadcast_to(lax.rsqrt(mean + EPSILON), (GROUP_ROWS, LANES))

    def scale(g, factor, out_ref, row):
        part = pl.ds(pl.multiple_of(row, GROUP_ROWS), GROUP_ROWS)
        for b in range(blocks):
            for j in range(tiles):
                lanes = slice(j * LANES, (j + 1) * LANES)
                from_lane = b * width + j * LANES
                values = held_ref[g, :, from_lane : from_lane + LANES].astype(jnp.float32)
                out_ref[b, part, lanes] = (values * factor * gain_ref[b, :, lanes]).astype(
                    jnp.bfloat16
                )

    for g in range(groups):
        copy(g).start()
    copy(0).wait()

    factor = factor_of(0)
    for i, out_ref in enumerate(out_refs):
        start = i * rows // GROUP_ROWS
        stop = min(start + rows // GROUP_ROWS, groups - 1)

        def step(g, factor, out_ref=out_ref, start=start):
            copy(g + 1).wait()
            following = factor_of(g + 1)
            scale(g, factor, out_ref, (g - start) * GROUP_ROWS)
            return following

        factor = lax.fori_loop(start, stop, step, factor)
    scale(groups - 1, factor, out_refs[-1], rows - GROUP_ROWS)


def normalise(hidden, gains, first, parts):
    blocks, _, width = gains.shape
    groups = parts * NORM_ROWS // GROUP_ROWS
    return call(
        functools.partial(norm_kernel, first),
        "normalise",
        [IN_HBM, IN_VMEM],
        (shape((blocks, NORM_ROWS, width), jnp.bfloat16),) * parts,
        [
            pltpu.VMEM((groups, GROUP_ROWS, blocks * width), jnp.bfloat16),
            pltpu.SemaphoreType.DMA((groups,)),
        ],
    )(pltpu.with_memory_space_constraint(hidden, pltpu.HBM), gains)


def join_kernel(*refs):
    ins, (out_ref, sems) = refs[:-2], refs[-2:]
    rows = ins[0].shape[0]
    copies = [
        pltpu.make_async_copy(ref, out_ref.at[pl.ds(i * rows, rows), :], sems.at[i])
        for i, ref in enumerate(ins)
    ]
    for copy in copies:
        copy.start()
    for copy in copies:
        copy.wait()


def join(*arrays):
    rows, columns = arrays[0].shape
    return call(
        join_kernel,
        "join",
        [IN_ANY] * len(arrays),
        shape((len(arrays) * rows, columns), arrays[0].dtype),
        [pltpu.SemaphoreType.DMA((len(arrays),))],
    )(*arrays)


def query_kernel(
    features, place_ref, squares_ref, tokens_ref, gains_ref, query_ref, key_ref, value_ref, out_ref
):
    requests = tokens_ref.shape[0]
    factor = lax.rsqrt(squares_ref[:, :1] / features + EPSILON)
    normed = (tokens_ref[...] * factor * gains_ref[place_ref[0]]).astype(jnp.bfloat16)
    row = 0
    for weight_ref in (query_ref, key_ref, value_ref):
        part = jnp.dot(normed, weight_ref[...], preferred_element_type=jnp.float32)
        for h in range(weight_ref.shape[1] // LANES):
            for r in range(requests):
                out_ref[r, row : row + 1, :] = part[r : r + 1, h * LANES : (h + 1) * LANES]
            row += 1


def blocks_dot(pieces, place, row_refs, block_refs, total):
    for ((even, odd), first), block_ref in zip(pieces, block_refs):
        distance = jnp.where(lax.rem(place, 2) == 0, even, odd)
        rows = jnp.concatenate([ref[place ^ distance] for ref in row_refs], axis=0)
        block = block_ref[first : first + rows.shape[1], :]
        part = jnp.dot(rows, block, preferred_element_type=jnp.float32)
        total = part if total is None else total + part
    return total


def project_kernel(pieces, row_count, has_total, place_ref, *refs):
    rows, refs = refs[:row_count], refs[row_count:]
    total = refs[len(pieces)][...] if has_total else None
    refs[-1][...] = blocks_dot(pieces, place_ref[0], rows, refs, total)


def project(place, rows, blocks, total=None):
    extra = [] if total is None else [total]
    row_count = sum(r.shape[1] for r in rows)
    return call(
        functools.partial(project_kernel, [b[1:] for b in blocks], len(rows), total is not None),
        "project",
        [IN_SMEM] + [IN_VMEM] * (len(rows) + len(blocks) + len(extra)),
        shape((row_count, LANES)),
    )(place, *rows, *[b[0] for b in blocks], *extra)


def live_rows(dims, team, place, lengths_ref):
    rows = dims[1]
    within = lax.rem(place, team) * rows + lax.broadcasted_iota(jnp.int32, dims, 1)
    return within < lengths_ref[lax.div(place, team)]


def score_kernel(team, place_ref, lengths_ref, *refs):
    keys_ref, cos_ref, sin_ref, new_cos_ref, new_sin_ref, summed_ref = refs[:6]
    masked_ref, top_ref, self_ref = refs[6:]
    place = place_ref[0]
    request = lax.div(place, team)
    heads = masked_ref.shape[0]
    scale = 1.0 / math.sqrt(LANES)
    turned = turn(
        summed_ref[...], new_cos_ref[pl.ds(request, 1), :], new_sin_ref[pl.ds(request, 1), :]
    ).astype(jnp.bfloat16)
    queries = turned[:heads]
    self_key = turned[heads : heads + 1].astype(jnp.float32)
    self_scores = (
        jnp.sum(queries.astype(jnp.float32) * self_key, axis=-1, keepdims=True) * scale
    )
    keys = turn(keys_ref[...], cos_ref[...], sin_ref[...]).astype(jnp.bfloat16)
    scores = (
        lax.dot_general(
            queries, keys, (((1,), (1,)), ((), ())), preferred_element_type=jnp.float32
        )
        * scale
    )
    masked = jnp.where(live_rows(scores.shape, team, place, lengths_ref), scores, FLOOR)
    masked_ref[...] = masked
    top = jnp.maximum(jnp.max(masked, axis=-1, keepdims=True), self_scores)
    top_ref[...] = jnp.broadcast_to(top, top_ref.shape)
    self_ref[...] = jnp.broadcast_to(self_scores, self_ref.shape)


def weigh_kernel(pieces, row_count, team, place_ref, lengths_ref, *refs):
    rows, refs = refs[:row_count], refs[row_count:]
    blocks, refs = refs[: len(pieces)], refs[len(pieces) :]
    total_ref, masked_ref, top_ref, self_ref, summed_ref, out_ref = refs
    place = place_ref[0]
    heads = masked_ref.shape[0]
    masked = masked_ref[...]
    top = top_ref[:, :1]
    live = live_rows(masked.shape, team, place, lengths_ref)
    weights = jnp.where(live, jnp.exp(masked - top), 0.0).astype(jnp.bfloat16)
    self_weight = jnp.exp(self_ref[...] - top_ref[...]).astype(jnp.bfloat16).astype(jnp.float32)
    self_weight = jnp.where(lax.rem(place, team) == 0, self_weight, 0.0)
    self_value = summed_ref[heads + 1 : heads + 2, :].astype(jnp.bfloat16).astype(jnp.float32)
    mass = jnp.sum(weights.astype(jnp.float32), axis=-1, keepdims=True) + self_weight
    values = blocks_dot(pieces, place, rows, blocks, total_ref[...]).astype(jnp.bfloat16)
    accum = jnp.dot(weights, values, preferred_element_type=jnp.float32)
    out_ref[:, :LANES] = accum + self_weight * self_value
    out_ref[:, LANES:] = mass


def output_kernel(team, place_ref, sums_ref, weight_ref, out_ref):
    request = lax.div(place_ref[0], team)
    heads = sums_ref.shape[0] // 2
    attended = []
    for own in (slice(0, heads), slice(heads, 2 * heads)):
        attended.append(sums_ref[own, :LANES] / sums_ref[own, LANES:])
    first = jnp.where(request == 0, attended[0], attended[1]).astype(jnp.bfloat16)
    second = jnp.where(request == 0, attended[1], attended[0]).astype(jnp.bfloat16)
    both = jnp.concatenate(
        [
            jnp.concatenate((first[h : h + 1], second[h : h + 1]), axis=0)
            for h in range(heads)
        ],
        axis=1,
    )
    out_ref[...] = jnp.dot(both, weight_ref[...], preferred_element_type=jnp.float32)


def shards(
    new_tokens,
    ctx_hidden,
    norm_gain,
    query_weight,
    key_weight,
    value_weight,
    out_weight,
    lengths,
    positions,
):
    ctx_count = lax.axis_size("ctx")
    kv_count = lax.axis_size("kv")
    place = lax.axis_index("ctx").astype(jnp.int32)
    places = place.reshape(1)
    row_count, features = ctx_hidden.shape[1:]
    head_size = key_weight.shape[2]
    heads = query_weight.shape[2] // head_size
    requests, width = new_tokens.shape
    slot_count = row_count * ctx_count // requests
    team = slot_count // row_count
    assert requests == 2 and slot_count % row_count == 0 and row_count % NORM_ROWS == 0
    assert head_size == LANES
    gains = norm_gain.reshape(ctx_count, 1, width)

    split = ctx_count == 8
    chip_bits = bits_below(ctx_count)[1:]
    rows = []
    squares, core, own_request, first_row = call(
        functools.partial(squares_kernel, team, row_count),
        "squares",
        [IN_SMEM, IN_VMEM],
        (shape((requests, LANES)),) + (shape((1, LANES), jnp.int32),) * 3,
    )(places, new_tokens)

    def normalise_next(parts, sent):
        first = len(rows) * NORM_ROWS
        rows.extend(normalise(after(ctx_hidden[0], sent), gains, first, parts))

    def sum_chips(value, norm_parts=(0, 0)):
        received = by_core(value, 4, 2)
        if norm_parts[0]:
            normalise_next(norm_parts[0], value)
            received = after(received, rows[-1])
        told = swap(received, "ctx", 1)
        opposite = by_core(told, 4, 2)
        if norm_parts[1]:
            normalise_next(norm_parts[1], told)
            opposite = after(opposite, rows[-1])
        over_x = jnp.where(core == 0, told, received)
        over_y = jnp.where(core == 0, received, told)
        return (value + over_x) + (over_y + opposite), told

    own_key, own_value = key_weight[0], value_weight[0]
    key_partner = swap(own_key, "ctx", 1)
    value_partner = swap(own_value, "ctx", 1)
    squares = squares + swap(squares, "ctx", 1)
    squares = after(squares, key_partner, value_partner)
    norm_calls = row_count // NORM_ROWS
    if split:
        key_far = by_core(join(own_key, key_partner), 2, 4)
        squares, _ = sum_chips(squares, (2, norm_calls - 2))
        key_told = swap(after(key_far, squares), "ctx", 1)
        value_far = by_core(join(own_value, value_partner), 2, 4)
        key_last = by_core(key_told[:width], 2, 4)
    else:
        normalise_next(norm_calls, squares)
        squares = butterfly(squares, "ctx", chip_bits, jnp.add)

    parts = call(
        functools.partial(query_kernel, features),
        "query_products",
        [IN_SMEM] + [IN_VMEM] * 6,
        shape((requests, heads + 2, head_size)),
    )(places, squares, new_tokens, gains, query_weight[0], key_weight[0], value_weight[0])
    parts = parts + swap(parts, "ctx", 1)
    if split:
        parts, told = sum_chips(parts)
        summed = jnp.where(own_request == 0, parts[0], parts[1])
    else:
        own_part = jnp.where(own_request == 0, parts[0], parts[1])
        other_part = jnp.where(own_request == 0, parts[1], parts[0])
        summed = own_part + swap(other_part, "ctx", team)
        summed = butterfly(summed, "ctx", chip_bits[:-1], jnp.add)

    key_total = project(
        places, rows, [(own_key, (0, 0), 0), (key_partner, (1, 1), 0)]
    )
    if split:
        blocks = [
            (key_far, (2, 4), 0),
            (key_far, (3, 5), width),
            (key_told, (5, 3), 0),
            (key_told, (4, 2), width),
        ]
        key_total = project(places, rows, blocks, key_total)
        value_told = swap(after(value_far, told), "ctx", 1)
        value_last = by_core(value_told[:width], 2, 4)
        shared = swap(after(key_last, key_total), "ctx", 1)
        blocks = [(key_last, (7, 7), 0), (shared, (6, 6), 0)]
        key_total = project(places, rows, blocks, key_total)
    else:
        blocks = [(swap(own_key, "ctx", d), (d, d), 0) for d in range(2, ctx_count)]
        key_total = project(places, rows, blocks, key_total)

    within = first_row[0, :1] + jnp.arange(row_count, dtype=jnp.int32)
    cosine, sine_part = tables(within.astype(jnp.float32), head_size)
    new_cosine, new_sine = tables(positions.astype(jnp.float32), head_size)
    masked, top, self_scores = call(
        functools.partial(score_kernel, team),
        "scores",
        [IN_SMEM] * 2 + [IN_VMEM] * 6,
        (shape((heads, row_count)), shape((heads, LANES)), shape((heads, LANES))),
    )(places, lengths, key_total, cosine, sine_part, new_cosine, new_sine, summed)
    top = butterfly(top, "ctx", [1], jnp.maximum)
    near_top = top
    top = butterfly(top, "ctx", bits_below(team)[1:], jnp.maximum)

    value_total = project(
        after(places, near_top), rows, [(own_value, (0, 0), 0), (value_partner, (1, 1), 0)]
    )
    if split:
        blocks = [
            (value_far, (2, 4), 0),
            (value_far, (3, 5), width),
            (value_told, (5, 3), 0),
            (value_told, (4, 2), width),
        ]
        value_total = project(after(places, top), rows, blocks, value_total)
        blocks = [(swap(after(value_last, value_total), "ctx", 1), (6, 6), 0)]
        value_total = project(places, rows, [(value_last, (7, 7), 0)], value_total)
    else:
        blocks = [(swap(own_value, "ctx", d), (d, d), 0) for d in range(2, ctx_count)]
    packed = call(
        functools.partial(weigh_kernel, [b[1:] for b in blocks], len(rows), team),
        "weighted_values",
        [IN_SMEM] * 2 + [IN_VMEM] * (len(rows) + len(blocks) + 5),
        shape((heads, 2 * head_size)),
    )(
        places,
        lengths,
        *rows,
        *[b[0] for b in blocks],
        value_total,
        masked,
        top,
        self_scores,
        summed,
    )
    if split:
        packed = packed + swap(packed, "ctx", 1)
        packed = packed + by_core(packed, 0, 2)
        sums = jnp.concatenate((packed, by_core(packed, 0, 4)), axis=0)
        told = lax.ppermute(sums, "ctx", [(i, i ^ 1) for i in range(1, ctx_count, 2)])
        sums = jnp.where(core[:, :1] == 0, told, sums)
    else:
        packed = butterfly(packed, "ctx", bits_below(team), jnp.add)
        sums = jnp.concatenate((packed, swap(packed, "ctx", team)), axis=0)
    update = call(
        functools.partial(output_kernel, team),
        "output_products",
        [IN_SMEM] + [IN_VMEM] * 2,
        shape((requests, out_weight.shape[2])),
    )(places, sums, out_weight[0])
    return new_tokens + butterfly(update, "kv", bits_below(kv_count), jnp.add)


def solution(mesh):
    in_specs = (
        P(None, "ctx"),
        P(None, "ctx", None),
        P(),
        P(None, "ctx", "kv"),
        P(None, "ctx", "kv"),
        P(None, "ctx", "kv"),
        P(None, "kv", "ctx"),
        P(),
        P(),
    )
    out_specs = P(None, "ctx")
    return jax.shard_map(shards, mesh=mesh, in_specs=in_specs, out_specs=out_specs, check_vma=False)
```

```python
import functools
import math

import jax
import jax.numpy as jnp
from jax import lax
from jax.experimental import pallas as pl
from jax.experimental.pallas import tpu as pltpu
from jax.sharding import PartitionSpec as P

ROPE_BASE = 500000.0
EPSILON = 1e-05
FLOOR = -1e30
LANES = 128
NORM_ROWS = 64
GROUP_ROWS = 16
VMEM_BYTES = 16 * 1024 * 1024
CHEAP = pl.CostEstimate(flops=1000, bytes_accessed=1000, transcendentals=0)
IN_VMEM = pl.BlockSpec(memory_space=pltpu.VMEM)
IN_SMEM = pl.BlockSpec(memory_space=pltpu.SMEM)
IN_HBM = pl.BlockSpec(memory_space=pltpu.HBM)


def call(kernel, name, in_specs, out_shape, scratch_shapes=()):
    return pl.pallas_call(
        kernel,
        in_specs=in_specs,
        out_specs=jax.tree.map(lambda _: IN_VMEM, out_shape),
        out_shape=out_shape,
        scratch_shapes=scratch_shapes,
        compiler_params=pltpu.CompilerParams(vmem_limit_bytes=VMEM_BYTES),
        cost_estimate=CHEAP,
        name=name,
    )


def shape(dims, dtype=jnp.float32):
    return jax.ShapeDtypeStruct(dims, dtype)


def swap(value, axis, distance):
    count = lax.axis_size(axis)
    return lax.ppermute(value, axis, [(i, i ^ distance) for i in range(count)])


def after(value, *others):
    return lax.optimization_barrier((value, *others))[0]


def bits_below(count):
    return [1 << b for b in range(count.bit_length() - 1)]


def butterfly(value, axis, bits, join):
    for bit in bits:
        value = join(value, swap(value, axis, bit))
    return value


def by_core(value, bit_0, bit_1):
    count = lax.axis_size("ctx")
    bits = (bit_0, bit_1)
    pairs = [(i, i ^ bits[i % 2]) for i in range(count) if bits[i % 2]]
    return lax.ppermute(value, "ctx", pairs)


def send_first(own, partner):
    count = lax.axis_size("ctx")
    if count != 8:
        return [((d, d), swap(own, "ctx", d)) for d in range(2, count // 2)]
    return [((2, 4), by_core(own, 2, 4)), ((3, 5), by_core(partner, 2, 4))]


def share(blocks, *before):
    count = lax.axis_size("ctx")
    if count != 8:
        return []
    return [
        ((odd ^ 1, even ^ 1), swap(after(block, *before) if before else block, "ctx", 1))
        for (even, odd), block in blocks
    ]


def send_last(own, received):
    count = lax.axis_size("ctx")
    if count != 8:
        return [((d, d), swap(own, "ctx", d)) for d in range(count // 2, count)]
    return [((7, 7), by_core(received[0][1], 2, 4))]


def tables(placed, head_size):
    half_size = head_size // 2
    frequency = jnp.exp(
        jnp.arange(half_size, dtype=jnp.float32) * (-2.0 * math.log(ROPE_BASE) / head_size)
    )
    angles = placed[..., None] * frequency
    return jnp.cos(angles), jnp.sin(angles)


def turn(values, cosine, sine_part):
    half_size = values.shape[-1] // 2
    leading = values[:, :half_size]
    trailing = values[:, half_size:]
    return jnp.concatenate(
        (leading * cosine - trailing * sine_part, trailing * cosine + leading * sine_part), axis=-1
    )


def squares_kernel(team, row_count, place_ref, tokens_ref, out_ref, core_ref, request_ref, row_ref):
    values = tokens_ref[...]
    total = jnp.sum(values * values, axis=-1, keepdims=True)
    out_ref[...] = jnp.broadcast_to(total, out_ref.shape)
    place = place_ref[0]
    core_ref[...] = jnp.full(core_ref.shape, lax.rem(place, 2))
    request_ref[...] = jnp.full(request_ref.shape, lax.div(place, team))
    row_ref[...] = jnp.full(row_ref.shape, lax.rem(place, team) * row_count)


def norm_kernel(first, x_ref, gain_ref, *refs):
    out_refs, (held_ref, sems) = refs[:-2], refs[-2:]
    blocks, rows, width = out_refs[0].shape
    features = blocks * width
    groups = len(out_refs) * rows // GROUP_ROWS
    tiles = width // LANES

    def copy(g):
        return pltpu.make_async_copy(
            x_ref.at[pl.ds(first + g * GROUP_ROWS, GROUP_ROWS), :], held_ref.at[g], sems.at[g]
        )

    def factor_of(g):
        totals = [jnp.zeros((GROUP_ROWS, LANES), jnp.float32) for _ in range(4)]
        for j in range(blocks * tiles):
            values = held_ref[g, :, j * LANES : (j + 1) * LANES].astype(jnp.float32)
            totals[j % 4] = totals[j % 4] + values * values
        total = (totals[0] + totals[1]) + (totals[2] + totals[3])
        mean = jnp.sum(total, axis=-1, keepdims=True) / features
        return jnp.broadcast_to(lax.rsqrt(mean + EPSILON), (GROUP_ROWS, LANES))

    def scale(g, factor, out_ref, row):
        part = pl.ds(pl.multiple_of(row, GROUP_ROWS), GROUP_ROWS)
        for b in range(blocks):
            for j in range(tiles):
                lanes = slice(j * LANES, (j + 1) * LANES)
                from_lane = b * width + j * LANES
                values = held_ref[g, :, from_lane : from_lane + LANES].astype(jnp.float32)
                out_ref[b, part, lanes] = (values * factor * gain_ref[b, :, lanes]).astype(
                    jnp.bfloat16
                )

    for g in range(groups):
        copy(g).start()
    copy(0).wait()

    factor = factor_of(0)
    for i, out_ref in enumerate(out_refs):
        start = i * rows // GROUP_ROWS
        stop = min(start + rows // GROUP_ROWS, groups - 1)

        def step(g, factor, out_ref=out_ref, start=start):
            copy(g + 1).wait()
            following = factor_of(g + 1)
            scale(g, factor, out_ref, (g - start) * GROUP_ROWS)
            return following

        factor = lax.fori_loop(start, stop, step, factor)
    scale(groups - 1, factor, out_refs[-1], rows - GROUP_ROWS)


def normalise(hidden, gains, first, parts):
    blocks, _, width = gains.shape
    groups = parts * NORM_ROWS // GROUP_ROWS
    return call(
        functools.partial(norm_kernel, first),
        "normalise",
        [IN_HBM, IN_VMEM],
        (shape((blocks, NORM_ROWS, width), jnp.bfloat16),) * parts,
        [
            pltpu.VMEM((groups, GROUP_ROWS, blocks * width), jnp.bfloat16),
            pltpu.SemaphoreType.DMA((groups,)),
        ],
    )(pltpu.with_memory_space_constraint(hidden, pltpu.HBM), gains)


def query_kernel(
    features, place_ref, squares_ref, tokens_ref, gains_ref, query_ref, key_ref, value_ref, out_ref
):
    requests = tokens_ref.shape[0]
    factor = lax.rsqrt(squares_ref[:, :1] / features + EPSILON)
    normed = (tokens_ref[...] * factor * gains_ref[place_ref[0]]).astype(jnp.bfloat16)
    row = 0
    for weight_ref in (query_ref, key_ref, value_ref):
        part = jnp.dot(normed, weight_ref[...], preferred_element_type=jnp.float32)
        for h in range(weight_ref.shape[1] // LANES):
            for r in range(requests):
                out_ref[r, row : row + 1, :] = part[r : r + 1, h * LANES : (h + 1) * LANES]
            row += 1


def blocks_dot(distances, place, row_refs, block_refs, total):
    for (even, odd), block_ref in zip(distances, block_refs):
        distance = jnp.where(lax.rem(place, 2) == 0, even, odd)
        rows = jnp.concatenate([ref[place ^ distance] for ref in row_refs], axis=0)
        part = jnp.dot(rows, block_ref[...], preferred_element_type=jnp.float32)
        total = part if total is None else total + part
    return total


def project_kernel(distances, row_count, has_total, place_ref, *refs):
    rows, refs = refs[:row_count], refs[row_count:]
    total = refs[len(distances)][...] if has_total else None
    refs[-1][...] = blocks_dot(distances, place_ref[0], rows, refs, total)


def project(place, rows, blocks, total=None):
    extra = [] if total is None else [total]
    row_count = sum(r.shape[1] for r in rows)
    return call(
        functools.partial(project_kernel, [d for d, _ in blocks], len(rows), total is not None),
        "project",
        [IN_SMEM] + [IN_VMEM] * (len(rows) + len(blocks) + len(extra)),
        shape((row_count, LANES)),
    )(place, *rows, *[block for _, block in blocks], *extra)


def live_rows(dims, team, place, lengths_ref):
    rows = dims[1]
    within = lax.rem(place, team) * rows + lax.broadcasted_iota(jnp.int32, dims, 1)
    return within < lengths_ref[lax.div(place, team)]


def score_kernel(team, place_ref, lengths_ref, *refs):
    keys_ref, cos_ref, sin_ref, new_cos_ref, new_sin_ref, summed_ref = refs[:6]
    masked_ref, top_ref, self_ref = refs[6:]
    place = place_ref[0]
    request = lax.div(place, team)
    heads = masked_ref.shape[0]
    scale = 1.0 / math.sqrt(LANES)
    turned = turn(
        summed_ref[...], new_cos_ref[pl.ds(request, 1), :], new_sin_ref[pl.ds(request, 1), :]
    ).astype(jnp.bfloat16)
    queries = turned[:heads]
    self_key = turned[heads : heads + 1].astype(jnp.float32)
    self_scores = (
        jnp.sum(queries.astype(jnp.float32) * self_key, axis=-1, keepdims=True) * scale
    )
    keys = turn(keys_ref[...], cos_ref[...], sin_ref[...]).astype(jnp.bfloat16)
    scores = (
        lax.dot_general(
            queries, keys, (((1,), (1,)), ((), ())), preferred_element_type=jnp.float32
        )
        * scale
    )
    masked = jnp.where(live_rows(scores.shape, team, place, lengths_ref), scores, FLOOR)
    masked_ref[...] = masked
    top = jnp.maximum(jnp.max(masked, axis=-1, keepdims=True), self_scores)
    top_ref[...] = jnp.broadcast_to(top, top_ref.shape)
    self_ref[...] = jnp.broadcast_to(self_scores, self_ref.shape)


def weigh_kernel(distances, row_count, team, place_ref, lengths_ref, *refs):
    rows, refs = refs[:row_count], refs[row_count:]
    blocks, refs = refs[: len(distances)], refs[len(distances) :]
    total_ref, masked_ref, top_ref, self_ref, summed_ref, out_ref = refs
    place = place_ref[0]
    heads = masked_ref.shape[0]
    masked = masked_ref[...]
    top = top_ref[:, :1]
    live = live_rows(masked.shape, team, place, lengths_ref)
    weights = jnp.where(live, jnp.exp(masked - top), 0.0).astype(jnp.bfloat16)
    self_weight = jnp.exp(self_ref[...] - top_ref[...]).astype(jnp.bfloat16).astype(jnp.float32)
    self_weight = jnp.where(lax.rem(place, team) == 0, self_weight, 0.0)
    self_value = summed_ref[heads + 1 : heads + 2, :].astype(jnp.bfloat16).astype(jnp.float32)
    mass = jnp.sum(weights.astype(jnp.float32), axis=-1, keepdims=True) + self_weight
    values = blocks_dot(distances, place, rows, blocks, total_ref[...]).astype(jnp.bfloat16)
    accum = jnp.dot(weights, values, preferred_element_type=jnp.float32)
    out_ref[:, :LANES] = accum + self_weight * self_value
    out_ref[:, LANES:] = mass


def output_kernel(team, place_ref, mine_ref, other_ref, weight_ref, out_ref):
    request = lax.div(place_ref[0], team)
    heads = mine_ref.shape[0]
    attended = []
    for ref in (mine_ref, other_ref):
        attended.append(ref[:, :LANES] / ref[:, LANES:])
    first = jnp.where(request == 0, attended[0], attended[1]).astype(jnp.bfloat16)
    second = jnp.where(request == 0, attended[1], attended[0]).astype(jnp.bfloat16)
    both = jnp.concatenate(
        [
            jnp.concatenate((first[h : h + 1], second[h : h + 1]), axis=0)
            for h in range(heads)
        ],
        axis=1,
    )
    out_ref[...] = jnp.dot(both, weight_ref[...], preferred_element_type=jnp.float32)


def shards(
    new_tokens,
    ctx_hidden,
    norm_gain,
    query_weight,
    key_weight,
    value_weight,
    out_weight,
    lengths,
    positions,
):
    ctx_count = lax.axis_size("ctx")
    kv_count = lax.axis_size("kv")
    place = lax.axis_index("ctx").astype(jnp.int32)
    places = place.reshape(1)
    row_count, features = ctx_hidden.shape[1:]
    head_size = key_weight.shape[2]
    heads = query_weight.shape[2] // head_size
    requests, width = new_tokens.shape
    slot_count = row_count * ctx_count // requests
    team = slot_count // row_count
    assert requests == 2 and slot_count % row_count == 0 and row_count % NORM_ROWS == 0
    assert head_size == LANES
    gains = norm_gain.reshape(ctx_count, 1, width)

    split = ctx_count == 8
    chip_bits = bits_below(ctx_count)[1:]
    rows = []
    squares, core, own_request, first_row = call(
        functools.partial(squares_kernel, team, row_count),
        "squares",
        [IN_SMEM, IN_VMEM],
        (shape((requests, LANES)),) + (shape((1, LANES), jnp.int32),) * 3,
    )(places, new_tokens)

    def beside(received, sent, parts):
        first = len(rows) * NORM_ROWS
        rows.extend(normalise(after(ctx_hidden[0], sent), gains, first, parts))
        return after(received, rows[-1])

    def sum_chips(value, norm_parts=0):
        received = by_core(value, 4, 2)
        if norm_parts:
            received = beside(received, value, norm_parts)
        told = swap(received, "ctx", 1)
        opposite = by_core(told, 4, 2)
        if norm_parts:
            opposite = beside(opposite, told, row_count // NORM_ROWS - norm_parts)
        over_x = jnp.where(core == 0, told, received)
        over_y = jnp.where(core == 0, received, told)
        return (value + over_x) + (over_y + opposite), told, received

    key_partner = swap(key_weight[0], "ctx", 1)
    value_partner = swap(value_weight[0], "ctx", 1)
    key_near = [((0, 0), key_weight[0]), ((1, 1), key_partner)]
    value_near = [((0, 0), value_weight[0]), ((1, 1), value_partner)]
    key_far = send_first(key_weight[0], key_partner)

    squares = squares + swap(squares, "ctx", 1)
    squares = after(squares, key_partner, value_partner)
    if split:
        squares, told, _ = sum_chips(squares, row_count // NORM_ROWS // 2)
        key_shared = share(key_far, told)
        squares = after(squares, key_far[1][1], key_shared[0][1])
    else:
        key_shared = share(key_far)
        squares = beside(squares, squares, row_count // NORM_ROWS)
        squares = butterfly(squares, "ctx", chip_bits, jnp.add)
    key_last = send_last(key_weight[0], key_shared)

    parts = call(
        functools.partial(query_kernel, features),
        "query_products",
        [IN_SMEM] + [IN_VMEM] * 6,
        shape((requests, heads + 2, head_size)),
    )(places, squares, new_tokens, gains, query_weight[0], key_weight[0], value_weight[0])
    parts = parts + swap(parts, "ctx", 1)
    parts_sent = parts
    value_far = send_first(value_weight[0], after(value_partner, parts))
    if split:
        parts, _, parts_sent = sum_chips(parts)
        summed = jnp.where(own_request == 0, parts[0], parts[1])
    else:
        own_part = jnp.where(own_request == 0, parts[0], parts[1])
        other_part = jnp.where(own_request == 0, parts[1], parts[0])
        summed = own_part + swap(other_part, "ctx", team)
        summed = butterfly(summed, "ctx", chip_bits[:-1], jnp.add)

    key_total = project(places, rows, key_near)
    key_total = project(places, rows, key_far + key_shared, key_total)
    key_mid = key_total
    key_total = project(places, rows, key_last + share(key_last), key_total)

    within = first_row[0, :1] + jnp.arange(row_count, dtype=jnp.int32)
    cosine, sine_part = tables(within.astype(jnp.float32), head_size)
    new_cosine, new_sine = tables(positions.astype(jnp.float32), head_size)
    masked, top, self_scores = call(
        functools.partial(score_kernel, team),
        "scores",
        [IN_SMEM] * 2 + [IN_VMEM] * 6,
        (shape((heads, row_count)), shape((heads, LANES)), shape((heads, LANES))),
    )(places, lengths, key_total, cosine, sine_part, new_cosine, new_sine, summed)
    top = butterfly(top, "ctx", [1], jnp.maximum)
    near_top = top
    top = butterfly(top, "ctx", bits_below(team)[1:], jnp.maximum)

    value_shared = share(value_far[:1], parts_sent)
    value_last = send_last(value_weight[0], value_shared)
    value_shared += share(value_far[1:], key_mid, *[block for _, block in value_shared])
    value_total = project(after(places, near_top), rows, value_near)
    value_total = project(after(places, top), rows, value_far + value_shared, value_total)

    blocks = share(value_last, value_total)
    value_total = project(places, rows, value_last, value_total)
    packed = call(
        functools.partial(weigh_kernel, [d for d, _ in blocks], len(rows), team),
        "weighted_values",
        [IN_SMEM] * 2 + [IN_VMEM] * (len(rows) + len(blocks) + 5),
        shape((heads, 2 * head_size)),
    )(
        places,
        lengths,
        *rows,
        *[block for _, block in blocks],
        value_total,
        masked,
        top,
        self_scores,
        summed,
    )
    packed = butterfly(packed, "ctx", bits_below(team), jnp.add)
    other = swap(packed, "ctx", team)
    update = call(
        functools.partial(output_kernel, team),
        "output_products",
        [IN_SMEM] + [IN_VMEM] * 3,
        shape((requests, out_weight.shape[2])),
    )(places, packed, other, out_weight[0])
    return new_tokens + butterfly(update, "kv", bits_below(kv_count), jnp.add)


def solution(mesh):
    in_specs = (
        P(None, "ctx"),
        P(None, "ctx", None),
        P(),
        P(None, "ctx", "kv"),
        P(None, "ctx", "kv"),
        P(None, "ctx", "kv"),
        P(None, "kv", "ctx"),
        P(),
        P(),
    )
    out_specs = P(None, "ctx")
    return jax.shard_map(shards, mesh=mesh, in_specs=in_specs, out_specs=out_specs, check_vma=False)
```

```python
import functools
import math

import jax
import jax.numpy as jnp
from jax import lax
from jax.experimental import pallas as pl
from jax.experimental.pallas import tpu as pltpu
from jax.sharding import PartitionSpec as P

ROPE_BASE = 500000.0
EPSILON = 1e-05
FLOOR = -1e30
LANES = 128
NORM_ROWS = 64
GROUP_ROWS = 16
VMEM_BYTES = 16 * 1024 * 1024
CHEAP = pl.CostEstimate(flops=1000, bytes_accessed=1000, transcendentals=0)
IN_VMEM = pl.BlockSpec(memory_space=pltpu.VMEM)
IN_SMEM = pl.BlockSpec(memory_space=pltpu.SMEM)
IN_HBM = pl.BlockSpec(memory_space=pltpu.HBM)


def call(kernel, name, in_specs, out_shape, scratch_shapes=()):
    return pl.pallas_call(
        kernel,
        in_specs=in_specs,
        out_specs=jax.tree.map(lambda _: IN_VMEM, out_shape),
        out_shape=out_shape,
        scratch_shapes=scratch_shapes,
        compiler_params=pltpu.CompilerParams(vmem_limit_bytes=VMEM_BYTES),
        cost_estimate=CHEAP,
        name=name,
    )


def shape(dims, dtype=jnp.float32):
    return jax.ShapeDtypeStruct(dims, dtype)


def swap(value, axis, distance):
    count = lax.axis_size(axis)
    return lax.ppermute(value, axis, [(i, i ^ distance) for i in range(count)])


def after(value, *others):
    return lax.optimization_barrier((value, *others))[0]


def bits_below(count):
    return [1 << b for b in range(count.bit_length() - 1)]


def butterfly(value, axis, bits, join):
    for bit in bits:
        value = join(value, swap(value, axis, bit))
    return value


def by_core(value, bit_0, bit_1):
    count = lax.axis_size("ctx")
    bits = (bit_0, bit_1)
    pairs = [(i, i ^ bits[i % 2]) for i in range(count) if bits[i % 2]]
    return lax.ppermute(value, "ctx", pairs)


def send_first(own, partner):
    count = lax.axis_size("ctx")
    if count != 8:
        return [((d, d), swap(own, "ctx", d)) for d in range(2, count // 2)]
    return [((2, 4), by_core(own, 2, 4)), ((3, 5), by_core(partner, 2, 4))]


def share(blocks, *before):
    count = lax.axis_size("ctx")
    if count != 8:
        return []
    return [
        ((odd ^ 1, even ^ 1), swap(after(block, *before) if before else block, "ctx", 1))
        for (even, odd), block in blocks
    ]


def send_last(own, received):
    count = lax.axis_size("ctx")
    if count != 8:
        return [((d, d), swap(own, "ctx", d)) for d in range(count // 2, count)]
    return [((7, 7), by_core(received[0][1], 2, 4))]


def tables(placed, head_size):
    half_size = head_size // 2
    frequency = jnp.exp(
        jnp.arange(half_size, dtype=jnp.float32) * (-2.0 * math.log(ROPE_BASE) / head_size)
    )
    angles = placed[..., None] * frequency
    return jnp.cos(angles), jnp.sin(angles)


def turn(values, cosine, sine_part):
    half_size = values.shape[-1] // 2
    leading = values[:, :half_size]
    trailing = values[:, half_size:]
    return jnp.concatenate(
        (leading * cosine - trailing * sine_part, trailing * cosine + leading * sine_part), axis=-1
    )


def squares_kernel(team, row_count, place_ref, tokens_ref, out_ref, core_ref, request_ref, row_ref):
    values = tokens_ref[...]
    total = jnp.sum(values * values, axis=-1, keepdims=True)
    out_ref[...] = jnp.broadcast_to(total, out_ref.shape)
    place = place_ref[0]
    core_ref[...] = jnp.full(core_ref.shape, lax.rem(place, 2))
    request_ref[...] = jnp.full(request_ref.shape, lax.div(place, team))
    row_ref[...] = jnp.full(row_ref.shape, lax.rem(place, team) * row_count)


def norm_kernel(first, x_ref, gain_ref, *refs):
    out_refs, (held_ref, sems) = refs[:-2], refs[-2:]
    blocks, rows, width = out_refs[0].shape
    features = blocks * width
    groups = len(out_refs) * rows // GROUP_ROWS
    tiles = width // LANES

    def copy(g):
        return pltpu.make_async_copy(
            x_ref.at[pl.ds(first + g * GROUP_ROWS, GROUP_ROWS), :], held_ref.at[g], sems.at[g]
        )

    def factor_of(g):
        totals = [jnp.zeros((GROUP_ROWS, LANES), jnp.float32) for _ in range(4)]
        for j in range(blocks * tiles):
            values = held_ref[g, :, j * LANES : (j + 1) * LANES].astype(jnp.float32)
            totals[j % 4] = totals[j % 4] + values * values
        total = (totals[0] + totals[1]) + (totals[2] + totals[3])
        mean = jnp.sum(total, axis=-1, keepdims=True) / features
        return jnp.broadcast_to(lax.rsqrt(mean + EPSILON), (GROUP_ROWS, LANES))

    def scale(g, factor, out_ref, row):
        part = pl.ds(pl.multiple_of(row, GROUP_ROWS), GROUP_ROWS)
        for b in range(blocks):
            for j in range(tiles):
                lanes = slice(j * LANES, (j + 1) * LANES)
                from_lane = b * width + j * LANES
                values = held_ref[g, :, from_lane : from_lane + LANES].astype(jnp.float32)
                out_ref[b, part, lanes] = (values * factor * gain_ref[b, :, lanes]).astype(
                    jnp.bfloat16
                )

    for g in range(groups):
        copy(g).start()
    copy(0).wait()

    factor = factor_of(0)
    for i, out_ref in enumerate(out_refs):
        start = i * rows // GROUP_ROWS
        stop = min(start + rows // GROUP_ROWS, groups - 1)

        def step(g, factor, out_ref=out_ref, start=start):
            copy(g + 1).wait()
            following = factor_of(g + 1)
            scale(g, factor, out_ref, (g - start) * GROUP_ROWS)
            return following

        factor = lax.fori_loop(start, stop, step, factor)
    scale(groups - 1, factor, out_refs[-1], rows - GROUP_ROWS)


def normalise(hidden, gains, first, parts):
    blocks, _, width = gains.shape
    groups = parts * NORM_ROWS // GROUP_ROWS
    return call(
        functools.partial(norm_kernel, first),
        "normalise",
        [IN_HBM, IN_VMEM],
        (shape((blocks, NORM_ROWS, width), jnp.bfloat16),) * parts,
        [
            pltpu.VMEM((groups, GROUP_ROWS, blocks * width), jnp.bfloat16),
            pltpu.SemaphoreType.DMA((groups,)),
        ],
    )(pltpu.with_memory_space_constraint(hidden, pltpu.HBM), gains)


def query_kernel(
    features, place_ref, squares_ref, tokens_ref, gains_ref, query_ref, key_ref, value_ref, out_ref
):
    requests = tokens_ref.shape[0]
    factor = lax.rsqrt(squares_ref[:, :1] / features + EPSILON)
    normed = (tokens_ref[...] * factor * gains_ref[place_ref[0]]).astype(jnp.bfloat16)
    row = 0
    for weight_ref in (query_ref, key_ref, value_ref):
        part = jnp.dot(normed, weight_ref[...], preferred_element_type=jnp.float32)
        for h in range(weight_ref.shape[1] // LANES):
            for r in range(requests):
                out_ref[r, row : row + 1, :] = part[r : r + 1, h * LANES : (h + 1) * LANES]
            row += 1


def blocks_dot(distances, place, row_refs, block_refs, total):
    for (even, odd), block_ref in zip(distances, block_refs):
        distance = jnp.where(lax.rem(place, 2) == 0, even, odd)
        rows = jnp.concatenate([ref[place ^ distance] for ref in row_refs], axis=0)
        part = jnp.dot(rows, block_ref[...], preferred_element_type=jnp.float32)
        total = part if total is None else total + part
    return total


def project_kernel(distances, row_count, has_total, place_ref, *refs):
    rows, refs = refs[:row_count], refs[row_count:]
    total = refs[len(distances)][...] if has_total else None
    refs[-1][...] = blocks_dot(distances, place_ref[0], rows, refs, total)


def project(place, rows, blocks, total=None):
    extra = [] if total is None else [total]
    row_count = sum(r.shape[1] for r in rows)
    return call(
        functools.partial(project_kernel, [d for d, _ in blocks], len(rows), total is not None),
        "project",
        [IN_SMEM] + [IN_VMEM] * (len(rows) + len(blocks) + len(extra)),
        shape((row_count, LANES)),
    )(place, *rows, *[block for _, block in blocks], *extra)


def live_rows(dims, team, place, lengths_ref):
    rows = dims[1]
    within = lax.rem(place, team) * rows + lax.broadcasted_iota(jnp.int32, dims, 1)
    return within < lengths_ref[lax.div(place, team)]


def score_kernel(team, place_ref, lengths_ref, *refs):
    keys_ref, cos_ref, sin_ref, new_cos_ref, new_sin_ref, summed_ref = refs[:6]
    masked_ref, top_ref, self_ref = refs[6:]
    place = place_ref[0]
    request = lax.div(place, team)
    heads = masked_ref.shape[0]
    scale = 1.0 / math.sqrt(LANES)
    turned = turn(
        summed_ref[...], new_cos_ref[pl.ds(request, 1), :], new_sin_ref[pl.ds(request, 1), :]
    ).astype(jnp.bfloat16)
    queries = turned[:heads]
    self_key = turned[heads : heads + 1].astype(jnp.float32)
    self_scores = (
        jnp.sum(queries.astype(jnp.float32) * self_key, axis=-1, keepdims=True) * scale
    )
    keys = turn(keys_ref[...], cos_ref[...], sin_ref[...]).astype(jnp.bfloat16)
    scores = (
        lax.dot_general(
            queries, keys, (((1,), (1,)), ((), ())), preferred_element_type=jnp.float32
        )
        * scale
    )
    masked = jnp.where(live_rows(scores.shape, team, place, lengths_ref), scores, FLOOR)
    masked_ref[...] = masked
    top = jnp.maximum(jnp.max(masked, axis=-1, keepdims=True), self_scores)
    top_ref[...] = jnp.broadcast_to(top, top_ref.shape)
    self_ref[...] = jnp.broadcast_to(self_scores, self_ref.shape)


def weigh_kernel(distances, row_count, team, place_ref, lengths_ref, *refs):
    rows, refs = refs[:row_count], refs[row_count:]
    blocks, refs = refs[: len(distances)], refs[len(distances) :]
    total_ref, masked_ref, top_ref, self_ref, summed_ref, out_ref = refs
    place = place_ref[0]
    heads = masked_ref.shape[0]
    masked = masked_ref[...]
    top = top_ref[:, :1]
    live = live_rows(masked.shape, team, place, lengths_ref)
    weights = jnp.where(live, jnp.exp(masked - top), 0.0).astype(jnp.bfloat16)
    self_weight = jnp.exp(self_ref[...] - top_ref[...]).astype(jnp.bfloat16).astype(jnp.float32)
    self_weight = jnp.where(lax.rem(place, team) == 0, self_weight, 0.0)
    self_value = summed_ref[heads + 1 : heads + 2, :].astype(jnp.bfloat16).astype(jnp.float32)
    mass = jnp.sum(weights.astype(jnp.float32), axis=-1, keepdims=True) + self_weight
    values = blocks_dot(distances, place, rows, blocks, total_ref[...]).astype(jnp.bfloat16)
    accum = jnp.dot(weights, values, preferred_element_type=jnp.float32)
    out_ref[:, :LANES] = accum + self_weight * self_value
    out_ref[:, LANES:] = mass


def output_kernel(team, place_ref, mine_ref, other_ref, weight_ref, out_ref):
    request = lax.div(place_ref[0], team)
    heads = mine_ref.shape[0]
    attended = []
    for ref in (mine_ref, other_ref):
        attended.append(ref[:, :LANES] / ref[:, LANES:])
    first = jnp.where(request == 0, attended[0], attended[1]).astype(jnp.bfloat16)
    second = jnp.where(request == 0, attended[1], attended[0]).astype(jnp.bfloat16)
    both = jnp.concatenate(
        [
            jnp.concatenate((first[h : h + 1], second[h : h + 1]), axis=0)
            for h in range(heads)
        ],
        axis=1,
    )
    out_ref[...] = jnp.dot(both, weight_ref[...], preferred_element_type=jnp.float32)


def shards(
    new_tokens,
    ctx_hidden,
    norm_gain,
    query_weight,
    key_weight,
    value_weight,
    out_weight,
    lengths,
    positions,
):
    ctx_count = lax.axis_size("ctx")
    kv_count = lax.axis_size("kv")
    place = lax.axis_index("ctx").astype(jnp.int32)
    places = place.reshape(1)
    row_count, features = ctx_hidden.shape[1:]
    head_size = key_weight.shape[2]
    heads = query_weight.shape[2] // head_size
    requests, width = new_tokens.shape
    slot_count = row_count * ctx_count // requests
    team = slot_count // row_count
    assert requests == 2 and slot_count % row_count == 0 and row_count % NORM_ROWS == 0
    assert head_size == LANES
    gains = norm_gain.reshape(ctx_count, 1, width)

    split = ctx_count == 8
    chip_bits = bits_below(ctx_count)[1:]
    rows = []
    squares, core, own_request, first_row = call(
        functools.partial(squares_kernel, team, row_count),
        "squares",
        [IN_SMEM, IN_VMEM],
        (shape((requests, LANES)),) + (shape((1, LANES), jnp.int32),) * 3,
    )(places, new_tokens)

    def beside(received, sent, parts):
        first = len(rows) * NORM_ROWS
        rows.extend(normalise(after(ctx_hidden[0], sent), gains, first, parts))
        return after(received, rows[-1])

    def sum_chips(value, norm_parts=0):
        received = by_core(value, 4, 2)
        if norm_parts:
            received = beside(received, value, norm_parts)
        told = swap(received, "ctx", 1)
        opposite = by_core(told, 4, 2)
        if norm_parts:
            opposite = beside(opposite, told, row_count // NORM_ROWS - norm_parts)
        over_x = jnp.where(core == 0, told, received)
        over_y = jnp.where(core == 0, received, told)
        return (value + over_x) + (over_y + opposite), told, received

    key_partner = swap(key_weight[0], "ctx", 1)
    value_partner = swap(value_weight[0], "ctx", 1)
    key_near = [((0, 0), key_weight[0]), ((1, 1), key_partner)]
    value_near = [((0, 0), value_weight[0]), ((1, 1), value_partner)]
    key_far = send_first(key_weight[0], key_partner)

    squares = squares + swap(squares, "ctx", 1)
    squares = after(squares, key_partner, value_partner)
    if split:
        squares, told, _ = sum_chips(squares, row_count // NORM_ROWS // 2)
        key_shared = share(key_far, told)
        own_values = after(value_weight[0], key_far[0][1])
        squares = after(squares, key_far[1][1], key_shared[0][1])
    else:
        key_shared = share(key_far)
        own_values = value_weight[0]
        squares = beside(squares, squares, row_count // NORM_ROWS)
        squares = butterfly(squares, "ctx", chip_bits, jnp.add)
    key_last = send_last(key_weight[0], key_shared)

    parts = call(
        functools.partial(query_kernel, features),
        "query_products",
        [IN_SMEM] + [IN_VMEM] * 6,
        shape((requests, heads + 2, head_size)),
    )(places, squares, new_tokens, gains, query_weight[0], key_weight[0], value_weight[0])
    parts = parts + swap(parts, "ctx", 1)
    parts_sent = parts
    value_far = send_first(own_values, after(value_partner, parts))
    if split:
        parts, _, parts_sent = sum_chips(parts)
        summed = jnp.where(own_request == 0, parts[0], parts[1])
    else:
        own_part = jnp.where(own_request == 0, parts[0], parts[1])
        other_part = jnp.where(own_request == 0, parts[1], parts[0])
        summed = own_part + swap(other_part, "ctx", team)
        summed = butterfly(summed, "ctx", chip_bits[:-1], jnp.add)

    key_total = project(places, rows, key_near)
    key_total = project(places, rows, key_far + key_shared, key_total)
    key_mid = key_total
    key_total = project(places, rows, key_last + share(key_last), key_total)

    within = first_row[0, :1] + jnp.arange(row_count, dtype=jnp.int32)
    cosine, sine_part = tables(within.astype(jnp.float32), head_size)
    new_cosine, new_sine = tables(positions.astype(jnp.float32), head_size)
    masked, top, self_scores = call(
        functools.partial(score_kernel, team),
        "scores",
        [IN_SMEM] * 2 + [IN_VMEM] * 6,
        (shape((heads, row_count)), shape((heads, LANES)), shape((heads, LANES))),
    )(places, lengths, key_total, cosine, sine_part, new_cosine, new_sine, summed)
    value_mid = value_far[:1] + share(value_far[:1], parts_sent)
    value_next = send_last(own_values, value_mid[1:])
    top = butterfly(top, "ctx", [1], jnp.maximum)
    top = after(top, *[block for _, block in value_next])
    near_top = top
    if split:
        received = jnp.maximum(top, after(by_core(top, 4, 2), value_far[1][1]))
        top = jnp.where(core == 0, swap(received, "ctx", 1), received)
    else:
        top = butterfly(top, "ctx", bits_below(team)[1:], jnp.maximum)
        received = top

    value_mid += value_next + share(value_next, near_top)
    value_total = project(after(places, near_top), rows, value_near)
    value_total = project(places, rows, value_mid, value_total)

    blocks = share(value_far[1:], received)
    if blocks:
        value_total = project(places, rows, value_far[1:], value_total)
    else:
        blocks = value_far[1:]
    packed = call(
        functools.partial(weigh_kernel, [d for d, _ in blocks], len(rows), team),
        "weighted_values",
        [IN_SMEM] * 2 + [IN_VMEM] * (len(rows) + len(blocks) + 5),
        shape((heads, 2 * head_size)),
    )(
        places,
        lengths,
        *rows,
        *[block for _, block in blocks],
        value_total,
        masked,
        top,
        self_scores,
        summed,
    )
    packed = butterfly(packed, "ctx", bits_below(team), jnp.add)
    other = swap(packed, "ctx", team)
    update = call(
        functools.partial(output_kernel, team),
        "output_products",
        [IN_SMEM] + [IN_VMEM] * 3,
        shape((requests, out_weight.shape[2])),
    )(places, packed, other, out_weight[0])
    return new_tokens + butterfly(update, "kv", bits_below(kv_count), jnp.add)


def solution(mesh):
    in_specs = (
        P(None, "ctx"),
        P(None, "ctx", None),
        P(),
        P(None, "ctx", "kv"),
        P(None, "ctx", "kv"),
        P(None, "ctx", "kv"),
        P(None, "kv", "ctx"),
        P(),
        P(),
    )
    out_specs = P(None, "ctx")
    return jax.shard_map(shards, mesh=mesh, in_specs=in_specs, out_specs=out_specs, check_vma=False)
```

```python
import functools
import math

import jax
import jax.numpy as jnp
from jax import lax
from jax.experimental import pallas as pl
from jax.experimental.pallas import tpu as pltpu
from jax.sharding import PartitionSpec as P

ROPE_BASE = 500000.0
EPSILON = 1e-05
FLOOR = -1e30
LANES = 128
NORM_ROWS = 64
GROUP_ROWS = 16
VMEM_BYTES = 16 * 1024 * 1024
CHEAP = pl.CostEstimate(flops=1000, bytes_accessed=1000, transcendentals=0)
IN_VMEM = pl.BlockSpec(memory_space=pltpu.VMEM)
IN_SMEM = pl.BlockSpec(memory_space=pltpu.SMEM)
IN_HBM = pl.BlockSpec(memory_space=pltpu.HBM)


def call(kernel, name, in_specs, out_shape, scratch_shapes=()):
    return pl.pallas_call(
        kernel,
        in_specs=in_specs,
        out_specs=jax.tree.map(lambda _: IN_VMEM, out_shape),
        out_shape=out_shape,
        scratch_shapes=scratch_shapes,
        compiler_params=pltpu.CompilerParams(vmem_limit_bytes=VMEM_BYTES),
        cost_estimate=CHEAP,
        name=name,
    )


def shape(dims, dtype=jnp.float32):
    return jax.ShapeDtypeStruct(dims, dtype)


def swap(value, axis, distance):
    count = lax.axis_size(axis)
    return lax.ppermute(value, axis, [(i, i ^ distance) for i in range(count)])


def after(value, *others):
    return lax.optimization_barrier((value, *others))[0]


def bits_below(count):
    return [1 << b for b in range(count.bit_length() - 1)]


def butterfly(value, axis, bits, join):
    for bit in bits:
        value = join(value, swap(value, axis, bit))
    return value


def by_core(value, bit_0, bit_1):
    count = lax.axis_size("ctx")
    bits = (bit_0, bit_1)
    pairs = [(i, i ^ bits[i % 2]) for i in range(count) if bits[i % 2]]
    return lax.ppermute(value, "ctx", pairs)


def send_first(own, partner):
    count = lax.axis_size("ctx")
    if count != 8:
        return [((d, d), swap(own, "ctx", d)) for d in range(2, count // 2)]
    return [((2, 4), by_core(own, 2, 4)), ((3, 5), by_core(partner, 2, 4))]


def share(blocks, *before):
    count = lax.axis_size("ctx")
    if count != 8:
        return []
    return [
        ((odd ^ 1, even ^ 1), swap(after(block, *before) if before else block, "ctx", 1))
        for (even, odd), block in blocks
    ]


def send_last(own, received):
    count = lax.axis_size("ctx")
    if count != 8:
        return [((d, d), swap(own, "ctx", d)) for d in range(count // 2, count)]
    return [((7, 7), by_core(received[0][1], 2, 4))]


def tables(placed, head_size):
    half_size = head_size // 2
    frequency = jnp.exp(
        jnp.arange(half_size, dtype=jnp.float32) * (-2.0 * math.log(ROPE_BASE) / head_size)
    )
    angles = placed[..., None] * frequency
    return jnp.cos(angles), jnp.sin(angles)


def turn(values, cosine, sine_part):
    half_size = values.shape[-1] // 2
    leading = values[:, :half_size]
    trailing = values[:, half_size:]
    return jnp.concatenate(
        (leading * cosine - trailing * sine_part, trailing * cosine + leading * sine_part), axis=-1
    )


def squares_kernel(team, row_count, place_ref, tokens_ref, out_ref, core_ref, request_ref, row_ref):
    values = tokens_ref[...]
    total = jnp.sum(values * values, axis=-1, keepdims=True)
    out_ref[...] = jnp.broadcast_to(total, out_ref.shape)
    place = place_ref[0]
    core_ref[...] = jnp.full(core_ref.shape, lax.rem(place, 2))
    request_ref[...] = jnp.full(request_ref.shape, lax.div(place, team))
    row_ref[...] = jnp.full(row_ref.shape, lax.rem(place, team) * row_count)


def norm_kernel(first, x_ref, gain_ref, *refs):
    out_refs, (held_ref, sems) = refs[:-2], refs[-2:]
    blocks, rows, width = out_refs[0].shape
    features = blocks * width
    groups = len(out_refs) * rows // GROUP_ROWS
    tiles = width // LANES

    def copy(g):
        return pltpu.make_async_copy(
            x_ref.at[pl.ds(first + g * GROUP_ROWS, GROUP_ROWS), :], held_ref.at[g], sems.at[g]
        )

    def factor_of(g):
        totals = [jnp.zeros((GROUP_ROWS, LANES), jnp.float32) for _ in range(4)]
        for j in range(blocks * tiles):
            values = held_ref[g, :, j * LANES : (j + 1) * LANES].astype(jnp.float32)
            totals[j % 4] = totals[j % 4] + values * values
        total = (totals[0] + totals[1]) + (totals[2] + totals[3])
        mean = jnp.sum(total, axis=-1, keepdims=True) / features
        return jnp.broadcast_to(lax.rsqrt(mean + EPSILON), (GROUP_ROWS, LANES))

    def scale(g, factor, out_ref, row):
        part = pl.ds(pl.multiple_of(row, GROUP_ROWS), GROUP_ROWS)
        for b in range(blocks):
            for j in range(tiles):
                lanes = slice(j * LANES, (j + 1) * LANES)
                from_lane = b * width + j * LANES
                values = held_ref[g, :, from_lane : from_lane + LANES].astype(jnp.float32)
                out_ref[b, part, lanes] = (values * factor * gain_ref[b, :, lanes]).astype(
                    jnp.bfloat16
                )

    for g in range(groups):
        copy(g).start()
    copy(0).wait()

    factor = factor_of(0)
    for i, out_ref in enumerate(out_refs):
        start = i * rows // GROUP_ROWS
        stop = min(start + rows // GROUP_ROWS, groups - 1)

        def step(g, factor, out_ref=out_ref, start=start):
            copy(g + 1).wait()
            following = factor_of(g + 1)
            scale(g, factor, out_ref, (g - start) * GROUP_ROWS)
            return following

        factor = lax.fori_loop(start, stop, step, factor)
    scale(groups - 1, factor, out_refs[-1], rows - GROUP_ROWS)


def normalise(hidden, gains, first, parts):
    blocks, _, width = gains.shape
    groups = parts * NORM_ROWS // GROUP_ROWS
    return call(
        functools.partial(norm_kernel, first),
        "normalise",
        [IN_HBM, IN_VMEM],
        (shape((blocks, NORM_ROWS, width), jnp.bfloat16),) * parts,
        [
            pltpu.VMEM((groups, GROUP_ROWS, blocks * width), jnp.bfloat16),
            pltpu.SemaphoreType.DMA((groups,)),
        ],
    )(pltpu.with_memory_space_constraint(hidden, pltpu.HBM), gains)


def query_kernel(
    features, place_ref, squares_ref, tokens_ref, gains_ref, query_ref, key_ref, value_ref, out_ref
):
    requests = tokens_ref.shape[0]
    factor = lax.rsqrt(squares_ref[:, :1] / features + EPSILON)
    normed = (tokens_ref[...] * factor * gains_ref[place_ref[0]]).astype(jnp.bfloat16)
    row = 0
    for weight_ref in (query_ref, key_ref, value_ref):
        part = jnp.dot(normed, weight_ref[...], preferred_element_type=jnp.float32)
        for h in range(weight_ref.shape[1] // LANES):
            for r in range(requests):
                out_ref[r, row : row + 1, :] = part[r : r + 1, h * LANES : (h + 1) * LANES]
            row += 1


def blocks_dot(distances, place, row_refs, block_refs, total):
    for (even, odd), block_ref in zip(distances, block_refs):
        distance = jnp.where(lax.rem(place, 2) == 0, even, odd)
        rows = jnp.concatenate([ref[place ^ distance] for ref in row_refs], axis=0)
        part = jnp.dot(rows, block_ref[...], preferred_element_type=jnp.float32)
        total = part if total is None else total + part
    return total


def project_kernel(distances, row_count, has_total, place_ref, *refs):
    rows, refs = refs[:row_count], refs[row_count:]
    total = refs[len(distances)][...] if has_total else None
    refs[-1][...] = blocks_dot(distances, place_ref[0], rows, refs, total)


def project(place, rows, blocks, total=None):
    extra = [] if total is None else [total]
    row_count = sum(r.shape[1] for r in rows)
    return call(
        functools.partial(project_kernel, [d for d, _ in blocks], len(rows), total is not None),
        "project",
        [IN_SMEM] + [IN_VMEM] * (len(rows) + len(blocks) + len(extra)),
        shape((row_count, LANES)),
    )(place, *rows, *[block for _, block in blocks], *extra)


def live_rows(dims, team, place, lengths_ref):
    rows = dims[1]
    within = lax.rem(place, team) * rows + lax.broadcasted_iota(jnp.int32, dims, 1)
    return within < lengths_ref[lax.div(place, team)]


def score_kernel(team, place_ref, lengths_ref, *refs):
    keys_ref, cos_ref, sin_ref, new_cos_ref, new_sin_ref, summed_ref = refs[:6]
    masked_ref, top_ref, self_ref = refs[6:]
    place = place_ref[0]
    request = lax.div(place, team)
    heads = masked_ref.shape[0]
    scale = 1.0 / math.sqrt(LANES)
    turned = turn(
        summed_ref[...], new_cos_ref[pl.ds(request, 1), :], new_sin_ref[pl.ds(request, 1), :]
    ).astype(jnp.bfloat16)
    queries = turned[:heads]
    self_key = turned[heads : heads + 1].astype(jnp.float32)
    self_scores = (
        jnp.sum(queries.astype(jnp.float32) * self_key, axis=-1, keepdims=True) * scale
    )
    keys = turn(keys_ref[...], cos_ref[...], sin_ref[...]).astype(jnp.bfloat16)
    scores = (
        lax.dot_general(
            queries, keys, (((1,), (1,)), ((), ())), preferred_element_type=jnp.float32
        )
        * scale
    )
    masked = jnp.where(live_rows(scores.shape, team, place, lengths_ref), scores, FLOOR)
    masked_ref[...] = masked
    top = jnp.maximum(jnp.max(masked, axis=-1, keepdims=True), self_scores)
    top_ref[...] = jnp.broadcast_to(top, top_ref.shape)
    self_ref[...] = jnp.broadcast_to(self_scores, self_ref.shape)


def weigh_kernel(distances, row_count, team, place_ref, lengths_ref, *refs):
    rows, refs = refs[:row_count], refs[row_count:]
    blocks, refs = refs[: len(distances)], refs[len(distances) :]
    total_ref, masked_ref, top_ref, self_ref, summed_ref, out_ref = refs
    place = place_ref[0]
    heads = masked_ref.shape[0]
    masked = masked_ref[...]
    top = top_ref[:, :1]
    live = live_rows(masked.shape, team, place, lengths_ref)
    weights = jnp.where(live, jnp.exp(masked - top), 0.0).astype(jnp.bfloat16)
    self_weight = jnp.exp(self_ref[...] - top_ref[...]).astype(jnp.bfloat16).astype(jnp.float32)
    self_weight = jnp.where(lax.rem(place, team) == 0, self_weight, 0.0)
    self_value = summed_ref[heads + 1 : heads + 2, :].astype(jnp.bfloat16).astype(jnp.float32)
    mass = jnp.sum(weights.astype(jnp.float32), axis=-1, keepdims=True) + self_weight
    values = blocks_dot(distances, place, rows, blocks, total_ref[...]).astype(jnp.bfloat16)
    accum = jnp.dot(weights, values, preferred_element_type=jnp.float32)
    out_ref[:, :LANES] = accum + self_weight * self_value
    out_ref[:, LANES:] = mass


def output_kernel(team, place_ref, mine_ref, other_ref, weight_ref, out_ref):
    request = lax.div(place_ref[0], team)
    heads = mine_ref.shape[0]
    attended = []
    for ref in (mine_ref, other_ref):
        attended.append(ref[:, :LANES] / ref[:, LANES:])
    first = jnp.where(request == 0, attended[0], attended[1]).astype(jnp.bfloat16)
    second = jnp.where(request == 0, attended[1], attended[0]).astype(jnp.bfloat16)
    both = jnp.concatenate(
        [
            jnp.concatenate((first[h : h + 1], second[h : h + 1]), axis=0)
            for h in range(heads)
        ],
        axis=1,
    )
    out_ref[...] = jnp.dot(both, weight_ref[...], preferred_element_type=jnp.float32)


def shards(
    new_tokens,
    ctx_hidden,
    norm_gain,
    query_weight,
    key_weight,
    value_weight,
    out_weight,
    lengths,
    positions,
):
    ctx_count = lax.axis_size("ctx")
    kv_count = lax.axis_size("kv")
    place = lax.axis_index("ctx").astype(jnp.int32)
    places = place.reshape(1)
    row_count, features = ctx_hidden.shape[1:]
    head_size = key_weight.shape[2]
    heads = query_weight.shape[2] // head_size
    requests, width = new_tokens.shape
    slot_count = row_count * ctx_count // requests
    team = slot_count // row_count
    assert requests == 2 and slot_count % row_count == 0 and row_count % NORM_ROWS == 0
    assert head_size == LANES
    gains = norm_gain.reshape(ctx_count, 1, width)

    split = ctx_count == 8
    chip_bits = bits_below(ctx_count)[1:]
    rows = []
    squares, core, own_request, first_row = call(
        functools.partial(squares_kernel, team, row_count),
        "squares",
        [IN_SMEM, IN_VMEM],
        (shape((requests, LANES)),) + (shape((1, LANES), jnp.int32),) * 3,
    )(places, new_tokens)

    def beside(received, sent, parts):
        first = len(rows) * NORM_ROWS
        rows.extend(normalise(after(ctx_hidden[0], sent), gains, first, parts))
        return after(received, rows[-1])

    def sum_chips(value, norm_parts=0):
        received = by_core(value, 4, 2)
        if norm_parts:
            received = beside(received, value, norm_parts)
        told = swap(received, "ctx", 1)
        opposite = by_core(told, 4, 2)
        if norm_parts:
            opposite = beside(opposite, told, row_count // NORM_ROWS - norm_parts)
        over_x = jnp.where(core == 0, told, received)
        over_y = jnp.where(core == 0, received, told)
        return (value + over_x) + (over_y + opposite), told, received

    key_partner = swap(key_weight[0], "ctx", 1)
    value_partner = swap(value_weight[0], "ctx", 1)
    key_near = [((0, 0), key_weight[0]), ((1, 1), key_partner)]
    value_near = [((0, 0), value_weight[0]), ((1, 1), value_partner)]
    key_far = send_first(key_weight[0], key_partner)

    squares = squares + swap(squares, "ctx", 1)
    squares = after(squares, key_partner, value_partner)
    if split:
        squares, told, _ = sum_chips(squares, row_count // NORM_ROWS // 2)
        key_shared = share(key_far, told)
        own_values = after(value_weight[0], key_far[0][1])
        squares = after(squares, key_far[1][1], key_shared[0][1])
    else:
        key_shared = share(key_far)
        own_values = value_weight[0]
        squares = beside(squares, squares, row_count // NORM_ROWS)
        squares = butterfly(squares, "ctx", chip_bits, jnp.add)
    key_last = send_last(key_weight[0], key_shared)

    parts = call(
        functools.partial(query_kernel, features),
        "query_products",
        [IN_SMEM] + [IN_VMEM] * 6,
        shape((requests, heads + 2, head_size)),
    )(places, squares, new_tokens, gains, query_weight[0], key_weight[0], value_weight[0])
    parts = parts + swap(parts, "ctx", 1)
    parts_sent = parts
    value_far = send_first(own_values, after(value_partner, parts))
    if split:
        parts, _, parts_sent = sum_chips(parts)
        summed = jnp.where(own_request == 0, parts[0], parts[1])
    else:
        own_part = jnp.where(own_request == 0, parts[0], parts[1])
        other_part = jnp.where(own_request == 0, parts[1], parts[0])
        summed = own_part + swap(other_part, "ctx", team)
        summed = butterfly(summed, "ctx", chip_bits[:-1], jnp.add)

    key_total = project(places, rows, key_near)
    key_total = project(places, rows, key_far + key_shared, key_total)
    key_mid = key_total
    key_total = project(places, rows, key_last + share(key_last), key_total)

    within = first_row[0, :1] + jnp.arange(row_count, dtype=jnp.int32)
    cosine, sine_part = tables(within.astype(jnp.float32), head_size)
    new_cosine, new_sine = tables(positions.astype(jnp.float32), head_size)
    masked, top, self_scores = call(
        functools.partial(score_kernel, team),
        "scores",
        [IN_SMEM] * 2 + [IN_VMEM] * 6,
        (shape((heads, row_count)), shape((heads, LANES)), shape((heads, LANES))),
    )(places, lengths, key_total, cosine, sine_part, new_cosine, new_sine, summed)
    value_mid = value_far + share(value_far[:1], parts_sent)
    value_last = send_last(own_values, value_mid[-1:])
    top = butterfly(top, "ctx", [1], jnp.maximum)
    top = after(top, *[block for _, block in value_far[1:]])
    near_top = top
    if split:
        received = jnp.maximum(top, after(by_core(top, 4, 2), value_last[0][1]))
        top = jnp.where(core == 0, swap(received, "ctx", 1), received)
    else:
        top = butterfly(top, "ctx", bits_below(team)[1:], jnp.maximum)
        received = top

    value_mid += share(value_far[1:], near_top)
    value_total = project(after(places, near_top), rows, value_near)
    value_total = project(places, rows, value_mid, value_total)

    blocks = share(value_last, received)
    value_total = project(places, rows, value_last, value_total)
    packed = call(
        functools.partial(weigh_kernel, [d for d, _ in blocks], len(rows), team),
        "weighted_values",
        [IN_SMEM] * 2 + [IN_VMEM] * (len(rows) + len(blocks) + 5),
        shape((heads, 2 * head_size)),
    )(
        places,
        lengths,
        *rows,
        *[block for _, block in blocks],
        value_total,
        masked,
        top,
        self_scores,
        summed,
    )
    packed = butterfly(packed, "ctx", bits_below(team), jnp.add)
    other = swap(packed, "ctx", team)
    update = call(
        functools.partial(output_kernel, team),
        "output_products",
        [IN_SMEM] + [IN_VMEM] * 3,
        shape((requests, out_weight.shape[2])),
    )(places, packed, other, out_weight[0])
    return new_tokens + butterfly(update, "kv", bits_below(kv_count), jnp.add)


def solution(mesh):
    in_specs = (
        P(None, "ctx"),
        P(None, "ctx", None),
        P(),
        P(None, "ctx", "kv"),
        P(None, "ctx", "kv"),
        P(None, "ctx", "kv"),
        P(None, "kv", "ctx"),
        P(),
        P(),
    )
    out_specs = P(None, "ctx")
    return jax.shard_map(shards, mesh=mesh, in_specs=in_specs, out_specs=out_specs, check_vma=False)
```

```python
import functools
import math

import jax
import jax.numpy as jnp
from jax import lax
from jax.experimental import pallas as pl
from jax.experimental.pallas import tpu as pltpu
from jax.sharding import PartitionSpec as P

ROPE_BASE = 500000.0
EPSILON = 1e-05
FLOOR = -1e30
LANES = 128
NORM_ROWS = 64
GROUP_ROWS = 16
VMEM_BYTES = 16 * 1024 * 1024
CHEAP = pl.CostEstimate(flops=1000, bytes_accessed=1000, transcendentals=0)
IN_VMEM = pl.BlockSpec(memory_space=pltpu.VMEM)
IN_SMEM = pl.BlockSpec(memory_space=pltpu.SMEM)
IN_HBM = pl.BlockSpec(memory_space=pltpu.HBM)


def call(kernel, name, in_specs, out_shape, scratch_shapes=()):
    return pl.pallas_call(
        kernel,
        in_specs=in_specs,
        out_specs=jax.tree.map(lambda _: IN_VMEM, out_shape),
        out_shape=out_shape,
        scratch_shapes=scratch_shapes,
        compiler_params=pltpu.CompilerParams(vmem_limit_bytes=VMEM_BYTES),
        cost_estimate=CHEAP,
        name=name,
    )


def shape(dims, dtype=jnp.float32):
    return jax.ShapeDtypeStruct(dims, dtype)


def swap(value, axis, distance):
    count = lax.axis_size(axis)
    return lax.ppermute(value, axis, [(i, i ^ distance) for i in range(count)])


def after(value, *others):
    return lax.optimization_barrier((value, *others))[0]


def bits_below(count):
    return [1 << b for b in range(count.bit_length() - 1)]


def butterfly(value, axis, bits, join):
    for bit in bits:
        value = join(value, swap(value, axis, bit))
    return value


def by_core(value, bit_0, bit_1):
    count = lax.axis_size("ctx")
    bits = (bit_0, bit_1)
    pairs = [(i, i ^ bits[i % 2]) for i in range(count) if bits[i % 2]]
    return lax.ppermute(value, "ctx", pairs)


def send_first(own, partner):
    count = lax.axis_size("ctx")
    if count != 8:
        return [((d, d), swap(own, "ctx", d)) for d in range(2, count // 2)]
    return [((2, 4), by_core(own, 2, 4)), ((3, 5), by_core(partner, 2, 4))]


def share(blocks, *before):
    count = lax.axis_size("ctx")
    if count != 8:
        return []
    return [
        ((odd ^ 1, even ^ 1), swap(after(block, *before) if before else block, "ctx", 1))
        for (even, odd), block in blocks
    ]


def send_last(own, received):
    count = lax.axis_size("ctx")
    if count != 8:
        return [((d, d), swap(own, "ctx", d)) for d in range(count // 2, count)]
    return [((7, 7), by_core(received[0][1], 2, 4))]


def tables(placed, head_size):
    half_size = head_size // 2
    frequency = jnp.exp(
        jnp.arange(half_size, dtype=jnp.float32) * (-2.0 * math.log(ROPE_BASE) / head_size)
    )
    angles = placed[..., None] * frequency
    return jnp.cos(angles), jnp.sin(angles)


def turn(values, cosine, sine_part):
    half_size = values.shape[-1] // 2
    leading = values[:, :half_size]
    trailing = values[:, half_size:]
    return jnp.concatenate(
        (leading * cosine - trailing * sine_part, trailing * cosine + leading * sine_part), axis=-1
    )


def squares_kernel(team, row_count, place_ref, tokens_ref, out_ref, core_ref, request_ref, row_ref):
    values = tokens_ref[...]
    total = jnp.sum(values * values, axis=-1, keepdims=True)
    out_ref[...] = jnp.broadcast_to(total, out_ref.shape)
    place = place_ref[0]
    core_ref[...] = jnp.full(core_ref.shape, lax.rem(place, 2))
    request_ref[...] = jnp.full(request_ref.shape, lax.div(place, team))
    row_ref[...] = jnp.full(row_ref.shape, lax.rem(place, team) * row_count)


def norm_kernel(first, x_ref, gain_ref, *refs):
    out_refs, (held_ref, sems) = refs[:-2], refs[-2:]
    blocks, rows, width = out_refs[0].shape
    features = blocks * width
    groups = len(out_refs) * rows // GROUP_ROWS
    tiles = width // LANES

    def copy(g):
        return pltpu.make_async_copy(
            x_ref.at[pl.ds(first + g * GROUP_ROWS, GROUP_ROWS), :], held_ref.at[g], sems.at[g]
        )

    def factor_of(g):
        totals = [jnp.zeros((GROUP_ROWS, LANES), jnp.float32) for _ in range(4)]
        for j in range(blocks * tiles):
            values = held_ref[g, :, j * LANES : (j + 1) * LANES].astype(jnp.float32)
            totals[j % 4] = totals[j % 4] + values * values
        total = (totals[0] + totals[1]) + (totals[2] + totals[3])
        mean = jnp.sum(total, axis=-1, keepdims=True) / features
        return jnp.broadcast_to(lax.rsqrt(mean + EPSILON), (GROUP_ROWS, LANES))

    def scale(g, factor, out_ref, row):
        part = pl.ds(pl.multiple_of(row, GROUP_ROWS), GROUP_ROWS)
        for b in range(blocks):
            for j in range(tiles):
                lanes = slice(j * LANES, (j + 1) * LANES)
                from_lane = b * width + j * LANES
                values = held_ref[g, :, from_lane : from_lane + LANES].astype(jnp.float32)
                out_ref[b, part, lanes] = (values * factor * gain_ref[b, :, lanes]).astype(
                    jnp.bfloat16
                )

    for g in range(groups):
        copy(g).start()
    copy(0).wait()

    factor = factor_of(0)
    for i, out_ref in enumerate(out_refs):
        start = i * rows // GROUP_ROWS
        stop = min(start + rows // GROUP_ROWS, groups - 1)

        def step(g, factor, out_ref=out_ref, start=start):
            copy(g + 1).wait()
            following = factor_of(g + 1)
            scale(g, factor, out_ref, (g - start) * GROUP_ROWS)
            return following

        factor = lax.fori_loop(start, stop, step, factor)
    scale(groups - 1, factor, out_refs[-1], rows - GROUP_ROWS)


def normalise(hidden, gains, first, parts):
    blocks, _, width = gains.shape
    groups = parts * NORM_ROWS // GROUP_ROWS
    return call(
        functools.partial(norm_kernel, first),
        "normalise",
        [IN_HBM, IN_VMEM],
        (shape((blocks, NORM_ROWS, width), jnp.bfloat16),) * parts,
        [
            pltpu.VMEM((groups, GROUP_ROWS, blocks * width), jnp.bfloat16),
            pltpu.SemaphoreType.DMA((groups,)),
        ],
    )(pltpu.with_memory_space_constraint(hidden, pltpu.HBM), gains)


def query_kernel(
    features, place_ref, squares_ref, tokens_ref, gains_ref, query_ref, key_ref, value_ref, out_ref
):
    requests = tokens_ref.shape[0]
    factor = lax.rsqrt(squares_ref[:, :1] / features + EPSILON)
    normed = (tokens_ref[...] * factor * gains_ref[place_ref[0]]).astype(jnp.bfloat16)
    row = 0
    for weight_ref in (query_ref, key_ref, value_ref):
        part = jnp.dot(normed, weight_ref[...], preferred_element_type=jnp.float32)
        for h in range(weight_ref.shape[1] // LANES):
            for r in range(requests):
                out_ref[r, row : row + 1, :] = part[r : r + 1, h * LANES : (h + 1) * LANES]
            row += 1


def blocks_dot(distances, place, row_refs, block_refs, total):
    for (even, odd), block_ref in zip(distances, block_refs):
        distance = jnp.where(lax.rem(place, 2) == 0, even, odd)
        rows = jnp.concatenate([ref[place ^ distance] for ref in row_refs], axis=0)
        part = jnp.dot(rows, block_ref[...], preferred_element_type=jnp.float32)
        total = part if total is None else total + part
    return total


def project_kernel(distances, row_count, has_total, place_ref, *refs):
    rows, refs = refs[:row_count], refs[row_count:]
    total = refs[len(distances)][...] if has_total else None
    refs[-1][...] = blocks_dot(distances, place_ref[0], rows, refs, total)


def project(place, rows, blocks, total=None):
    extra = [] if total is None else [total]
    row_count = sum(r.shape[1] for r in rows)
    return call(
        functools.partial(project_kernel, [d for d, _ in blocks], len(rows), total is not None),
        "project",
        [IN_SMEM] + [IN_VMEM] * (len(rows) + len(blocks) + len(extra)),
        shape((row_count, LANES)),
    )(place, *rows, *[block for _, block in blocks], *extra)


def live_rows(dims, team, place, lengths_ref):
    rows = dims[1]
    within = lax.rem(place, team) * rows + lax.broadcasted_iota(jnp.int32, dims, 1)
    return within < lengths_ref[lax.div(place, team)]


def score_kernel(team, place_ref, lengths_ref, *refs):
    keys_ref, cos_ref, sin_ref, new_cos_ref, new_sin_ref, summed_ref = refs[:6]
    masked_ref, top_ref, self_ref = refs[6:]
    place = place_ref[0]
    request = lax.div(place, team)
    heads = masked_ref.shape[0]
    scale = 1.0 / math.sqrt(LANES)
    turned = turn(
        summed_ref[...], new_cos_ref[pl.ds(request, 1), :], new_sin_ref[pl.ds(request, 1), :]
    ).astype(jnp.bfloat16)
    queries = turned[:heads]
    self_key = turned[heads : heads + 1].astype(jnp.float32)
    self_scores = (
        jnp.sum(queries.astype(jnp.float32) * self_key, axis=-1, keepdims=True) * scale
    )
    keys = turn(keys_ref[...], cos_ref[...], sin_ref[...]).astype(jnp.bfloat16)
    scores = (
        lax.dot_general(
            queries, keys, (((1,), (1,)), ((), ())), preferred_element_type=jnp.float32
        )
        * scale
    )
    masked = jnp.where(live_rows(scores.shape, team, place, lengths_ref), scores, FLOOR)
    masked_ref[...] = masked
    top = jnp.maximum(jnp.max(masked, axis=-1, keepdims=True), self_scores)
    top_ref[...] = jnp.broadcast_to(top, top_ref.shape)
    self_ref[...] = jnp.broadcast_to(self_scores, self_ref.shape)


def weigh_kernel(distances, row_count, team, place_ref, lengths_ref, *refs):
    rows, refs = refs[:row_count], refs[row_count:]
    blocks, refs = refs[: len(distances)], refs[len(distances) :]
    total_ref, masked_ref, top_ref, self_ref, summed_ref, out_ref = refs
    place = place_ref[0]
    heads = masked_ref.shape[0]
    masked = masked_ref[...]
    top = top_ref[:, :1]
    live = live_rows(masked.shape, team, place, lengths_ref)
    weights = jnp.where(live, jnp.exp(masked - top), 0.0).astype(jnp.bfloat16)
    self_weight = jnp.exp(self_ref[...] - top_ref[...]).astype(jnp.bfloat16).astype(jnp.float32)
    self_weight = jnp.where(lax.rem(place, team) == 0, self_weight, 0.0)
    self_value = summed_ref[heads + 1 : heads + 2, :].astype(jnp.bfloat16).astype(jnp.float32)
    mass = jnp.sum(weights.astype(jnp.float32), axis=-1, keepdims=True) + self_weight
    values = blocks_dot(distances, place, rows, blocks, total_ref[...]).astype(jnp.bfloat16)
    accum = jnp.dot(weights, values, preferred_element_type=jnp.float32)
    out_ref[:, :LANES] = accum + self_weight * self_value
    out_ref[:, LANES:] = mass


def output_kernel(team, place_ref, mine_ref, other_ref, weight_ref, out_ref):
    request = lax.div(place_ref[0], team)
    heads = mine_ref.shape[0]
    attended = []
    for ref in (mine_ref, other_ref):
        attended.append(ref[:, :LANES] / ref[:, LANES:])
    first = jnp.where(request == 0, attended[0], attended[1]).astype(jnp.bfloat16)
    second = jnp.where(request == 0, attended[1], attended[0]).astype(jnp.bfloat16)
    both = jnp.concatenate(
        [
            jnp.concatenate((first[h : h + 1], second[h : h + 1]), axis=0)
            for h in range(heads)
        ],
        axis=1,
    )
    out_ref[...] = jnp.dot(both, weight_ref[...], preferred_element_type=jnp.float32)


def shards(
    new_tokens,
    ctx_hidden,
    norm_gain,
    query_weight,
    key_weight,
    value_weight,
    out_weight,
    lengths,
    positions,
):
    ctx_count = lax.axis_size("ctx")
    kv_count = lax.axis_size("kv")
    place = lax.axis_index("ctx").astype(jnp.int32)
    places = place.reshape(1)
    row_count, features = ctx_hidden.shape[1:]
    head_size = key_weight.shape[2]
    heads = query_weight.shape[2] // head_size
    requests, width = new_tokens.shape
    slot_count = row_count * ctx_count // requests
    team = slot_count // row_count
    assert requests == 2 and slot_count % row_count == 0 and row_count % NORM_ROWS == 0
    assert head_size == LANES
    gains = norm_gain.reshape(ctx_count, 1, width)

    split = ctx_count == 8
    chip_bits = bits_below(ctx_count)[1:]
    rows = []
    squares, core, own_request, first_row = call(
        functools.partial(squares_kernel, team, row_count),
        "squares",
        [IN_SMEM, IN_VMEM],
        (shape((requests, LANES)),) + (shape((1, LANES), jnp.int32),) * 3,
    )(places, new_tokens)

    def beside(received, sent, parts):
        first = len(rows) * NORM_ROWS
        rows.extend(normalise(after(ctx_hidden[0], sent), gains, first, parts))
        return after(received, rows[-1])

    def sum_chips(value, norm_parts=0):
        received = by_core(value, 4, 2)
        if norm_parts:
            received = beside(received, value, norm_parts)
        told = swap(received, "ctx", 1)
        opposite = by_core(told, 4, 2)
        if norm_parts:
            opposite = beside(opposite, told, row_count // NORM_ROWS - norm_parts)
        over_x = jnp.where(core == 0, told, received)
        over_y = jnp.where(core == 0, received, told)
        return (value + over_x) + (over_y + opposite), told, received

    key_partner = swap(key_weight[0], "ctx", 1)
    value_partner = swap(value_weight[0], "ctx", 1)
    key_near = [((0, 0), key_weight[0]), ((1, 1), key_partner)]
    value_near = [((0, 0), value_weight[0]), ((1, 1), value_partner)]
    key_far = send_first(key_weight[0], key_partner)

    squares = squares + swap(squares, "ctx", 1)
    squares = after(squares, key_partner, value_partner)
    if split:
        squares, told, _ = sum_chips(squares, row_count // NORM_ROWS // 2)
        key_shared = share(key_far, told)
        own_values = after(value_weight[0], key_far[0][1])
        squares = after(squares, key_far[1][1], key_shared[0][1])
    else:
        key_shared = share(key_far)
        own_values = value_weight[0]
        squares = beside(squares, squares, row_count // NORM_ROWS)
        squares = butterfly(squares, "ctx", chip_bits, jnp.add)
    key_last = send_last(key_weight[0], key_shared)

    parts = call(
        functools.partial(query_kernel, features),
        "query_products",
        [IN_SMEM] + [IN_VMEM] * 6,
        shape((requests, heads + 2, head_size)),
    )(places, squares, new_tokens, gains, query_weight[0], key_weight[0], value_weight[0])
    parts = parts + swap(parts, "ctx", 1)
    parts_sent = parts
    value_far = send_first(own_values, after(value_partner, parts))
    if split:
        parts, _, parts_sent = sum_chips(parts)
        summed = jnp.where(own_request == 0, parts[0], parts[1])
    else:
        own_part = jnp.where(own_request == 0, parts[0], parts[1])
        other_part = jnp.where(own_request == 0, parts[1], parts[0])
        summed = own_part + swap(other_part, "ctx", team)
        summed = butterfly(summed, "ctx", chip_bits[:-1], jnp.add)

    key_total = project(places, rows, key_near)
    key_total = project(places, rows, key_far + key_shared, key_total)
    key_mid = key_total
    key_total = project(places, rows, key_last + share(key_last), key_total)

    within = first_row[0, :1] + jnp.arange(row_count, dtype=jnp.int32)
    cosine, sine_part = tables(within.astype(jnp.float32), head_size)
    new_cosine, new_sine = tables(positions.astype(jnp.float32), head_size)
    masked, top, self_scores = call(
        functools.partial(score_kernel, team),
        "scores",
        [IN_SMEM] * 2 + [IN_VMEM] * 6,
        (shape((heads, row_count)), shape((heads, LANES)), shape((heads, LANES))),
    )(places, lengths, key_total, cosine, sine_part, new_cosine, new_sine, summed)
    value_first = share(value_far[:1], parts_sent)
    value_last = send_last(own_values, value_first)
    value_first += value_far[:1]
    value_total = project(after(places, masked), rows, value_near + value_first)
    top = butterfly(after(top, value_total), "ctx", [1], jnp.maximum)
    top = after(top, *[block for _, block in value_far[1:]])
    near_top = top
    if split:
        received = jnp.maximum(top, after(by_core(top, 4, 2), value_last[0][1]))
        top = jnp.where(core == 0, swap(received, "ctx", 1), received)
    else:
        top = butterfly(top, "ctx", bits_below(team)[1:], jnp.maximum)
        received = top

    value_second = value_far[1:] + share(value_far[1:], near_top)
    value_total = project(places, rows, value_second, value_total)

    blocks = share(value_last, received)
    value_total = project(places, rows, value_last, value_total)
    packed = call(
        functools.partial(weigh_kernel, [d for d, _ in blocks], len(rows), team),
        "weighted_values",
        [IN_SMEM] * 2 + [IN_VMEM] * (len(rows) + len(blocks) + 5),
        shape((heads, 2 * head_size)),
    )(
        places,
        lengths,
        *rows,
        *[block for _, block in blocks],
        value_total,
        masked,
        top,
        self_scores,
        summed,
    )
    packed = butterfly(packed, "ctx", bits_below(team), jnp.add)
    other = swap(packed, "ctx", team)
    update = call(
        functools.partial(output_kernel, team),
        "output_products",
        [IN_SMEM] + [IN_VMEM] * 3,
        shape((requests, out_weight.shape[2])),
    )(places, packed, other, out_weight[0])
    return new_tokens + butterfly(update, "kv", bits_below(kv_count), jnp.add)


def solution(mesh):
    in_specs = (
        P(None, "ctx"),
        P(None, "ctx", None),
        P(),
        P(None, "ctx", "kv"),
        P(None, "ctx", "kv"),
        P(None, "ctx", "kv"),
        P(None, "kv", "ctx"),
        P(),
        P(),
    )
    out_specs = P(None, "ctx")
    return jax.shard_map(shards, mesh=mesh, in_specs=in_specs, out_specs=out_specs, check_vma=False)
```

```python
import functools
import math

import jax
import jax.numpy as jnp
from jax import lax
from jax.experimental import pallas as pl
from jax.experimental.pallas import tpu as pltpu
from jax.sharding import PartitionSpec as P

ROPE_BASE = 500000.0
EPSILON = 1e-05
FLOOR = -1e30
LANES = 128
NORM_ROWS = 64
GROUP_ROWS = 16
VMEM_BYTES = 16 * 1024 * 1024
CHEAP = pl.CostEstimate(flops=1000, bytes_accessed=1000, transcendentals=0)
IN_VMEM = pl.BlockSpec(memory_space=pltpu.VMEM)
IN_SMEM = pl.BlockSpec(memory_space=pltpu.SMEM)
IN_HBM = pl.BlockSpec(memory_space=pltpu.HBM)


def call(kernel, name, in_specs, out_shape, scratch_shapes=()):
    return pl.pallas_call(
        kernel,
        in_specs=in_specs,
        out_specs=jax.tree.map(lambda _: IN_VMEM, out_shape),
        out_shape=out_shape,
        scratch_shapes=scratch_shapes,
        compiler_params=pltpu.CompilerParams(vmem_limit_bytes=VMEM_BYTES),
        cost_estimate=CHEAP,
        name=name,
    )


def shape(dims, dtype=jnp.float32):
    return jax.ShapeDtypeStruct(dims, dtype)


def swap(value, axis, distance):
    count = lax.axis_size(axis)
    return lax.ppermute(value, axis, [(i, i ^ distance) for i in range(count)])


def after(value, *others):
    return lax.optimization_barrier((value, *others))[0]


def bits_below(count):
    return [1 << b for b in range(count.bit_length() - 1)]


def butterfly(value, axis, bits, join):
    for bit in bits:
        value = join(value, swap(value, axis, bit))
    return value


def by_core(value, bit_0, bit_1):
    count = lax.axis_size("ctx")
    bits = (bit_0, bit_1)
    pairs = [(i, i ^ bits[i % 2]) for i in range(count) if bits[i % 2]]
    return lax.ppermute(value, "ctx", pairs)


def send_first(own, partner):
    count = lax.axis_size("ctx")
    if count != 8:
        return [((d, d), swap(own, "ctx", d)) for d in range(2, count // 2)]
    return [((2, 4), by_core(own, 2, 4)), ((3, 5), by_core(partner, 2, 4))]


def share(blocks, *before):
    count = lax.axis_size("ctx")
    if count != 8:
        return []
    return [
        ((odd ^ 1, even ^ 1), swap(after(block, *before) if before else block, "ctx", 1))
        for (even, odd), block in blocks
    ]


def send_last(own, received):
    count = lax.axis_size("ctx")
    if count != 8:
        return [((d, d), swap(own, "ctx", d)) for d in range(count // 2, count)]
    return [((7, 7), by_core(received[0][1], 2, 4))]


def tables(placed, head_size):
    half_size = head_size // 2
    frequency = jnp.exp(
        jnp.arange(half_size, dtype=jnp.float32) * (-2.0 * math.log(ROPE_BASE) / head_size)
    )
    angles = placed[..., None] * frequency
    return jnp.cos(angles), jnp.sin(angles)


def turn(values, cosine, sine_part):
    half_size = values.shape[-1] // 2
    leading = values[:, :half_size]
    trailing = values[:, half_size:]
    return jnp.concatenate(
        (leading * cosine - trailing * sine_part, trailing * cosine + leading * sine_part), axis=-1
    )


def squares_kernel(team, row_count, place_ref, tokens_ref, out_ref, core_ref, request_ref, row_ref):
    values = tokens_ref[...]
    total = jnp.sum(values * values, axis=-1, keepdims=True)
    out_ref[...] = jnp.broadcast_to(total, out_ref.shape)
    place = place_ref[0]
    core_ref[...] = jnp.full(core_ref.shape, lax.rem(place, 2))
    request_ref[...] = jnp.full(request_ref.shape, lax.div(place, team))
    row_ref[...] = jnp.full(row_ref.shape, lax.rem(place, team) * row_count)


def norm_kernel(first, x_ref, gain_ref, *refs):
    out_refs, (held_ref, sems) = refs[:-2], refs[-2:]
    blocks, rows, width = out_refs[0].shape
    features = blocks * width
    groups = len(out_refs) * rows // GROUP_ROWS
    tiles = width // LANES

    def copy(g):
        return pltpu.make_async_copy(
            x_ref.at[pl.ds(first + g * GROUP_ROWS, GROUP_ROWS), :], held_ref.at[g], sems.at[g]
        )

    def factor_of(g):
        totals = [jnp.zeros((GROUP_ROWS, LANES), jnp.float32) for _ in range(4)]
        for j in range(blocks * tiles):
            values = held_ref[g, :, j * LANES : (j + 1) * LANES].astype(jnp.float32)
            totals[j % 4] = totals[j % 4] + values * values
        total = (totals[0] + totals[1]) + (totals[2] + totals[3])
        mean = jnp.sum(total, axis=-1, keepdims=True) / features
        return jnp.broadcast_to(lax.rsqrt(mean + EPSILON), (GROUP_ROWS, LANES))

    def scale(g, factor, out_ref, row):
        part = pl.ds(pl.multiple_of(row, GROUP_ROWS), GROUP_ROWS)
        for b in range(blocks):
            for j in range(tiles):
                lanes = slice(j * LANES, (j + 1) * LANES)
                from_lane = b * width + j * LANES
                values = held_ref[g, :, from_lane : from_lane + LANES].astype(jnp.float32)
                out_ref[b, part, lanes] = (values * factor * gain_ref[b, :, lanes]).astype(
                    jnp.bfloat16
                )

    for g in range(groups):
        copy(g).start()
    copy(0).wait()

    factor = factor_of(0)
    for i, out_ref in enumerate(out_refs):
        start = i * rows // GROUP_ROWS
        stop = min(start + rows // GROUP_ROWS, groups - 1)

        def step(g, factor, out_ref=out_ref, start=start):
            copy(g + 1).wait()
            following = factor_of(g + 1)
            scale(g, factor, out_ref, (g - start) * GROUP_ROWS)
            return following

        factor = lax.fori_loop(start, stop, step, factor)
    scale(groups - 1, factor, out_refs[-1], rows - GROUP_ROWS)


def normalise(hidden, gains, first, parts):
    blocks, _, width = gains.shape
    groups = parts * NORM_ROWS // GROUP_ROWS
    return call(
        functools.partial(norm_kernel, first),
        "normalise",
        [IN_HBM, IN_VMEM],
        (shape((blocks, NORM_ROWS, width), jnp.bfloat16),) * parts,
        [
            pltpu.VMEM((groups, GROUP_ROWS, blocks * width), jnp.bfloat16),
            pltpu.SemaphoreType.DMA((groups,)),
        ],
    )(pltpu.with_memory_space_constraint(hidden, pltpu.HBM), gains)


def query_kernel(
    features, place_ref, squares_ref, tokens_ref, gains_ref, query_ref, key_ref, value_ref, out_ref
):
    requests = tokens_ref.shape[0]
    factor = lax.rsqrt(squares_ref[:, :1] / features + EPSILON)
    normed = (tokens_ref[...] * factor * gains_ref[place_ref[0]]).astype(jnp.bfloat16)
    row = 0
    for weight_ref in (query_ref, key_ref, value_ref):
        part = jnp.dot(normed, weight_ref[...], preferred_element_type=jnp.float32)
        for h in range(weight_ref.shape[1] // LANES):
            for r in range(requests):
                out_ref[r, row : row + 1, :] = part[r : r + 1, h * LANES : (h + 1) * LANES]
            row += 1


def blocks_dot(distances, place, row_refs, block_refs, total):
    for (even, odd), block_ref in zip(distances, block_refs):
        distance = jnp.where(lax.rem(place, 2) == 0, even, odd)
        rows = jnp.concatenate([ref[place ^ distance] for ref in row_refs], axis=0)
        part = jnp.dot(rows, block_ref[...], preferred_element_type=jnp.float32)
        total = part if total is None else total + part
    return total


def project_kernel(distances, row_count, has_total, place_ref, *refs):
    rows, refs = refs[:row_count], refs[row_count:]
    total = refs[len(distances)][...] if has_total else None
    refs[-1][...] = blocks_dot(distances, place_ref[0], rows, refs, total)


def project(place, rows, blocks, total=None):
    extra = [] if total is None else [total]
    row_count = sum(r.shape[1] for r in rows)
    return call(
        functools.partial(project_kernel, [d for d, _ in blocks], len(rows), total is not None),
        "project",
        [IN_SMEM] + [IN_VMEM] * (len(rows) + len(blocks) + len(extra)),
        shape((row_count, LANES)),
    )(place, *rows, *[block for _, block in blocks], *extra)


def live_rows(dims, team, place, lengths_ref):
    rows = dims[1]
    within = lax.rem(place, team) * rows + lax.broadcasted_iota(jnp.int32, dims, 1)
    return within < lengths_ref[lax.div(place, team)]


def score_kernel(team, place_ref, lengths_ref, *refs):
    keys_ref, cos_ref, sin_ref, new_cos_ref, new_sin_ref, summed_ref = refs[:6]
    masked_ref, top_ref, self_ref = refs[6:]
    place = place_ref[0]
    request = lax.div(place, team)
    heads = masked_ref.shape[0]
    scale = 1.0 / math.sqrt(LANES)
    turned = turn(
        summed_ref[...], new_cos_ref[pl.ds(request, 1), :], new_sin_ref[pl.ds(request, 1), :]
    ).astype(jnp.bfloat16)
    queries = turned[:heads]
    self_key = turned[heads : heads + 1].astype(jnp.float32)
    self_scores = (
        jnp.sum(queries.astype(jnp.float32) * self_key, axis=-1, keepdims=True) * scale
    )
    keys = turn(keys_ref[...], cos_ref[...], sin_ref[...]).astype(jnp.bfloat16)
    scores = (
        lax.dot_general(
            queries, keys, (((1,), (1,)), ((), ())), preferred_element_type=jnp.float32
        )
        * scale
    )
    masked = jnp.where(live_rows(scores.shape, team, place, lengths_ref), scores, FLOOR)
    masked_ref[...] = masked
    top = jnp.maximum(jnp.max(masked, axis=-1, keepdims=True), self_scores)
    top_ref[...] = jnp.broadcast_to(top, top_ref.shape)
    self_ref[...] = jnp.broadcast_to(self_scores, self_ref.shape)


def weigh_kernel(distances, row_count, team, place_ref, lengths_ref, *refs):
    rows, refs = refs[:row_count], refs[row_count:]
    blocks, refs = refs[: len(distances)], refs[len(distances) :]
    total_ref, masked_ref, top_ref, self_ref, summed_ref, out_ref = refs
    place = place_ref[0]
    heads = masked_ref.shape[0]
    masked = masked_ref[...]
    top = top_ref[:, :1]
    live = live_rows(masked.shape, team, place, lengths_ref)
    weights = jnp.where(live, jnp.exp(masked - top), 0.0).astype(jnp.bfloat16)
    self_weight = jnp.exp(self_ref[...] - top_ref[...]).astype(jnp.bfloat16).astype(jnp.float32)
    self_weight = jnp.where(lax.rem(place, team) == 0, self_weight, 0.0)
    self_value = summed_ref[heads + 1 : heads + 2, :].astype(jnp.bfloat16).astype(jnp.float32)
    mass = jnp.sum(weights.astype(jnp.float32), axis=-1, keepdims=True) + self_weight
    values = blocks_dot(distances, place, rows, blocks, total_ref[...]).astype(jnp.bfloat16)
    accum = jnp.dot(weights, values, preferred_element_type=jnp.float32)
    out_ref[:, :LANES] = accum + self_weight * self_value
    out_ref[:, LANES:] = mass


def output_kernel(team, place_ref, mine_ref, other_ref, weight_ref, out_ref):
    request = lax.div(place_ref[0], team)
    heads = mine_ref.shape[0]
    attended = []
    for ref in (mine_ref, other_ref):
        attended.append(ref[:, :LANES] / ref[:, LANES:])
    first = jnp.where(request == 0, attended[0], attended[1]).astype(jnp.bfloat16)
    second = jnp.where(request == 0, attended[1], attended[0]).astype(jnp.bfloat16)
    both = jnp.concatenate(
        [
            jnp.concatenate((first[h : h + 1], second[h : h + 1]), axis=0)
            for h in range(heads)
        ],
        axis=1,
    )
    out_ref[...] = jnp.dot(both, weight_ref[...], preferred_element_type=jnp.float32)


def shards(
    new_tokens,
    ctx_hidden,
    norm_gain,
    query_weight,
    key_weight,
    value_weight,
    out_weight,
    lengths,
    positions,
):
    ctx_count = lax.axis_size("ctx")
    kv_count = lax.axis_size("kv")
    place = lax.axis_index("ctx").astype(jnp.int32)
    places = place.reshape(1)
    row_count, features = ctx_hidden.shape[1:]
    head_size = key_weight.shape[2]
    heads = query_weight.shape[2] // head_size
    requests, width = new_tokens.shape
    slot_count = row_count * ctx_count // requests
    team = slot_count // row_count
    assert requests == 2 and slot_count % row_count == 0 and row_count % NORM_ROWS == 0
    assert head_size == LANES
    gains = norm_gain.reshape(ctx_count, 1, width)

    split = ctx_count == 8
    chip_bits = bits_below(ctx_count)[1:]
    rows = []
    squares, core, own_request, first_row = call(
        functools.partial(squares_kernel, team, row_count),
        "squares",
        [IN_SMEM, IN_VMEM],
        (shape((requests, LANES)),) + (shape((1, LANES), jnp.int32),) * 3,
    )(places, new_tokens)

    def beside(received, sent, parts):
        first = len(rows) * NORM_ROWS
        rows.extend(normalise(after(ctx_hidden[0], sent), gains, first, parts))
        return after(received, rows[-1])

    def sum_chips(value, norm_parts=0):
        received = by_core(value, 4, 2)
        if norm_parts:
            received = beside(received, value, norm_parts)
        told = swap(received, "ctx", 1)
        opposite = by_core(told, 4, 2)
        if norm_parts:
            opposite = beside(opposite, told, row_count // NORM_ROWS - norm_parts)
        over_x = jnp.where(core == 0, told, received)
        over_y = jnp.where(core == 0, received, told)
        return (value + over_x) + (over_y + opposite), told, received

    key_partner = swap(key_weight[0], "ctx", 1)
    value_partner = swap(value_weight[0], "ctx", 1)
    key_near = [((0, 0), key_weight[0]), ((1, 1), key_partner)]
    value_near = [((0, 0), value_weight[0]), ((1, 1), value_partner)]
    key_far = send_first(key_weight[0], key_partner)

    squares = squares + swap(squares, "ctx", 1)
    squares = after(squares, key_partner, value_partner)
    if split:
        squares, told, _ = sum_chips(squares, row_count // NORM_ROWS // 2)
        key_shared = share(key_far, told)
        own_values = value_weight[0]
        squares = after(squares, key_far[1][1])
    else:
        key_shared = share(key_far)
        own_values = value_weight[0]
        squares = beside(squares, squares, row_count // NORM_ROWS)
        squares = butterfly(squares, "ctx", chip_bits, jnp.add)
    key_last = send_last(key_weight[0], key_shared)

    parts = call(
        functools.partial(query_kernel, features),
        "query_products",
        [IN_SMEM] + [IN_VMEM] * 6,
        shape((requests, heads + 2, head_size)),
    )(places, squares, new_tokens, gains, query_weight[0], key_weight[0], value_weight[0])
    parts = parts + swap(parts, "ctx", 1)
    parts_sent = parts
    value_far = send_first(own_values, value_partner)
    if split:
        parts, _, parts_sent = sum_chips(parts)
        summed = jnp.where(own_request == 0, parts[0], parts[1])
    else:
        own_part = jnp.where(own_request == 0, parts[0], parts[1])
        other_part = jnp.where(own_request == 0, parts[1], parts[0])
        summed = own_part + swap(other_part, "ctx", team)
        summed = butterfly(summed, "ctx", chip_bits[:-1], jnp.add)

    key_total = project(places, rows, key_near)
    key_total = project(places, rows, key_far + key_shared, key_total)
    key_mid = key_total
    key_total = project(places, rows, key_last + share(key_last, key_total), key_total)

    within = first_row[0, :1] + jnp.arange(row_count, dtype=jnp.int32)
    cosine, sine_part = tables(within.astype(jnp.float32), head_size)
    new_cosine, new_sine = tables(positions.astype(jnp.float32), head_size)
    masked, top, self_scores = call(
        functools.partial(score_kernel, team),
        "scores",
        [IN_SMEM] * 2 + [IN_VMEM] * 6,
        (shape((heads, row_count)), shape((heads, LANES)), shape((heads, LANES))),
    )(places, lengths, key_total, cosine, sine_part, new_cosine, new_sine, summed)
    value_first = share(value_far[:1], parts_sent)
    value_last = send_last(own_values, value_first)
    value_first += value_far[:1]
    value_total = project(after(places, masked), rows, value_near + value_first)
    top = butterfly(after(top, value_total), "ctx", [1], jnp.maximum)
    top = after(top, *[block for _, block in value_far[1:]])
    near_top = top
    if split:
        received = jnp.maximum(top, after(by_core(top, 4, 2), value_last[0][1]))
        top = jnp.where(core == 0, swap(received, "ctx", 1), received)
    else:
        top = butterfly(top, "ctx", bits_below(team)[1:], jnp.maximum)
        received = top

    value_second = value_far[1:] + share(value_far[1:], near_top)
    value_total = project(places, rows, value_second, value_total)

    blocks = share(value_last, received)
    value_total = project(places, rows, value_last, value_total)
    packed = call(
        functools.partial(weigh_kernel, [d for d, _ in blocks], len(rows), team),
        "weighted_values",
        [IN_SMEM] * 2 + [IN_VMEM] * (len(rows) + len(blocks) + 5),
        shape((heads, 2 * head_size)),
    )(
        places,
        lengths,
        *rows,
        *[block for _, block in blocks],
        value_total,
        masked,
        top,
        self_scores,
        summed,
    )
    packed = butterfly(packed, "ctx", bits_below(team), jnp.add)
    other = swap(packed, "ctx", team)
    update = call(
        functools.partial(output_kernel, team),
        "output_products",
        [IN_SMEM] + [IN_VMEM] * 3,
        shape((requests, out_weight.shape[2])),
    )(places, packed, other, out_weight[0])
    return new_tokens + butterfly(update, "kv", bits_below(kv_count), jnp.add)


def solution(mesh):
    in_specs = (
        P(None, "ctx"),
        P(None, "ctx", None),
        P(),
        P(None, "ctx", "kv"),
        P(None, "ctx", "kv"),
        P(None, "ctx", "kv"),
        P(None, "kv", "ctx"),
        P(),
        P(),
    )
    out_specs = P(None, "ctx")
    return jax.shard_map(shards, mesh=mesh, in_specs=in_specs, out_specs=out_specs, check_vma=False)
```

```python
import functools
import math

import jax
import jax.numpy as jnp
from jax import lax
from jax.experimental import pallas as pl
from jax.experimental.pallas import tpu as pltpu
from jax.sharding import PartitionSpec as P

ROPE_BASE = 500000.0
EPSILON = 1e-05
FLOOR = -1e30
LANES = 128
NORM_ROWS = 64
GROUP_ROWS = 16
VMEM_BYTES = 16 * 1024 * 1024
CHEAP = pl.CostEstimate(flops=1000, bytes_accessed=1000, transcendentals=0)
IN_VMEM = pl.BlockSpec(memory_space=pltpu.VMEM)
IN_SMEM = pl.BlockSpec(memory_space=pltpu.SMEM)
IN_HBM = pl.BlockSpec(memory_space=pltpu.HBM)


def call(kernel, name, in_specs, out_shape, scratch_shapes=()):
    return pl.pallas_call(
        kernel,
        in_specs=in_specs,
        out_specs=jax.tree.map(lambda _: IN_VMEM, out_shape),
        out_shape=out_shape,
        scratch_shapes=scratch_shapes,
        compiler_params=pltpu.CompilerParams(vmem_limit_bytes=VMEM_BYTES),
        cost_estimate=CHEAP,
        name=name,
    )


def shape(dims, dtype=jnp.float32):
    return jax.ShapeDtypeStruct(dims, dtype)


def swap(value, axis, distance):
    count = lax.axis_size(axis)
    return lax.ppermute(value, axis, [(i, i ^ distance) for i in range(count)])


def after(value, *others):
    return lax.optimization_barrier((value, *others))[0]


def bits_below(count):
    return [1 << b for b in range(count.bit_length() - 1)]


def butterfly(value, axis, bits, join):
    for bit in bits:
        value = join(value, swap(value, axis, bit))
    return value


def by_core(value, bit_0, bit_1):
    count = lax.axis_size("ctx")
    bits = (bit_0, bit_1)
    pairs = [(i, i ^ bits[i % 2]) for i in range(count) if bits[i % 2]]
    return lax.ppermute(value, "ctx", pairs)


def send_first(own, partner):
    count = lax.axis_size("ctx")
    if count != 8:
        return [((d, d), swap(own, "ctx", d)) for d in range(2, count // 2)]
    return [((2, 4), by_core(own, 2, 4)), ((3, 5), by_core(partner, 2, 4))]


def share(blocks, *before):
    count = lax.axis_size("ctx")
    if count != 8:
        return []
    return [
        ((odd ^ 1, even ^ 1), swap(after(block, *before) if before else block, "ctx", 1))
        for (even, odd), block in blocks
    ]


def send_last(own, received):
    count = lax.axis_size("ctx")
    if count != 8:
        return [((d, d), swap(own, "ctx", d)) for d in range(count // 2, count)]
    return [((7, 7), by_core(received[0][1], 2, 4))]


def tables(placed, head_size):
    half_size = head_size // 2
    frequency = jnp.exp(
        jnp.arange(half_size, dtype=jnp.float32) * (-2.0 * math.log(ROPE_BASE) / head_size)
    )
    angles = placed[..., None] * frequency
    return jnp.cos(angles), jnp.sin(angles)


def turn(values, cosine, sine_part):
    half_size = values.shape[-1] // 2
    leading = values[:, :half_size]
    trailing = values[:, half_size:]
    return jnp.concatenate(
        (leading * cosine - trailing * sine_part, trailing * cosine + leading * sine_part), axis=-1
    )


def squares_kernel(team, row_count, place_ref, tokens_ref, out_ref, core_ref, request_ref, row_ref):
    values = tokens_ref[...]
    total = jnp.sum(values * values, axis=-1, keepdims=True)
    out_ref[...] = jnp.broadcast_to(total, out_ref.shape)
    place = place_ref[0]
    core_ref[...] = jnp.full(core_ref.shape, lax.rem(place, 2))
    request_ref[...] = jnp.full(request_ref.shape, lax.div(place, team))
    row_ref[...] = jnp.full(row_ref.shape, lax.rem(place, team) * row_count)


def norm_kernel(first, x_ref, gain_ref, *refs):
    out_refs, (held_ref, sems) = refs[:-2], refs[-2:]
    blocks, rows, width = out_refs[0].shape
    features = blocks * width
    groups = len(out_refs) * rows // GROUP_ROWS
    tiles = width // LANES

    def copy(g):
        return pltpu.make_async_copy(
            x_ref.at[pl.ds(first + g * GROUP_ROWS, GROUP_ROWS), :], held_ref.at[g], sems.at[g]
        )

    def factor_of(g):
        totals = [jnp.zeros((GROUP_ROWS, LANES), jnp.float32) for _ in range(4)]
        for j in range(blocks * tiles):
            values = held_ref[g, :, j * LANES : (j + 1) * LANES].astype(jnp.float32)
            totals[j % 4] = totals[j % 4] + values * values
        total = (totals[0] + totals[1]) + (totals[2] + totals[3])
        mean = jnp.sum(total, axis=-1, keepdims=True) / features
        return jnp.broadcast_to(lax.rsqrt(mean + EPSILON), (GROUP_ROWS, LANES))

    def scale(g, factor, out_ref, row):
        part = pl.ds(pl.multiple_of(row, GROUP_ROWS), GROUP_ROWS)
        for b in range(blocks):
            for j in range(tiles):
                lanes = slice(j * LANES, (j + 1) * LANES)
                from_lane = b * width + j * LANES
                values = held_ref[g, :, from_lane : from_lane + LANES].astype(jnp.float32)
                out_ref[b, part, lanes] = (values * factor * gain_ref[b, :, lanes]).astype(
                    jnp.bfloat16
                )

    for g in range(groups):
        copy(g).start()
    copy(0).wait()

    factor = factor_of(0)
    for i, out_ref in enumerate(out_refs):
        start = i * rows // GROUP_ROWS
        stop = min(start + rows // GROUP_ROWS, groups - 1)

        def step(g, factor, out_ref=out_ref, start=start):
            copy(g + 1).wait()
            following = factor_of(g + 1)
            scale(g, factor, out_ref, (g - start) * GROUP_ROWS)
            return following

        factor = lax.fori_loop(start, stop, step, factor)
    scale(groups - 1, factor, out_refs[-1], rows - GROUP_ROWS)


def normalise(hidden, gains, first, parts):
    blocks, _, width = gains.shape
    groups = parts * NORM_ROWS // GROUP_ROWS
    return call(
        functools.partial(norm_kernel, first),
        "normalise",
        [IN_HBM, IN_VMEM],
        (shape((blocks, NORM_ROWS, width), jnp.bfloat16),) * parts,
        [
            pltpu.VMEM((groups, GROUP_ROWS, blocks * width), jnp.bfloat16),
            pltpu.SemaphoreType.DMA((groups,)),
        ],
    )(pltpu.with_memory_space_constraint(hidden, pltpu.HBM), gains)


def query_kernel(
    features, place_ref, squares_ref, tokens_ref, gains_ref, query_ref, key_ref, value_ref, out_ref
):
    requests = tokens_ref.shape[0]
    factor = lax.rsqrt(squares_ref[:, :1] / features + EPSILON)
    normed = (tokens_ref[...] * factor * gains_ref[place_ref[0]]).astype(jnp.bfloat16)
    row = 0
    for weight_ref in (query_ref, key_ref, value_ref):
        part = jnp.dot(normed, weight_ref[...], preferred_element_type=jnp.float32)
        for h in range(weight_ref.shape[1] // LANES):
            for r in range(requests):
                out_ref[r, row : row + 1, :] = part[r : r + 1, h * LANES : (h + 1) * LANES]
            row += 1


def blocks_dot(distances, place, row_refs, block_refs, total):
    for (even, odd), block_ref in zip(distances, block_refs):
        distance = jnp.where(lax.rem(place, 2) == 0, even, odd)
        rows = jnp.concatenate([ref[place ^ distance] for ref in row_refs], axis=0)
        part = jnp.dot(rows, block_ref[...], preferred_element_type=jnp.float32)
        total = part if total is None else total + part
    return total


def project_kernel(distances, row_count, has_total, place_ref, *refs):
    rows, refs = refs[:row_count], refs[row_count:]
    total = refs[len(distances)][...] if has_total else None
    refs[-1][...] = blocks_dot(distances, place_ref[0], rows, refs, total)


def project(place, rows, blocks, total=None):
    extra = [] if total is None else [total]
    row_count = sum(r.shape[1] for r in rows)
    return call(
        functools.partial(project_kernel, [d for d, _ in blocks], len(rows), total is not None),
        "project",
        [IN_SMEM] + [IN_VMEM] * (len(rows) + len(blocks) + len(extra)),
        shape((row_count, LANES)),
    )(place, *rows, *[block for _, block in blocks], *extra)


def live_rows(dims, team, place, lengths_ref):
    rows = dims[1]
    within = lax.rem(place, team) * rows + lax.broadcasted_iota(jnp.int32, dims, 1)
    return within < lengths_ref[lax.div(place, team)]


def score_kernel(team, place_ref, lengths_ref, *refs):
    keys_ref, cos_ref, sin_ref, new_cos_ref, new_sin_ref, summed_ref = refs[:6]
    masked_ref, top_ref, self_ref = refs[6:]
    place = place_ref[0]
    request = lax.div(place, team)
    heads = masked_ref.shape[0]
    scale = 1.0 / math.sqrt(LANES)
    turned = turn(
        summed_ref[...], new_cos_ref[pl.ds(request, 1), :], new_sin_ref[pl.ds(request, 1), :]
    ).astype(jnp.bfloat16)
    queries = turned[:heads]
    self_key = turned[heads : heads + 1].astype(jnp.float32)
    self_scores = (
        jnp.sum(queries.astype(jnp.float32) * self_key, axis=-1, keepdims=True) * scale
    )
    keys = turn(keys_ref[...], cos_ref[...], sin_ref[...]).astype(jnp.bfloat16)
    scores = (
        lax.dot_general(
            queries, keys, (((1,), (1,)), ((), ())), preferred_element_type=jnp.float32
        )
        * scale
    )
    masked = jnp.where(live_rows(scores.shape, team, place, lengths_ref), scores, FLOOR)
    masked_ref[...] = masked
    top = jnp.maximum(jnp.max(masked, axis=-1, keepdims=True), self_scores)
    top_ref[...] = jnp.broadcast_to(top, top_ref.shape)
    self_ref[...] = jnp.broadcast_to(self_scores, self_ref.shape)


def weigh_kernel(distances, row_count, team, place_ref, lengths_ref, *refs):
    rows, refs = refs[:row_count], refs[row_count:]
    blocks, refs = refs[: len(distances)], refs[len(distances) :]
    total_ref, masked_ref, top_ref, self_ref, summed_ref, out_ref = refs
    place = place_ref[0]
    heads = masked_ref.shape[0]
    masked = masked_ref[...]
    top = top_ref[:, :1]
    live = live_rows(masked.shape, team, place, lengths_ref)
    weights = jnp.where(live, jnp.exp(masked - top), 0.0).astype(jnp.bfloat16)
    self_weight = jnp.exp(self_ref[...] - top_ref[...]).astype(jnp.bfloat16).astype(jnp.float32)
    self_weight = jnp.where(lax.rem(place, team) == 0, self_weight, 0.0)
    self_value = summed_ref[heads + 1 : heads + 2, :].astype(jnp.bfloat16).astype(jnp.float32)
    mass = jnp.sum(weights.astype(jnp.float32), axis=-1, keepdims=True) + self_weight
    values = blocks_dot(distances, place, rows, blocks, total_ref[...]).astype(jnp.bfloat16)
    accum = jnp.dot(weights, values, preferred_element_type=jnp.float32)
    out_ref[:, :LANES] = accum + self_weight * self_value
    out_ref[:, LANES:] = mass


def output_kernel(team, place_ref, mine_ref, other_ref, weight_ref, out_ref):
    request = lax.div(place_ref[0], team)
    heads = mine_ref.shape[0]
    attended = []
    for ref in (mine_ref, other_ref):
        attended.append(ref[:, :LANES] / ref[:, LANES:])
    first = jnp.where(request == 0, attended[0], attended[1]).astype(jnp.bfloat16)
    second = jnp.where(request == 0, attended[1], attended[0]).astype(jnp.bfloat16)
    both = jnp.concatenate(
        [
            jnp.concatenate((first[h : h + 1], second[h : h + 1]), axis=0)
            for h in range(heads)
        ],
        axis=1,
    )
    out_ref[...] = jnp.dot(both, weight_ref[...], preferred_element_type=jnp.float32)


def shards(
    new_tokens,
    ctx_hidden,
    norm_gain,
    query_weight,
    key_weight,
    value_weight,
    out_weight,
    lengths,
    positions,
):
    ctx_count = lax.axis_size("ctx")
    kv_count = lax.axis_size("kv")
    place = lax.axis_index("ctx").astype(jnp.int32)
    places = place.reshape(1)
    row_count, features = ctx_hidden.shape[1:]
    head_size = key_weight.shape[2]
    heads = query_weight.shape[2] // head_size
    requests, width = new_tokens.shape
    slot_count = row_count * ctx_count // requests
    team = slot_count // row_count
    assert requests == 2 and slot_count % row_count == 0 and row_count % NORM_ROWS == 0
    assert head_size == LANES
    gains = norm_gain.reshape(ctx_count, 1, width)

    split = ctx_count == 8
    chip_bits = bits_below(ctx_count)[1:]
    rows = []
    squares, core, own_request, first_row = call(
        functools.partial(squares_kernel, team, row_count),
        "squares",
        [IN_SMEM, IN_VMEM],
        (shape((requests, LANES)),) + (shape((1, LANES), jnp.int32),) * 3,
    )(places, new_tokens)

    def beside(received, sent, parts):
        first = len(rows) * NORM_ROWS
        rows.extend(normalise(after(ctx_hidden[0], sent), gains, first, parts))
        return after(received, rows[-1])

    def sum_chips(value, norm_parts=0):
        received = by_core(value, 4, 2)
        if norm_parts:
            received = beside(received, value, norm_parts)
        told = swap(received, "ctx", 1)
        opposite = by_core(told, 4, 2)
        if norm_parts:
            opposite = beside(opposite, told, row_count // NORM_ROWS - norm_parts)
        over_x = jnp.where(core == 0, told, received)
        over_y = jnp.where(core == 0, received, told)
        return (value + over_x) + (over_y + opposite), told, received

    key_partner = swap(key_weight[0], "ctx", 1)
    value_partner = swap(value_weight[0], "ctx", 1)
    key_near = [((0, 0), key_weight[0]), ((1, 1), key_partner)]
    value_near = [((0, 0), value_weight[0]), ((1, 1), value_partner)]
    key_far = send_first(key_weight[0], key_partner)

    squares = squares + swap(squares, "ctx", 1)
    squares = after(squares, key_partner, value_partner)
    if split:
        squares, told, _ = sum_chips(squares, row_count // NORM_ROWS // 2)
        key_shared = share(key_far, told)
        own_values = value_weight[0]
        squares = after(squares, key_far[1][1])
    else:
        key_shared = share(key_far)
        own_values = value_weight[0]
        squares = beside(squares, squares, row_count // NORM_ROWS)
        squares = butterfly(squares, "ctx", chip_bits, jnp.add)
    key_last = send_last(key_weight[0], key_shared)

    parts = call(
        functools.partial(query_kernel, features),
        "query_products",
        [IN_SMEM] + [IN_VMEM] * 6,
        shape((requests, heads + 2, head_size)),
    )(places, squares, new_tokens, gains, query_weight[0], key_weight[0], value_weight[0])
    parts = parts + swap(parts, "ctx", 1)
    parts_sent = parts
    value_far = send_first(own_values, value_partner)
    if split:
        parts, _, parts_sent = sum_chips(parts)
        summed = jnp.where(own_request == 0, parts[0], parts[1])
    else:
        own_part = jnp.where(own_request == 0, parts[0], parts[1])
        other_part = jnp.where(own_request == 0, parts[1], parts[0])
        summed = own_part + swap(other_part, "ctx", team)
        summed = butterfly(summed, "ctx", chip_bits[:-1], jnp.add)

    key_total = project(places, rows, key_near)
    key_total = project(places, rows, key_far + key_shared, key_total)
    key_mid = key_total
    key_total = project(places, rows, key_last + share(key_last, key_total), key_total)

    within = first_row[0, :1] + jnp.arange(row_count, dtype=jnp.int32)
    cosine, sine_part = tables(within.astype(jnp.float32), head_size)
    new_cosine, new_sine = tables(positions.astype(jnp.float32), head_size)
    masked, top, self_scores = call(
        functools.partial(score_kernel, team),
        "scores",
        [IN_SMEM] * 2 + [IN_VMEM] * 6,
        (shape((heads, row_count)), shape((heads, LANES)), shape((heads, LANES))),
    )(places, lengths, key_total, cosine, sine_part, new_cosine, new_sine, summed)
    value_first = share(value_far[:1], parts_sent)
    value_last = send_last(own_values, value_first)
    value_first += value_far[:1]
    top = butterfly(top, "ctx", [1], jnp.maximum)
    top = after(top, *[block for _, block in value_far[1:]])
    near_top = top
    value_total = project(after(places, near_top), rows, value_near + value_first)
    if split:
        received = jnp.maximum(top, after(by_core(top, 4, 2), value_last[0][1], value_total))
        top = jnp.where(core == 0, swap(received, "ctx", 1), received)
    else:
        top = butterfly(top, "ctx", bits_below(team)[1:], jnp.maximum)
        received = top

    value_second = value_far[1:] + share(value_far[1:], masked)

    blocks = share(value_last, received)
    value_total = project(places, rows, value_second + value_last, value_total)
    packed = call(
        functools.partial(weigh_kernel, [d for d, _ in blocks], len(rows), team),
        "weighted_values",
        [IN_SMEM] * 2 + [IN_VMEM] * (len(rows) + len(blocks) + 5),
        shape((heads, 2 * head_size)),
    )(
        places,
        lengths,
        *rows,
        *[block for _, block in blocks],
        value_total,
        masked,
        top,
        self_scores,
        summed,
    )
    packed = butterfly(packed, "ctx", bits_below(team), jnp.add)
    other = swap(packed, "ctx", team)
    update = call(
        functools.partial(output_kernel, team),
        "output_products",
        [IN_SMEM] + [IN_VMEM] * 3,
        shape((requests, out_weight.shape[2])),
    )(places, packed, other, out_weight[0])
    return new_tokens + butterfly(update, "kv", bits_below(kv_count), jnp.add)


def solution(mesh):
    in_specs = (
        P(None, "ctx"),
        P(None, "ctx", None),
        P(),
        P(None, "ctx", "kv"),
        P(None, "ctx", "kv"),
        P(None, "ctx", "kv"),
        P(None, "kv", "ctx"),
        P(),
        P(),
    )
    out_specs = P(None, "ctx")
    return jax.shard_map(shards, mesh=mesh, in_specs=in_specs, out_specs=out_specs, check_vma=False)
```

```python
import functools
import math

import jax
import jax.numpy as jnp
from jax import lax
from jax.experimental import pallas as pl
from jax.experimental.pallas import tpu as pltpu
from jax.sharding import PartitionSpec as P

ROPE_BASE = 500000.0
EPSILON = 1e-05
FLOOR = -1e30
LANES = 128
NORM_ROWS = 64
GROUP_ROWS = 16
VMEM_BYTES = 16 * 1024 * 1024
CHEAP = pl.CostEstimate(flops=1000, bytes_accessed=1000, transcendentals=0)
IN_VMEM = pl.BlockSpec(memory_space=pltpu.VMEM)
IN_SMEM = pl.BlockSpec(memory_space=pltpu.SMEM)
IN_HBM = pl.BlockSpec(memory_space=pltpu.HBM)


def call(kernel, name, in_specs, out_shape, scratch_shapes=()):
    return pl.pallas_call(
        kernel,
        in_specs=in_specs,
        out_specs=jax.tree.map(lambda _: IN_VMEM, out_shape),
        out_shape=out_shape,
        scratch_shapes=scratch_shapes,
        compiler_params=pltpu.CompilerParams(vmem_limit_bytes=VMEM_BYTES),
        cost_estimate=CHEAP,
        name=name,
    )


def shape(dims, dtype=jnp.float32):
    return jax.ShapeDtypeStruct(dims, dtype)


def swap(value, axis, distance):
    count = lax.axis_size(axis)
    return lax.ppermute(value, axis, [(i, i ^ distance) for i in range(count)])


def after(value, *others):
    return lax.optimization_barrier((value, *others))[0]


def bits_below(count):
    return [1 << b for b in range(count.bit_length() - 1)]


def butterfly(value, axis, bits, join):
    for bit in bits:
        value = join(value, swap(value, axis, bit))
    return value


def by_core(value, bit_0, bit_1):
    count = lax.axis_size("ctx")
    bits = (bit_0, bit_1)
    pairs = [(i, i ^ bits[i % 2]) for i in range(count) if bits[i % 2]]
    return lax.ppermute(value, "ctx", pairs)


def send_first(own, partner):
    count = lax.axis_size("ctx")
    if count != 8:
        return [((d, d), swap(own, "ctx", d)) for d in range(2, count // 2)]
    return [((2, 4), by_core(own, 2, 4)), ((3, 5), by_core(partner, 2, 4))]


def share(blocks, *before):
    count = lax.axis_size("ctx")
    if count != 8:
        return []
    return [
        ((odd ^ 1, even ^ 1), swap(after(block, *before) if before else block, "ctx", 1))
        for (even, odd), block in blocks
    ]


def send_last(own, received):
    count = lax.axis_size("ctx")
    if count != 8:
        return [((d, d), swap(own, "ctx", d)) for d in range(count // 2, count)]
    return [((7, 7), by_core(received[0][1], 2, 4))]


def tables(placed, head_size):
    half_size = head_size // 2
    frequency = jnp.exp(
        jnp.arange(half_size, dtype=jnp.float32) * (-2.0 * math.log(ROPE_BASE) / head_size)
    )
    angles = placed[..., None] * frequency
    return jnp.cos(angles), jnp.sin(angles)


def turn(values, cosine, sine_part):
    half_size = values.shape[-1] // 2
    leading = values[:, :half_size]
    trailing = values[:, half_size:]
    return jnp.concatenate(
        (leading * cosine - trailing * sine_part, trailing * cosine + leading * sine_part), axis=-1
    )


def squares_kernel(team, row_count, place_ref, tokens_ref, out_ref, core_ref, request_ref, row_ref):
    values = tokens_ref[...]
    total = jnp.sum(values * values, axis=-1, keepdims=True)
    out_ref[...] = jnp.broadcast_to(total, out_ref.shape)
    place = place_ref[0]
    core_ref[...] = jnp.full(core_ref.shape, lax.rem(place, 2))
    request_ref[...] = jnp.full(request_ref.shape, lax.div(place, team))
    row_ref[...] = jnp.full(row_ref.shape, lax.rem(place, team) * row_count)


def norm_kernel(first, x_ref, gain_ref, *refs):
    out_refs, (held_ref, sems) = refs[:-2], refs[-2:]
    blocks, rows, width = out_refs[0].shape
    features = blocks * width
    groups = len(out_refs) * rows // GROUP_ROWS
    tiles = width // LANES

    def copy(g):
        return pltpu.make_async_copy(
            x_ref.at[pl.ds(first + g * GROUP_ROWS, GROUP_ROWS), :], held_ref.at[g], sems.at[g]
        )

    def factor_of(g):
        totals = [jnp.zeros((GROUP_ROWS, LANES), jnp.float32) for _ in range(4)]
        for j in range(blocks * tiles):
            values = held_ref[g, :, j * LANES : (j + 1) * LANES].astype(jnp.float32)
            totals[j % 4] = totals[j % 4] + values * values
        total = (totals[0] + totals[1]) + (totals[2] + totals[3])
        mean = jnp.sum(total, axis=-1, keepdims=True) / features
        return jnp.broadcast_to(lax.rsqrt(mean + EPSILON), (GROUP_ROWS, LANES))

    def scale(g, factor, out_ref, row):
        part = pl.ds(pl.multiple_of(row, GROUP_ROWS), GROUP_ROWS)
        for b in range(blocks):
            for j in range(tiles):
                lanes = slice(j * LANES, (j + 1) * LANES)
                from_lane = b * width + j * LANES
                values = held_ref[g, :, from_lane : from_lane + LANES].astype(jnp.float32)
                out_ref[b, part, lanes] = (values * factor * gain_ref[b, :, lanes]).astype(
                    jnp.bfloat16
                )

    for g in range(groups):
        copy(g).start()
    copy(0).wait()

    factor = factor_of(0)
    for i, out_ref in enumerate(out_refs):
        start = i * rows // GROUP_ROWS
        stop = min(start + rows // GROUP_ROWS, groups - 1)

        def step(g, factor, out_ref=out_ref, start=start):
            copy(g + 1).wait()
            following = factor_of(g + 1)
            scale(g, factor, out_ref, (g - start) * GROUP_ROWS)
            return following

        factor = lax.fori_loop(start, stop, step, factor)
    scale(groups - 1, factor, out_refs[-1], rows - GROUP_ROWS)


def normalise(hidden, gains, first, parts):
    blocks, _, width = gains.shape
    groups = parts * NORM_ROWS // GROUP_ROWS
    return call(
        functools.partial(norm_kernel, first),
        "normalise",
        [IN_HBM, IN_VMEM],
        (shape((blocks, NORM_ROWS, width), jnp.bfloat16),) * parts,
        [
            pltpu.VMEM((groups, GROUP_ROWS, blocks * width), jnp.bfloat16),
            pltpu.SemaphoreType.DMA((groups,)),
        ],
    )(pltpu.with_memory_space_constraint(hidden, pltpu.HBM), gains)


def query_kernel(
    features, place_ref, squares_ref, tokens_ref, gains_ref, query_ref, key_ref, value_ref, out_ref
):
    requests = tokens_ref.shape[0]
    factor = lax.rsqrt(squares_ref[:, :1] / features + EPSILON)
    normed = (tokens_ref[...] * factor * gains_ref[place_ref[0]]).astype(jnp.bfloat16)
    row = 0
    for weight_ref in (query_ref, key_ref, value_ref):
        part = jnp.dot(normed, weight_ref[...], preferred_element_type=jnp.float32)
        for h in range(weight_ref.shape[1] // LANES):
            for r in range(requests):
                out_ref[r, row : row + 1, :] = part[r : r + 1, h * LANES : (h + 1) * LANES]
            row += 1


def blocks_dot(distances, place, row_refs, block_refs, total):
    for (even, odd), block_ref in zip(distances, block_refs):
        distance = jnp.where(lax.rem(place, 2) == 0, even, odd)
        rows = jnp.concatenate([ref[place ^ distance] for ref in row_refs], axis=0)
        part = jnp.dot(rows, block_ref[...], preferred_element_type=jnp.float32)
        total = part if total is None else total + part
    return total


def project_kernel(distances, row_count, has_total, place_ref, *refs):
    rows, refs = refs[:row_count], refs[row_count:]
    total = refs[len(distances)][...] if has_total else None
    refs[-1][...] = blocks_dot(distances, place_ref[0], rows, refs, total)


def project(place, rows, blocks, total=None):
    extra = [] if total is None else [total]
    row_count = sum(r.shape[1] for r in rows)
    return call(
        functools.partial(project_kernel, [d for d, _ in blocks], len(rows), total is not None),
        "project",
        [IN_SMEM] + [IN_VMEM] * (len(rows) + len(blocks) + len(extra)),
        shape((row_count, LANES)),
    )(place, *rows, *[block for _, block in blocks], *extra)


def live_rows(dims, team, place, lengths_ref):
    rows = dims[1]
    within = lax.rem(place, team) * rows + lax.broadcasted_iota(jnp.int32, dims, 1)
    return within < lengths_ref[lax.div(place, team)]


def score_kernel(team, place_ref, lengths_ref, *refs):
    keys_ref, cos_ref, sin_ref, new_cos_ref, new_sin_ref, summed_ref = refs[:6]
    masked_ref, top_ref, self_ref = refs[6:]
    place = place_ref[0]
    request = lax.div(place, team)
    heads = masked_ref.shape[0]
    scale = 1.0 / math.sqrt(LANES)
    turned = turn(
        summed_ref[...], new_cos_ref[pl.ds(request, 1), :], new_sin_ref[pl.ds(request, 1), :]
    ).astype(jnp.bfloat16)
    queries = turned[:heads]
    self_key = turned[heads : heads + 1].astype(jnp.float32)
    self_scores = (
        jnp.sum(queries.astype(jnp.float32) * self_key, axis=-1, keepdims=True) * scale
    )
    keys = turn(keys_ref[...], cos_ref[...], sin_ref[...]).astype(jnp.bfloat16)
    scores = (
        lax.dot_general(
            queries, keys, (((1,), (1,)), ((), ())), preferred_element_type=jnp.float32
        )
        * scale
    )
    masked = jnp.where(live_rows(scores.shape, team, place, lengths_ref), scores, FLOOR)
    masked_ref[...] = masked
    top = jnp.maximum(jnp.max(masked, axis=-1, keepdims=True), self_scores)
    top_ref[...] = jnp.broadcast_to(top, top_ref.shape)
    self_ref[...] = jnp.broadcast_to(self_scores, self_ref.shape)


def weigh_kernel(distances, row_count, team, place_ref, lengths_ref, *refs):
    rows, refs = refs[:row_count], refs[row_count:]
    blocks, refs = refs[: len(distances)], refs[len(distances) :]
    total_ref, masked_ref, top_ref, self_ref, summed_ref, out_ref = refs
    place = place_ref[0]
    heads = masked_ref.shape[0]
    masked = masked_ref[...]
    top = top_ref[:, :1]
    live = live_rows(masked.shape, team, place, lengths_ref)
    weights = jnp.where(live, jnp.exp(masked - top), 0.0).astype(jnp.bfloat16)
    self_weight = jnp.exp(self_ref[...] - top_ref[...]).astype(jnp.bfloat16).astype(jnp.float32)
    self_weight = jnp.where(lax.rem(place, team) == 0, self_weight, 0.0)
    self_value = summed_ref[heads + 1 : heads + 2, :].astype(jnp.bfloat16).astype(jnp.float32)
    mass = jnp.sum(weights.astype(jnp.float32), axis=-1, keepdims=True) + self_weight
    values = blocks_dot(distances, place, rows, blocks, total_ref[...]).astype(jnp.bfloat16)
    accum = jnp.dot(weights, values, preferred_element_type=jnp.float32)
    out_ref[:, :LANES] = accum + self_weight * self_value
    out_ref[:, LANES:] = mass


def output_kernel(team, place_ref, mine_ref, other_ref, weight_ref, out_ref):
    request = lax.div(place_ref[0], team)
    heads = mine_ref.shape[0]
    attended = []
    for ref in (mine_ref, other_ref):
        attended.append(ref[:, :LANES] / ref[:, LANES:])
    first = jnp.where(request == 0, attended[0], attended[1]).astype(jnp.bfloat16)
    second = jnp.where(request == 0, attended[1], attended[0]).astype(jnp.bfloat16)
    both = jnp.concatenate(
        [
            jnp.concatenate((first[h : h + 1], second[h : h + 1]), axis=0)
            for h in range(heads)
        ],
        axis=1,
    )
    out_ref[...] = jnp.dot(both, weight_ref[...], preferred_element_type=jnp.float32)


def shards(
    new_tokens,
    ctx_hidden,
    norm_gain,
    query_weight,
    key_weight,
    value_weight,
    out_weight,
    lengths,
    positions,
):
    ctx_count = lax.axis_size("ctx")
    kv_count = lax.axis_size("kv")
    place = lax.axis_index("ctx").astype(jnp.int32)
    places = place.reshape(1)
    row_count, features = ctx_hidden.shape[1:]
    head_size = key_weight.shape[2]
    heads = query_weight.shape[2] // head_size
    requests, width = new_tokens.shape
    slot_count = row_count * ctx_count // requests
    team = slot_count // row_count
    assert requests == 2 and slot_count % row_count == 0 and row_count % NORM_ROWS == 0
    assert head_size == LANES
    gains = norm_gain.reshape(ctx_count, 1, width)

    split = ctx_count == 8
    chip_bits = bits_below(ctx_count)[1:]
    rows = []
    squares, core, own_request, first_row = call(
        functools.partial(squares_kernel, team, row_count),
        "squares",
        [IN_SMEM, IN_VMEM],
        (shape((requests, LANES)),) + (shape((1, LANES), jnp.int32),) * 3,
    )(places, new_tokens)

    def beside(received, sent, parts):
        first = len(rows) * NORM_ROWS
        rows.extend(normalise(after(ctx_hidden[0], sent), gains, first, parts))
        return after(received, rows[-1])

    def sum_chips(value, norm_parts=0):
        received = by_core(value, 4, 2)
        if norm_parts:
            received = beside(received, value, norm_parts)
        told = swap(received, "ctx", 1)
        opposite = by_core(told, 4, 2)
        if norm_parts:
            opposite = beside(opposite, told, row_count // NORM_ROWS - norm_parts)
        over_x = jnp.where(core == 0, told, received)
        over_y = jnp.where(core == 0, received, told)
        return (value + over_x) + (over_y + opposite), told, received

    key_partner = swap(key_weight[0], "ctx", 1)
    value_partner = swap(value_weight[0], "ctx", 1)
    key_near = [((0, 0), key_weight[0]), ((1, 1), key_partner)]
    value_near = [((0, 0), value_weight[0]), ((1, 1), value_partner)]
    key_far = send_first(key_weight[0], key_partner)

    squares = squares + swap(squares, "ctx", 1)
    squares = after(squares, key_partner, value_partner)
    if split:
        squares, told, _ = sum_chips(squares, row_count // NORM_ROWS // 2)
        key_shared = share(key_far, told)
        own_values = value_weight[0]
        squares = after(squares, key_far[1][1])
    else:
        key_shared = share(key_far)
        own_values = value_weight[0]
        squares = beside(squares, squares, row_count // NORM_ROWS)
        squares = butterfly(squares, "ctx", chip_bits, jnp.add)
    key_last = send_last(key_weight[0], key_shared)

    parts = call(
        functools.partial(query_kernel, features),
        "query_products",
        [IN_SMEM] + [IN_VMEM] * 6,
        shape((requests, heads + 2, head_size)),
    )(places, squares, new_tokens, gains, query_weight[0], key_weight[0], value_weight[0])
    parts = parts + swap(parts, "ctx", 1)
    parts_sent = parts
    value_far = send_first(own_values, value_partner)
    if split:
        parts, _, parts_sent = sum_chips(parts)
        summed = jnp.where(own_request == 0, parts[0], parts[1])
    else:
        own_part = jnp.where(own_request == 0, parts[0], parts[1])
        other_part = jnp.where(own_request == 0, parts[1], parts[0])
        summed = own_part + swap(other_part, "ctx", team)
        summed = butterfly(summed, "ctx", chip_bits[:-1], jnp.add)

    key_total = project(places, rows, key_near)
    key_total = project(places, rows, key_far + key_shared, key_total)
    key_mid = key_total
    key_total = project(places, rows, key_last + share(key_last, key_total), key_total)

    within = first_row[0, :1] + jnp.arange(row_count, dtype=jnp.int32)
    cosine, sine_part = tables(within.astype(jnp.float32), head_size)
    new_cosine, new_sine = tables(positions.astype(jnp.float32), head_size)
    masked, top, self_scores = call(
        functools.partial(score_kernel, team),
        "scores",
        [IN_SMEM] * 2 + [IN_VMEM] * 6,
        (shape((heads, row_count)), shape((heads, LANES)), shape((heads, LANES))),
    )(places, lengths, key_total, cosine, sine_part, new_cosine, new_sine, summed)
    value_first = share(value_far[:1], parts_sent)
    value_last = send_last(own_values, value_first)
    value_first += value_far[:1]
    top = butterfly(top, "ctx", [1], jnp.maximum)
    top = after(top, *[block for _, block in value_far[1:]])
    near_top = top
    value_total = project(after(places, near_top), rows, value_near + value_first)
    if split:
        received = jnp.maximum(top, after(by_core(top, 4, 2), value_last[0][1], value_total))
        top = jnp.where(core == 0, swap(received, "ctx", 1), received)
    else:
        top = butterfly(top, "ctx", bits_below(team)[1:], jnp.maximum)
        received = top

    value_second = value_far[1:] + share(value_far[1:], masked)
    value_total = project(places, rows, value_second, value_total)

    blocks = share(value_last, received)
    value_total = project(places, rows, value_last, value_total)
    packed = call(
        functools.partial(weigh_kernel, [d for d, _ in blocks], len(rows), team),
        "weighted_values",
        [IN_SMEM] * 2 + [IN_VMEM] * (len(rows) + len(blocks) + 5),
        shape((heads, 2 * head_size)),
    )(
        places,
        lengths,
        *rows,
        *[block for _, block in blocks],
        value_total,
        masked,
        top,
        self_scores,
        summed,
    )
    packed = butterfly(packed, "ctx", bits_below(team), jnp.add)
    other = swap(packed, "ctx", team)
    update = call(
        functools.partial(output_kernel, team),
        "output_products",
        [IN_SMEM] + [IN_VMEM] * 3,
        shape((requests, out_weight.shape[2])),
    )(places, packed, other, out_weight[0])
    return new_tokens + butterfly(update, "kv", bits_below(kv_count), jnp.add)


def solution(mesh):
    in_specs = (
        P(None, "ctx"),
        P(None, "ctx", None),
        P(),
        P(None, "ctx", "kv"),
        P(None, "ctx", "kv"),
        P(None, "ctx", "kv"),
        P(None, "kv", "ctx"),
        P(),
        P(),
    )
    out_specs = P(None, "ctx")
    return jax.shard_map(shards, mesh=mesh, in_specs=in_specs, out_specs=out_specs, check_vma=False)
```

```python
import functools
import math

import jax
import jax.numpy as jnp
from jax import lax
from jax.experimental import pallas as pl
from jax.experimental.pallas import tpu as pltpu
from jax.sharding import PartitionSpec as P

ROPE_BASE = 500000.0
EPSILON = 1e-05
FLOOR = -1e30
LANES = 128
NORM_ROWS = 64
GROUP_ROWS = 16
VMEM_BYTES = 16 * 1024 * 1024
CHEAP = pl.CostEstimate(flops=1000, bytes_accessed=1000, transcendentals=0)
IN_VMEM = pl.BlockSpec(memory_space=pltpu.VMEM)
IN_SMEM = pl.BlockSpec(memory_space=pltpu.SMEM)
IN_HBM = pl.BlockSpec(memory_space=pltpu.HBM)


def call(kernel, name, in_specs, out_shape, scratch_shapes=()):
    return pl.pallas_call(
        kernel,
        in_specs=in_specs,
        out_specs=jax.tree.map(lambda _: IN_VMEM, out_shape),
        out_shape=out_shape,
        scratch_shapes=scratch_shapes,
        compiler_params=pltpu.CompilerParams(vmem_limit_bytes=VMEM_BYTES),
        cost_estimate=CHEAP,
        name=name,
    )


def shape(dims, dtype=jnp.float32):
    return jax.ShapeDtypeStruct(dims, dtype)


def swap(value, axis, distance):
    count = lax.axis_size(axis)
    return lax.ppermute(value, axis, [(i, i ^ distance) for i in range(count)])


def after(value, *others):
    return lax.optimization_barrier((value, *others))[0]


def bits_below(count):
    return [1 << b for b in range(count.bit_length() - 1)]


def butterfly(value, axis, bits, join):
    for bit in bits:
        value = join(value, swap(value, axis, bit))
    return value


def by_core(value, bit_0, bit_1):
    count = lax.axis_size("ctx")
    bits = (bit_0, bit_1)
    pairs = [(i, i ^ bits[i % 2]) for i in range(count) if bits[i % 2]]
    return lax.ppermute(value, "ctx", pairs)


def send_first(own, partner):
    count = lax.axis_size("ctx")
    if count != 8:
        return [((d, d), swap(own, "ctx", d)) for d in range(2, count // 2)]
    return [((2, 4), by_core(own, 2, 4)), ((3, 5), by_core(partner, 2, 4))]


def share(blocks, *before):
    count = lax.axis_size("ctx")
    if count != 8:
        return []
    return [
        ((odd ^ 1, even ^ 1), swap(after(block, *before) if before else block, "ctx", 1))
        for (even, odd), block in blocks
    ]


def send_last(own, received):
    count = lax.axis_size("ctx")
    if count != 8:
        return [((d, d), swap(own, "ctx", d)) for d in range(count // 2, count)]
    return [((7, 7), by_core(received[0][1], 2, 4))]


def tables(placed, head_size):
    half_size = head_size // 2
    frequency = jnp.exp(
        jnp.arange(half_size, dtype=jnp.float32) * (-2.0 * math.log(ROPE_BASE) / head_size)
    )
    angles = placed[..., None] * frequency
    return jnp.cos(angles), jnp.sin(angles)


def turn(values, cosine, sine_part):
    half_size = values.shape[-1] // 2
    leading = values[:, :half_size]
    trailing = values[:, half_size:]
    return jnp.concatenate(
        (leading * cosine - trailing * sine_part, trailing * cosine + leading * sine_part), axis=-1
    )


def squares_kernel(team, row_count, place_ref, tokens_ref, out_ref, core_ref, request_ref, row_ref):
    values = tokens_ref[...]
    total = jnp.sum(values * values, axis=-1, keepdims=True)
    out_ref[...] = jnp.broadcast_to(total, out_ref.shape)
    place = place_ref[0]
    core_ref[...] = jnp.full(core_ref.shape, lax.rem(place, 2))
    request_ref[...] = jnp.full(request_ref.shape, lax.div(place, team))
    row_ref[...] = jnp.full(row_ref.shape, lax.rem(place, team) * row_count)


def norm_kernel(first, x_ref, gain_hbm_ref, *refs):
    out_refs, (held_ref, gain_ref, sems, gain_sem) = refs[:-4], refs[-4:]
    blocks, rows, width = out_refs[0].shape
    features = blocks * width
    groups = len(out_refs) * rows // GROUP_ROWS
    tiles = width // LANES

    def copy(g):
        return pltpu.make_async_copy(
            x_ref.at[pl.ds(first + g * GROUP_ROWS, GROUP_ROWS), :], held_ref.at[g], sems.at[g]
        )

    def factor_of(g):
        totals = [jnp.zeros((GROUP_ROWS, LANES), jnp.float32) for _ in range(4)]
        for j in range(blocks * tiles):
            values = held_ref[g, :, j * LANES : (j + 1) * LANES].astype(jnp.float32)
            totals[j % 4] = totals[j % 4] + values * values
        total = (totals[0] + totals[1]) + (totals[2] + totals[3])
        mean = jnp.sum(total, axis=-1, keepdims=True) / features
        return jnp.broadcast_to(lax.rsqrt(mean + EPSILON), (GROUP_ROWS, LANES))

    def scale(g, factor, out_ref, row):
        part = pl.ds(pl.multiple_of(row, GROUP_ROWS), GROUP_ROWS)
        for b in range(blocks):
            for j in range(tiles):
                lanes = slice(j * LANES, (j + 1) * LANES)
                from_lane = b * width + j * LANES
                values = held_ref[g, :, from_lane : from_lane + LANES].astype(jnp.float32)
                out_ref[b, part, lanes] = (values * factor * gain_ref[b, :, lanes]).astype(
                    jnp.bfloat16
                )

    gain_copy = pltpu.make_async_copy(gain_hbm_ref, gain_ref, gain_sem)
    for g in range(groups):
        copy(g).start()
        if g == 0:
            gain_copy.start()
    copy(0).wait()

    factor = factor_of(0)
    gain_copy.wait()
    for i, out_ref in enumerate(out_refs):
        start = i * rows // GROUP_ROWS
        stop = min(start + rows // GROUP_ROWS, groups - 1)

        def step(g, factor, out_ref=out_ref, start=start):
            copy(g + 1).wait()
            following = factor_of(g + 1)
            scale(g, factor, out_ref, (g - start) * GROUP_ROWS)
            return following

        factor = lax.fori_loop(start, stop, step, factor)
    scale(groups - 1, factor, out_refs[-1], rows - GROUP_ROWS)


def normalise(hidden, gains, first, parts):
    blocks, _, width = gains.shape
    groups = parts * NORM_ROWS // GROUP_ROWS
    return call(
        functools.partial(norm_kernel, first),
        "normalise",
        [IN_HBM, IN_HBM],
        (shape((blocks, NORM_ROWS, width), jnp.bfloat16),) * parts,
        [
            pltpu.VMEM((groups, GROUP_ROWS, blocks * width), jnp.bfloat16),
            pltpu.VMEM(gains.shape, jnp.float32),
            pltpu.SemaphoreType.DMA((groups,)),
            pltpu.SemaphoreType.DMA(()),
        ],
    )(
        pltpu.with_memory_space_constraint(hidden, pltpu.HBM),
        pltpu.with_memory_space_constraint(gains, pltpu.HBM),
    )


def query_kernel(
    features, place_ref, squares_ref, tokens_ref, gains_ref, query_ref, key_ref, value_ref, out_ref
):
    requests = tokens_ref.shape[0]
    factor = lax.rsqrt(squares_ref[:, :1] / features + EPSILON)
    normed = (tokens_ref[...] * factor * gains_ref[place_ref[0]]).astype(jnp.bfloat16)
    row = 0
    for weight_ref in (query_ref, key_ref, value_ref):
        part = jnp.dot(normed, weight_ref[...], preferred_element_type=jnp.float32)
        for h in range(weight_ref.shape[1] // LANES):
            for r in range(requests):
                out_ref[r, row : row + 1, :] = part[r : r + 1, h * LANES : (h + 1) * LANES]
            row += 1


def blocks_dot(distances, place, row_refs, block_refs, total):
    for (even, odd), block_ref in zip(distances, block_refs):
        distance = jnp.where(lax.rem(place, 2) == 0, even, odd)
        rows = jnp.concatenate([ref[place ^ distance] for ref in row_refs], axis=0)
        part = jnp.dot(rows, block_ref[...], preferred_element_type=jnp.float32)
        total = part if total is None else total + part
    return total


def project_kernel(distances, row_count, has_total, place_ref, *refs):
    rows, refs = refs[:row_count], refs[row_count:]
    total = refs[len(distances)][...] if has_total else None
    refs[-1][...] = blocks_dot(distances, place_ref[0], rows, refs, total)


def project(place, rows, blocks, total=None):
    extra = [] if total is None else [total]
    row_count = sum(r.shape[1] for r in rows)
    return call(
        functools.partial(project_kernel, [d for d, _ in blocks], len(rows), total is not None),
        "project",
        [IN_SMEM] + [IN_VMEM] * (len(rows) + len(blocks) + len(extra)),
        shape((row_count, LANES)),
    )(place, *rows, *[block for _, block in blocks], *extra)


def live_rows(dims, team, place, lengths_ref):
    rows = dims[1]
    within = lax.rem(place, team) * rows + lax.broadcasted_iota(jnp.int32, dims, 1)
    return within < lengths_ref[lax.div(place, team)]


def score_kernel(team, place_ref, lengths_ref, *refs):
    keys_ref, cos_ref, sin_ref, new_cos_ref, new_sin_ref, summed_ref = refs[:6]
    masked_ref, top_ref, self_ref = refs[6:]
    place = place_ref[0]
    request = lax.div(place, team)
    heads = masked_ref.shape[0]
    scale = 1.0 / math.sqrt(LANES)
    turned = turn(
        summed_ref[...], new_cos_ref[pl.ds(request, 1), :], new_sin_ref[pl.ds(request, 1), :]
    ).astype(jnp.bfloat16)
    queries = turned[:heads]
    self_key = turned[heads : heads + 1].astype(jnp.float32)
    self_scores = (
        jnp.sum(queries.astype(jnp.float32) * self_key, axis=-1, keepdims=True) * scale
    )
    keys = turn(keys_ref[...], cos_ref[...], sin_ref[...]).astype(jnp.bfloat16)
    scores = (
        lax.dot_general(
            queries, keys, (((1,), (1,)), ((), ())), preferred_element_type=jnp.float32
        )
        * scale
    )
    masked = jnp.where(live_rows(scores.shape, team, place, lengths_ref), scores, FLOOR)
    masked_ref[...] = masked
    top = jnp.maximum(jnp.max(masked, axis=-1, keepdims=True), self_scores)
    top_ref[...] = jnp.broadcast_to(top, top_ref.shape)
    self_ref[...] = jnp.broadcast_to(self_scores, self_ref.shape)


def weigh_kernel(distances, row_count, team, place_ref, lengths_ref, *refs):
    rows, refs = refs[:row_count], refs[row_count:]
    blocks, refs = refs[: len(distances)], refs[len(distances) :]
    total_ref, masked_ref, top_ref, self_ref, summed_ref, out_ref = refs
    place = place_ref[0]
    heads = masked_ref.shape[0]
    masked = masked_ref[...]
    top = top_ref[:, :1]
    live = live_rows(masked.shape, team, place, lengths_ref)
    weights = jnp.where(live, jnp.exp(masked - top), 0.0).astype(jnp.bfloat16)
    self_weight = jnp.exp(self_ref[...] - top_ref[...]).astype(jnp.bfloat16).astype(jnp.float32)
    self_weight = jnp.where(lax.rem(place, team) == 0, self_weight, 0.0)
    self_value = summed_ref[heads + 1 : heads + 2, :].astype(jnp.bfloat16).astype(jnp.float32)
    mass = jnp.sum(weights.astype(jnp.float32), axis=-1, keepdims=True) + self_weight
    values = blocks_dot(distances, place, rows, blocks, total_ref[...]).astype(jnp.bfloat16)
    accum = jnp.dot(weights, values, preferred_element_type=jnp.float32)
    out_ref[:, :LANES] = accum + self_weight * self_value
    out_ref[:, LANES:] = mass


def output_kernel(team, place_ref, mine_ref, other_ref, weight_ref, out_ref):
    request = lax.div(place_ref[0], team)
    heads = mine_ref.shape[0]
    attended = []
    for ref in (mine_ref, other_ref):
        attended.append(ref[:, :LANES] / ref[:, LANES:])
    first = jnp.where(request == 0, attended[0], attended[1]).astype(jnp.bfloat16)
    second = jnp.where(request == 0, attended[1], attended[0]).astype(jnp.bfloat16)
    both = jnp.concatenate(
        [
            jnp.concatenate((first[h : h + 1], second[h : h + 1]), axis=0)
            for h in range(heads)
        ],
        axis=1,
    )
    out_ref[...] = jnp.dot(both, weight_ref[...], preferred_element_type=jnp.float32)


def shards(
    new_tokens,
    ctx_hidden,
    norm_gain,
    query_weight,
    key_weight,
    value_weight,
    out_weight,
    lengths,
    positions,
):
    ctx_count = lax.axis_size("ctx")
    kv_count = lax.axis_size("kv")
    place = lax.axis_index("ctx").astype(jnp.int32)
    places = place.reshape(1)
    row_count, features = ctx_hidden.shape[1:]
    head_size = key_weight.shape[2]
    heads = query_weight.shape[2] // head_size
    requests, width = new_tokens.shape
    slot_count = row_count * ctx_count // requests
    team = slot_count // row_count
    assert requests == 2 and slot_count % row_count == 0 and row_count % NORM_ROWS == 0
    assert head_size == LANES
    gains = norm_gain.reshape(ctx_count, 1, width)

    split = ctx_count == 8
    chip_bits = bits_below(ctx_count)[1:]
    rows = []
    squares, core, own_request, first_row = call(
        functools.partial(squares_kernel, team, row_count),
        "squares",
        [IN_SMEM, IN_VMEM],
        (shape((requests, LANES)),) + (shape((1, LANES), jnp.int32),) * 3,
    )(places, new_tokens)

    def beside(received, sent, parts):
        first = len(rows) * NORM_ROWS
        rows.extend(normalise(after(ctx_hidden[0], sent), gains, first, parts))
        return after(received, rows[-1])

    def sum_chips(value, norm_parts=0):
        received = by_core(value, 4, 2)
        if norm_parts:
            received = beside(received, value, norm_parts)
        told = swap(received, "ctx", 1)
        opposite = by_core(told, 4, 2)
        if norm_parts:
            opposite = beside(opposite, told, row_count // NORM_ROWS - norm_parts)
        over_x = jnp.where(core == 0, told, received)
        over_y = jnp.where(core == 0, received, told)
        return (value + over_x) + (over_y + opposite), told, received

    key_partner = swap(key_weight[0], "ctx", 1)
    value_partner = swap(value_weight[0], "ctx", 1)
    key_near = [((0, 0), key_weight[0]), ((1, 1), key_partner)]
    value_near = [((0, 0), value_weight[0]), ((1, 1), value_partner)]
    key_far = send_first(key_weight[0], key_partner)

    squares = squares + swap(squares, "ctx", 1)
    squares = after(squares, key_partner, value_partner)
    if split:
        squares, told, _ = sum_chips(squares, row_count // NORM_ROWS // 2)
        key_shared = share(key_far, told)
        own_values = value_weight[0]
        squares = after(squares, key_far[1][1])
    else:
        key_shared = share(key_far)
        own_values = value_weight[0]
        squares = beside(squares, squares, row_count // NORM_ROWS)
        squares = butterfly(squares, "ctx", chip_bits, jnp.add)
    key_last = send_last(key_weight[0], key_shared)

    parts = call(
        functools.partial(query_kernel, features),
        "query_products",
        [IN_SMEM] + [IN_VMEM] * 6,
        shape((requests, heads + 2, head_size)),
    )(places, squares, new_tokens, gains, query_weight[0], key_weight[0], value_weight[0])
    parts = parts + swap(parts, "ctx", 1)
    parts_sent = parts
    value_far = send_first(own_values, value_partner)
    if split:
        parts, _, parts_sent = sum_chips(parts)
        summed = jnp.where(own_request == 0, parts[0], parts[1])
    else:
        own_part = jnp.where(own_request == 0, parts[0], parts[1])
        other_part = jnp.where(own_request == 0, parts[1], parts[0])
        summed = own_part + swap(other_part, "ctx", team)
        summed = butterfly(summed, "ctx", chip_bits[:-1], jnp.add)

    key_total = project(places, rows, key_near)
    key_total = project(places, rows, key_far + key_shared, key_total)
    key_mid = key_total
    key_total = project(places, rows, key_last + share(key_last, key_total), key_total)

    within = first_row[0, :1] + jnp.arange(row_count, dtype=jnp.int32)
    cosine, sine_part = tables(within.astype(jnp.float32), head_size)
    new_cosine, new_sine = tables(positions.astype(jnp.float32), head_size)
    masked, top, self_scores = call(
        functools.partial(score_kernel, team),
        "scores",
        [IN_SMEM] * 2 + [IN_VMEM] * 6,
        (shape((heads, row_count)), shape((heads, LANES)), shape((heads, LANES))),
    )(places, lengths, key_total, cosine, sine_part, new_cosine, new_sine, summed)
    value_first = share(value_far[:1], parts_sent)
    value_last = send_last(own_values, value_first)
    value_first += value_far[:1]
    top = butterfly(top, "ctx", [1], jnp.maximum)
    top = after(top, *[block for _, block in value_far[1:]])
    near_top = top
    value_total = project(after(places, near_top), rows, value_near + value_first)
    if split:
        received = jnp.maximum(top, after(by_core(top, 4, 2), value_last[0][1], value_total))
        top = jnp.where(core == 0, swap(received, "ctx", 1), received)
    else:
        top = butterfly(top, "ctx", bits_below(team)[1:], jnp.maximum)
        received = top

    value_second = value_far[1:] + share(value_far[1:], near_top)
    value_total = project(places, rows, value_second, value_total)

    blocks = share(value_last, received)
    value_total = project(places, rows, value_last, value_total)
    packed = call(
        functools.partial(weigh_kernel, [d for d, _ in blocks], len(rows), team),
        "weighted_values",
        [IN_SMEM] * 2 + [IN_VMEM] * (len(rows) + len(blocks) + 5),
        shape((heads, 2 * head_size)),
    )(
        places,
        lengths,
        *rows,
        *[block for _, block in blocks],
        value_total,
        masked,
        top,
        self_scores,
        summed,
    )
    packed = butterfly(packed, "ctx", bits_below(team), jnp.add)
    other = swap(packed, "ctx", team)
    update = call(
        functools.partial(output_kernel, team),
        "output_products",
        [IN_SMEM] + [IN_VMEM] * 3,
        shape((requests, out_weight.shape[2])),
    )(places, packed, other, out_weight[0])
    return new_tokens + butterfly(update, "kv", bits_below(kv_count), jnp.add)


def solution(mesh):
    in_specs = (
        P(None, "ctx"),
        P(None, "ctx", None),
        P(),
        P(None, "ctx", "kv"),
        P(None, "ctx", "kv"),
        P(None, "ctx", "kv"),
        P(None, "kv", "ctx"),
        P(),
        P(),
    )
    out_specs = P(None, "ctx")
    return jax.shard_map(shards, mesh=mesh, in_specs=in_specs, out_specs=out_specs, check_vma=False)
```

```python
import functools
import math

import jax
import jax.numpy as jnp
from jax import lax
from jax.experimental import pallas as pl
from jax.experimental.pallas import tpu as pltpu
from jax.sharding import PartitionSpec as P

ROPE_BASE = 500000.0
EPSILON = 1e-05
FLOOR = -1e30
LANES = 128
NORM_ROWS = 64
GROUP_ROWS = 16
VMEM_BYTES = 16 * 1024 * 1024
CHEAP = pl.CostEstimate(flops=1000, bytes_accessed=1000, transcendentals=0)
IN_VMEM = pl.BlockSpec(memory_space=pltpu.VMEM)
IN_SMEM = pl.BlockSpec(memory_space=pltpu.SMEM)
IN_HBM = pl.BlockSpec(memory_space=pltpu.HBM)


def call(kernel, name, in_specs, out_shape, scratch_shapes=()):
    return pl.pallas_call(
        kernel,
        in_specs=in_specs,
        out_specs=jax.tree.map(lambda _: IN_VMEM, out_shape),
        out_shape=out_shape,
        scratch_shapes=scratch_shapes,
        compiler_params=pltpu.CompilerParams(vmem_limit_bytes=VMEM_BYTES),
        cost_estimate=CHEAP,
        name=name,
    )


def shape(dims, dtype=jnp.float32):
    return jax.ShapeDtypeStruct(dims, dtype)


def swap(value, axis, distance):
    count = lax.axis_size(axis)
    return lax.ppermute(value, axis, [(i, i ^ distance) for i in range(count)])


def after(value, *others):
    return lax.optimization_barrier((value, *others))[0]


def bits_below(count):
    return [1 << b for b in range(count.bit_length() - 1)]


def butterfly(value, axis, bits, join):
    for bit in bits:
        value = join(value, swap(value, axis, bit))
    return value


def by_core(value, bit_0, bit_1):
    count = lax.axis_size("ctx")
    bits = (bit_0, bit_1)
    pairs = [(i, i ^ bits[i % 2]) for i in range(count) if bits[i % 2]]
    return lax.ppermute(value, "ctx", pairs)


def send_first(own, partner):
    count = lax.axis_size("ctx")
    if count != 8:
        return [((d, d), swap(own, "ctx", d)) for d in range(2, count // 2)]
    return [((2, 4), by_core(own, 2, 4)), ((3, 5), by_core(partner, 2, 4))]


def share(blocks, *before):
    count = lax.axis_size("ctx")
    if count != 8:
        return []
    return [
        ((odd ^ 1, even ^ 1), swap(after(block, *before) if before else block, "ctx", 1))
        for (even, odd), block in blocks
    ]


def send_last(own, received):
    count = lax.axis_size("ctx")
    if count != 8:
        return [((d, d), swap(own, "ctx", d)) for d in range(count // 2, count)]
    return [((7, 7), by_core(received[0][1], 2, 4))]


def tables(placed, head_size):
    half_size = head_size // 2
    frequency = jnp.exp(
        jnp.arange(half_size, dtype=jnp.float32) * (-2.0 * math.log(ROPE_BASE) / head_size)
    )
    angles = placed[..., None] * frequency
    return jnp.cos(angles), jnp.sin(angles)


def turn(values, cosine, sine_part):
    half_size = values.shape[-1] // 2
    leading = values[:, :half_size]
    trailing = values[:, half_size:]
    return jnp.concatenate(
        (leading * cosine - trailing * sine_part, trailing * cosine + leading * sine_part), axis=-1
    )


def squares_kernel(team, row_count, place_ref, tokens_ref, out_ref, core_ref, request_ref, row_ref):
    values = tokens_ref[...]
    total = jnp.sum(values * values, axis=-1, keepdims=True)
    out_ref[...] = jnp.broadcast_to(total, out_ref.shape)
    place = place_ref[0]
    core_ref[...] = jnp.full(core_ref.shape, lax.rem(place, 2))
    request_ref[...] = jnp.full(request_ref.shape, lax.div(place, team))
    row_ref[...] = jnp.full(row_ref.shape, lax.rem(place, team) * row_count)


def norm_kernel(first, x_ref, gain_ref, *refs):
    out_refs, (held_ref, sems) = refs[:-2], refs[-2:]
    blocks, rows, width = out_refs[0].shape
    features = blocks * width
    groups = len(out_refs) * rows // GROUP_ROWS
    tiles = width // LANES

    def copy(g):
        return pltpu.make_async_copy(
            x_ref.at[pl.ds(first + g * GROUP_ROWS, GROUP_ROWS), :], held_ref.at[g], sems.at[g]
        )

    def factor_of(g):
        totals = [jnp.zeros((GROUP_ROWS, LANES), jnp.float32) for _ in range(4)]
        for j in range(blocks * tiles):
            values = held_ref[g, :, j * LANES : (j + 1) * LANES].astype(jnp.float32)
            totals[j % 4] = totals[j % 4] + values * values
        total = (totals[0] + totals[1]) + (totals[2] + totals[3])
        mean = jnp.sum(total, axis=-1, keepdims=True) / features
        return jnp.broadcast_to(lax.rsqrt(mean + EPSILON), (GROUP_ROWS, LANES))

    def scale(g, factor, out_ref, row):
        part = pl.ds(pl.multiple_of(row, GROUP_ROWS), GROUP_ROWS)
        for b in range(blocks):
            for j in range(tiles):
                lanes = slice(j * LANES, (j + 1) * LANES)
                from_lane = b * width + j * LANES
                values = held_ref[g, :, from_lane : from_lane + LANES].astype(jnp.float32)
                out_ref[b, part, lanes] = (values * factor * gain_ref[b, :, lanes]).astype(
                    jnp.bfloat16
                )

    for g in range(groups):
        copy(g).start()
    copy(0).wait()

    factor = factor_of(0)
    for i, out_ref in enumerate(out_refs):
        start = i * rows // GROUP_ROWS
        stop = min(start + rows // GROUP_ROWS, groups - 1)

        def step(g, factor, out_ref=out_ref, start=start):
            copy(g + 1).wait()
            following = factor_of(g + 1)
            scale(g, factor, out_ref, (g - start) * GROUP_ROWS)
            return following

        factor = lax.fori_loop(start, stop, step, factor)
    scale(groups - 1, factor, out_refs[-1], rows - GROUP_ROWS)


def normalise(hidden, gains, first, parts):
    blocks, _, width = gains.shape
    groups = parts * NORM_ROWS // GROUP_ROWS
    return call(
        functools.partial(norm_kernel, first),
        "normalise",
        [IN_HBM, IN_VMEM],
        (shape((blocks, NORM_ROWS, width), jnp.bfloat16),) * parts,
        [
            pltpu.VMEM((groups, GROUP_ROWS, blocks * width), jnp.bfloat16),
            pltpu.SemaphoreType.DMA((groups,)),
        ],
    )(pltpu.with_memory_space_constraint(hidden, pltpu.HBM), gains)


def query_kernel(
    features, place_ref, squares_ref, tokens_ref, gains_ref, query_ref, key_ref, value_ref, out_ref
):
    requests = tokens_ref.shape[0]
    factor = lax.rsqrt(squares_ref[:, :1] / features + EPSILON)
    normed = (tokens_ref[...] * factor * gains_ref[place_ref[0]]).astype(jnp.bfloat16)
    row = 0
    for weight_ref in (query_ref, key_ref, value_ref):
        part = jnp.dot(normed, weight_ref[...], preferred_element_type=jnp.float32)
        for h in range(weight_ref.shape[1] // LANES):
            for r in range(requests):
                out_ref[r, row : row + 1, :] = part[r : r + 1, h * LANES : (h + 1) * LANES]
            row += 1


def blocks_dot(distances, place, row_refs, block_refs, total):
    for (even, odd), block_ref in zip(distances, block_refs):
        distance = jnp.where(lax.rem(place, 2) == 0, even, odd)
        rows = jnp.concatenate([ref[place ^ distance] for ref in row_refs], axis=0)
        part = jnp.dot(rows, block_ref[...], preferred_element_type=jnp.float32)
        total = part if total is None else total + part
    return total


def project_kernel(distances, row_count, has_total, place_ref, *refs):
    rows, refs = refs[:row_count], refs[row_count:]
    total = refs[len(distances)][...] if has_total else None
    refs[-1][...] = blocks_dot(distances, place_ref[0], rows, refs, total)


def project(place, rows, blocks, total=None):
    extra = [] if total is None else [total]
    row_count = sum(r.shape[1] for r in rows)
    return call(
        functools.partial(project_kernel, [d for d, _ in blocks], len(rows), total is not None),
        "project",
        [IN_SMEM] + [IN_VMEM] * (len(rows) + len(blocks) + len(extra)),
        shape((row_count, LANES)),
    )(place, *rows, *[block for _, block in blocks], *extra)


def live_rows(dims, team, place, lengths_ref):
    rows = dims[1]
    within = lax.rem(place, team) * rows + lax.broadcasted_iota(jnp.int32, dims, 1)
    return within < lengths_ref[lax.div(place, team)]


def score_kernel(team, place_ref, lengths_ref, *refs):
    keys_ref, cos_ref, sin_ref, new_cos_ref, new_sin_ref, summed_ref = refs[:6]
    masked_ref, top_ref, self_ref = refs[6:]
    place = place_ref[0]
    request = lax.div(place, team)
    heads = masked_ref.shape[0]
    scale = 1.0 / math.sqrt(LANES)
    turned = turn(
        summed_ref[...], new_cos_ref[pl.ds(request, 1), :], new_sin_ref[pl.ds(request, 1), :]
    ).astype(jnp.bfloat16)
    queries = turned[:heads]
    self_key = turned[heads : heads + 1].astype(jnp.float32)
    self_scores = (
        jnp.sum(queries.astype(jnp.float32) * self_key, axis=-1, keepdims=True) * scale
    )
    keys = turn(keys_ref[...], cos_ref[...], sin_ref[...]).astype(jnp.bfloat16)
    scores = (
        lax.dot_general(
            queries, keys, (((1,), (1,)), ((), ())), preferred_element_type=jnp.float32
        )
        * scale
    )
    masked = jnp.where(live_rows(scores.shape, team, place, lengths_ref), scores, FLOOR)
    masked_ref[...] = masked
    top = jnp.maximum(jnp.max(masked, axis=-1, keepdims=True), self_scores)
    top_ref[...] = jnp.broadcast_to(top, top_ref.shape)
    self_ref[...] = jnp.broadcast_to(self_scores, self_ref.shape)


def weigh_kernel(distances, row_count, team, place_ref, lengths_ref, *refs):
    rows, refs = refs[:row_count], refs[row_count:]
    blocks, refs = refs[: len(distances)], refs[len(distances) :]
    total_ref, masked_ref, top_ref, self_ref, summed_ref, out_ref = refs
    place = place_ref[0]
    heads = masked_ref.shape[0]
    masked = masked_ref[...]
    top = top_ref[:, :1]
    live = live_rows(masked.shape, team, place, lengths_ref)
    weights = jnp.where(live, jnp.exp(masked - top), 0.0).astype(jnp.bfloat16)
    self_weight = jnp.exp(self_ref[...] - top_ref[...]).astype(jnp.bfloat16).astype(jnp.float32)
    self_weight = jnp.where(lax.rem(place, team) == 0, self_weight, 0.0)
    self_value = summed_ref[heads + 1 : heads + 2, :].astype(jnp.bfloat16).astype(jnp.float32)
    mass = jnp.sum(weights.astype(jnp.float32), axis=-1, keepdims=True) + self_weight
    values = blocks_dot(distances, place, rows, blocks, total_ref[...]).astype(jnp.bfloat16)
    accum = jnp.dot(weights, values, preferred_element_type=jnp.float32)
    out_ref[:, :LANES] = accum + self_weight * self_value
    out_ref[:, LANES:] = mass


def output_kernel(team, place_ref, mine_ref, other_ref, weight_ref, out_ref):
    request = lax.div(place_ref[0], team)
    heads = mine_ref.shape[0]
    attended = []
    for ref in (mine_ref, other_ref):
        attended.append(ref[:, :LANES] / ref[:, LANES:])
    first = jnp.where(request == 0, attended[0], attended[1]).astype(jnp.bfloat16)
    second = jnp.where(request == 0, attended[1], attended[0]).astype(jnp.bfloat16)
    both = jnp.concatenate(
        [
            jnp.concatenate((first[h : h + 1], second[h : h + 1]), axis=0)
            for h in range(heads)
        ],
        axis=1,
    )
    out_ref[...] = jnp.dot(both, weight_ref[...], preferred_element_type=jnp.float32)


def shards(
    new_tokens,
    ctx_hidden,
    norm_gain,
    query_weight,
    key_weight,
    value_weight,
    out_weight,
    lengths,
    positions,
):
    ctx_count = lax.axis_size("ctx")
    kv_count = lax.axis_size("kv")
    place = lax.axis_index("ctx").astype(jnp.int32)
    places = place.reshape(1)
    row_count, features = ctx_hidden.shape[1:]
    head_size = key_weight.shape[2]
    heads = query_weight.shape[2] // head_size
    requests, width = new_tokens.shape
    slot_count = row_count * ctx_count // requests
    team = slot_count // row_count
    assert requests == 2 and slot_count % row_count == 0 and row_count % NORM_ROWS == 0
    assert head_size == LANES
    gains = norm_gain.reshape(ctx_count, 1, width)

    split = ctx_count == 8
    chip_bits = bits_below(ctx_count)[1:]
    rows = []
    squares, core, own_request, first_row = call(
        functools.partial(squares_kernel, team, row_count),
        "squares",
        [IN_SMEM, IN_VMEM],
        (shape((requests, LANES)),) + (shape((1, LANES), jnp.int32),) * 3,
    )(places, new_tokens)

    def beside(received, sent, parts):
        first = len(rows) * NORM_ROWS
        rows.extend(normalise(after(ctx_hidden[0], sent), gains, first, parts))
        return after(received, rows[-1])

    def sum_chips(value, first_parts=0, second_parts=0):
        received = by_core(value, 4, 2)
        if first_parts:
            received = beside(received, value, first_parts)
        told = swap(received, "ctx", 1)
        opposite = by_core(told, 4, 2)
        if second_parts:
            opposite = beside(opposite, told, second_parts)
        over_x = jnp.where(core == 0, told, received)
        over_y = jnp.where(core == 0, received, told)
        return (value + over_x) + (over_y + opposite), told, received

    key_partner = swap(key_weight[0], "ctx", 1)
    value_partner = swap(value_weight[0], "ctx", 1)
    key_near = [((0, 0), key_weight[0]), ((1, 1), key_partner)]
    value_near = [((0, 0), value_weight[0]), ((1, 1), value_partner)]
    key_far = send_first(key_weight[0], key_partner)

    squares = squares + swap(squares, "ctx", 1)
    squares = after(squares, key_partner, value_partner)
    if split:
        squares, told, _ = sum_chips(squares, 2, row_count // NORM_ROWS - 3)
        key_shared = share(key_far, told)
        own_values = value_weight[0]
        squares = after(squares, key_far[1][1])
    else:
        key_shared = share(key_far)
        own_values = value_weight[0]
        squares = beside(squares, squares, row_count // NORM_ROWS)
        squares = butterfly(squares, "ctx", chip_bits, jnp.add)
    key_last = send_last(key_weight[0], key_shared)

    parts = call(
        functools.partial(query_kernel, features),
        "query_products",
        [IN_SMEM] + [IN_VMEM] * 6,
        shape((requests, heads + 2, head_size)),
    )(places, squares, new_tokens, gains, query_weight[0], key_weight[0], value_weight[0])
    parts = parts + swap(parts, "ctx", 1)
    parts_sent = parts
    value_far = send_first(own_values, value_partner)
    if split:
        parts, _, parts_sent = sum_chips(parts, 1)
        summed = jnp.where(own_request == 0, parts[0], parts[1])
    else:
        own_part = jnp.where(own_request == 0, parts[0], parts[1])
        other_part = jnp.where(own_request == 0, parts[1], parts[0])
        summed = own_part + swap(other_part, "ctx", team)
        summed = butterfly(summed, "ctx", chip_bits[:-1], jnp.add)

    key_total = project(places, rows, key_near)
    key_total = project(places, rows, key_far + key_shared, key_total)
    key_mid = key_total
    key_total = project(places, rows, key_last + share(key_last, key_total), key_total)

    within = first_row[0, :1] + jnp.arange(row_count, dtype=jnp.int32)
    cosine, sine_part = tables(within.astype(jnp.float32), head_size)
    new_cosine, new_sine = tables(positions.astype(jnp.float32), head_size)
    masked, top, self_scores = call(
        functools.partial(score_kernel, team),
        "scores",
        [IN_SMEM] * 2 + [IN_VMEM] * 6,
        (shape((heads, row_count)), shape((heads, LANES)), shape((heads, LANES))),
    )(places, lengths, key_total, cosine, sine_part, new_cosine, new_sine, summed)
    value_first = share(value_far[:1], parts_sent)
    value_last = send_last(own_values, value_first)
    value_first += value_far[:1]
    top = butterfly(top, "ctx", [1], jnp.maximum)
    top = after(top, *[block for _, block in value_far[1:]])
    near_top = top
    value_total = project(after(places, near_top), rows, value_near + value_first)
    if split:
        received = jnp.maximum(top, after(by_core(top, 4, 2), value_last[0][1], value_total))
        top = jnp.where(core == 0, swap(received, "ctx", 1), received)
    else:
        top = butterfly(top, "ctx", bits_below(team)[1:], jnp.maximum)
        received = top

    value_second = value_far[1:] + share(value_far[1:], near_top)
    value_total = project(places, rows, value_second, value_total)

    blocks = share(value_last, received)
    value_total = project(places, rows, value_last, value_total)
    packed = call(
        functools.partial(weigh_kernel, [d for d, _ in blocks], len(rows), team),
        "weighted_values",
        [IN_SMEM] * 2 + [IN_VMEM] * (len(rows) + len(blocks) + 5),
        shape((heads, 2 * head_size)),
    )(
        places,
        lengths,
        *rows,
        *[block for _, block in blocks],
        value_total,
        masked,
        top,
        self_scores,
        summed,
    )
    packed = butterfly(packed, "ctx", bits_below(team), jnp.add)
    other = swap(packed, "ctx", team)
    update = call(
        functools.partial(output_kernel, team),
        "output_products",
        [IN_SMEM] + [IN_VMEM] * 3,
        shape((requests, out_weight.shape[2])),
    )(places, packed, other, out_weight[0])
    return new_tokens + butterfly(update, "kv", bits_below(kv_count), jnp.add)


def solution(mesh):
    in_specs = (
        P(None, "ctx"),
        P(None, "ctx", None),
        P(),
        P(None, "ctx", "kv"),
        P(None, "ctx", "kv"),
        P(None, "ctx", "kv"),
        P(None, "kv", "ctx"),
        P(),
        P(),
    )
    out_specs = P(None, "ctx")
    return jax.shard_map(shards, mesh=mesh, in_specs=in_specs, out_specs=out_specs, check_vma=False)
```

```python
import functools
import math

import jax
import jax.numpy as jnp
from jax import lax
from jax.experimental import pallas as pl
from jax.experimental.pallas import tpu as pltpu
from jax.sharding import PartitionSpec as P

ROPE_BASE = 500000.0
EPSILON = 1e-05
FLOOR = -1e30
LANES = 128
NORM_ROWS = 64
GROUP_ROWS = 16
VMEM_BYTES = 16 * 1024 * 1024
CHEAP = pl.CostEstimate(flops=1000, bytes_accessed=1000, transcendentals=0)
IN_VMEM = pl.BlockSpec(memory_space=pltpu.VMEM)
IN_SMEM = pl.BlockSpec(memory_space=pltpu.SMEM)
IN_HBM = pl.BlockSpec(memory_space=pltpu.HBM)


def call(kernel, name, in_specs, out_shape, scratch_shapes=()):
    return pl.pallas_call(
        kernel,
        in_specs=in_specs,
        out_specs=jax.tree.map(lambda _: IN_VMEM, out_shape),
        out_shape=out_shape,
        scratch_shapes=scratch_shapes,
        compiler_params=pltpu.CompilerParams(vmem_limit_bytes=VMEM_BYTES),
        cost_estimate=CHEAP,
        name=name,
    )


def shape(dims, dtype=jnp.float32):
    return jax.ShapeDtypeStruct(dims, dtype)


def swap(value, axis, distance):
    count = lax.axis_size(axis)
    return lax.ppermute(value, axis, [(i, i ^ distance) for i in range(count)])


def after(value, *others):
    return lax.optimization_barrier((value, *others))[0]


def bits_below(count):
    return [1 << b for b in range(count.bit_length() - 1)]


def butterfly(value, axis, bits, join):
    for bit in bits:
        value = join(value, swap(value, axis, bit))
    return value


def by_core(value, bit_0, bit_1):
    count = lax.axis_size("ctx")
    bits = (bit_0, bit_1)
    pairs = [(i, i ^ bits[i % 2]) for i in range(count) if bits[i % 2]]
    return lax.ppermute(value, "ctx", pairs)


def send_first(own, partner):
    count = lax.axis_size("ctx")
    if count != 8:
        return [((d, d), swap(own, "ctx", d)) for d in range(2, count // 2)]
    return [((2, 4), by_core(own, 2, 4)), ((3, 5), by_core(partner, 2, 4))]


def share(blocks, *before):
    count = lax.axis_size("ctx")
    if count != 8:
        return []
    return [
        ((odd ^ 1, even ^ 1), swap(after(block, *before) if before else block, "ctx", 1))
        for (even, odd), block in blocks
    ]


def send_last(own, received):
    count = lax.axis_size("ctx")
    if count != 8:
        return [((d, d), swap(own, "ctx", d)) for d in range(count // 2, count)]
    return [((7, 7), by_core(received[0][1], 2, 4))]


def tables(placed, head_size):
    half_size = head_size // 2
    frequency = jnp.exp(
        jnp.arange(half_size, dtype=jnp.float32) * (-2.0 * math.log(ROPE_BASE) / head_size)
    )
    angles = placed[..., None] * frequency
    return jnp.cos(angles), jnp.sin(angles)


def turn(values, cosine, sine_part):
    half_size = values.shape[-1] // 2
    leading = values[:, :half_size]
    trailing = values[:, half_size:]
    return jnp.concatenate(
        (leading * cosine - trailing * sine_part, trailing * cosine + leading * sine_part), axis=-1
    )


def squares_kernel(team, row_count, place_ref, tokens_ref, out_ref, core_ref, request_ref, row_ref):
    values = tokens_ref[...]
    total = jnp.sum(values * values, axis=-1, keepdims=True)
    out_ref[...] = jnp.broadcast_to(total, out_ref.shape)
    place = place_ref[0]
    core_ref[...] = jnp.full(core_ref.shape, lax.rem(place, 2))
    request_ref[...] = jnp.full(request_ref.shape, lax.div(place, team))
    row_ref[...] = jnp.full(row_ref.shape, lax.rem(place, team) * row_count)


def norm_kernel(first, x_ref, gain_ref, *refs):
    out_refs, (held_ref, sems) = refs[:-2], refs[-2:]
    blocks, rows, width = out_refs[0].shape
    features = blocks * width
    groups = len(out_refs) * rows // GROUP_ROWS
    tiles = width // LANES

    def copy(g):
        return pltpu.make_async_copy(
            x_ref.at[pl.ds(first + g * GROUP_ROWS, GROUP_ROWS), :], held_ref.at[g], sems.at[g]
        )

    def factor_of(g):
        totals = [jnp.zeros((GROUP_ROWS, LANES), jnp.float32) for _ in range(4)]
        for j in range(blocks * tiles):
            values = held_ref[g, :, j * LANES : (j + 1) * LANES].astype(jnp.float32)
            totals[j % 4] = totals[j % 4] + values * values
        total = (totals[0] + totals[1]) + (totals[2] + totals[3])
        mean = jnp.sum(total, axis=-1, keepdims=True) / features
        return jnp.broadcast_to(lax.rsqrt(mean + EPSILON), (GROUP_ROWS, LANES))

    def scale(g, factor, out_ref, row):
        part = pl.ds(pl.multiple_of(row, GROUP_ROWS), GROUP_ROWS)
        for b in range(blocks):
            for j in range(tiles):
                lanes = slice(j * LANES, (j + 1) * LANES)
                from_lane = b * width + j * LANES
                values = held_ref[g, :, from_lane : from_lane + LANES].astype(jnp.float32)
                out_ref[b, part, lanes] = (values * factor * gain_ref[b, :, lanes]).astype(
                    jnp.bfloat16
                )

    for g in range(groups):
        copy(g).start()
    copy(0).wait()

    factor = factor_of(0)
    for i, out_ref in enumerate(out_refs):
        start = i * rows // GROUP_ROWS
        stop = min(start + rows // GROUP_ROWS, groups - 1)

        def step(g, factor, out_ref=out_ref, start=start):
            copy(g + 1).wait()
            following = factor_of(g + 1)
            scale(g, factor, out_ref, (g - start) * GROUP_ROWS)
            return following

        factor = lax.fori_loop(start, stop, step, factor)
    scale(groups - 1, factor, out_refs[-1], rows - GROUP_ROWS)


def normalise(hidden, gains, first, parts):
    blocks, _, width = gains.shape
    groups = parts * NORM_ROWS // GROUP_ROWS
    return call(
        functools.partial(norm_kernel, first),
        "normalise",
        [IN_HBM, IN_VMEM],
        (shape((blocks, NORM_ROWS, width), jnp.bfloat16),) * parts,
        [
            pltpu.VMEM((groups, GROUP_ROWS, blocks * width), jnp.bfloat16),
            pltpu.SemaphoreType.DMA((groups,)),
        ],
    )(pltpu.with_memory_space_constraint(hidden, pltpu.HBM), gains)


def query_kernel(
    features, place_ref, squares_ref, tokens_ref, gains_ref, query_ref, key_ref, value_ref, out_ref
):
    requests = tokens_ref.shape[0]
    factor = lax.rsqrt(squares_ref[:, :1] / features + EPSILON)
    normed = (tokens_ref[...] * factor * gains_ref[place_ref[0]]).astype(jnp.bfloat16)
    row = 0
    for weight_ref in (query_ref, key_ref, value_ref):
        part = jnp.dot(normed, weight_ref[...], preferred_element_type=jnp.float32)
        for h in range(weight_ref.shape[1] // LANES):
            for r in range(requests):
                out_ref[r, row : row + 1, :] = part[r : r + 1, h * LANES : (h + 1) * LANES]
            row += 1


def blocks_dot(distances, place, row_refs, block_refs, total):
    for (even, odd), block_ref in zip(distances, block_refs):
        distance = jnp.where(lax.rem(place, 2) == 0, even, odd)
        rows = jnp.concatenate([ref[place ^ distance] for ref in row_refs], axis=0)
        part = jnp.dot(rows, block_ref[...], preferred_element_type=jnp.float32)
        total = part if total is None else total + part
    return total


def project_kernel(distances, row_count, has_total, place_ref, *refs):
    rows, refs = refs[:row_count], refs[row_count:]
    total = refs[len(distances)][...] if has_total else None
    refs[-1][...] = blocks_dot(distances, place_ref[0], rows, refs, total)


def project(place, rows, blocks, total=None):
    extra = [] if total is None else [total]
    row_count = sum(r.shape[1] for r in rows)
    return call(
        functools.partial(project_kernel, [d for d, _ in blocks], len(rows), total is not None),
        "project",
        [IN_SMEM] + [IN_VMEM] * (len(rows) + len(blocks) + len(extra)),
        shape((row_count, LANES)),
    )(place, *rows, *[block for _, block in blocks], *extra)


def live_rows(dims, team, place, lengths_ref):
    rows = dims[1]
    within = lax.rem(place, team) * rows + lax.broadcasted_iota(jnp.int32, dims, 1)
    return within < lengths_ref[lax.div(place, team)]


def score_kernel(team, place_ref, lengths_ref, *refs):
    keys_ref, cos_ref, sin_ref, new_cos_ref, new_sin_ref, summed_ref = refs[:6]
    masked_ref, top_ref, self_ref = refs[6:]
    place = place_ref[0]
    request = lax.div(place, team)
    heads = masked_ref.shape[0]
    scale = 1.0 / math.sqrt(LANES)
    turned = turn(
        summed_ref[...], new_cos_ref[pl.ds(request, 1), :], new_sin_ref[pl.ds(request, 1), :]
    ).astype(jnp.bfloat16)
    queries = turned[:heads]
    self_key = turned[heads : heads + 1].astype(jnp.float32)
    self_scores = (
        jnp.sum(queries.astype(jnp.float32) * self_key, axis=-1, keepdims=True) * scale
    )
    keys = turn(keys_ref[...], cos_ref[...], sin_ref[...]).astype(jnp.bfloat16)
    scores = (
        lax.dot_general(
            queries, keys, (((1,), (1,)), ((), ())), preferred_element_type=jnp.float32
        )
        * scale
    )
    masked = jnp.where(live_rows(scores.shape, team, place, lengths_ref), scores, FLOOR)
    masked_ref[...] = masked
    top = jnp.maximum(jnp.max(masked, axis=-1, keepdims=True), self_scores)
    top_ref[...] = jnp.broadcast_to(top, top_ref.shape)
    self_ref[...] = jnp.broadcast_to(self_scores, self_ref.shape)


def weigh_kernel(distances, row_count, team, place_ref, lengths_ref, *refs):
    rows, refs = refs[:row_count], refs[row_count:]
    blocks, refs = refs[: len(distances)], refs[len(distances) :]
    total_ref, masked_ref, top_ref, self_ref, summed_ref, out_ref = refs
    place = place_ref[0]
    heads = masked_ref.shape[0]
    masked = masked_ref[...]
    top = top_ref[:, :1]
    live = live_rows(masked.shape, team, place, lengths_ref)
    weights = jnp.where(live, jnp.exp(masked - top), 0.0).astype(jnp.bfloat16)
    self_weight = jnp.exp(self_ref[...] - top_ref[...]).astype(jnp.bfloat16).astype(jnp.float32)
    self_weight = jnp.where(lax.rem(place, team) == 0, self_weight, 0.0)
    self_value = summed_ref[heads + 1 : heads + 2, :].astype(jnp.bfloat16).astype(jnp.float32)
    mass = jnp.sum(weights.astype(jnp.float32), axis=-1, keepdims=True) + self_weight
    values = blocks_dot(distances, place, rows, blocks, total_ref[...]).astype(jnp.bfloat16)
    accum = jnp.dot(weights, values, preferred_element_type=jnp.float32)
    out_ref[:, :LANES] = accum + self_weight * self_value
    out_ref[:, LANES:] = mass


def output_kernel(team, place_ref, mine_ref, other_ref, weight_ref, out_ref):
    request = lax.div(place_ref[0], team)
    heads = mine_ref.shape[0]
    attended = []
    for ref in (mine_ref, other_ref):
        attended.append(ref[:, :LANES] / ref[:, LANES:])
    first = jnp.where(request == 0, attended[0], attended[1]).astype(jnp.bfloat16)
    second = jnp.where(request == 0, attended[1], attended[0]).astype(jnp.bfloat16)
    both = jnp.concatenate(
        [
            jnp.concatenate((first[h : h + 1], second[h : h + 1]), axis=0)
            for h in range(heads)
        ],
        axis=1,
    )
    out_ref[...] = jnp.dot(both, weight_ref[...], preferred_element_type=jnp.float32)


def shards(
    new_tokens,
    ctx_hidden,
    norm_gain,
    query_weight,
    key_weight,
    value_weight,
    out_weight,
    lengths,
    positions,
):
    ctx_count = lax.axis_size("ctx")
    kv_count = lax.axis_size("kv")
    place = lax.axis_index("ctx").astype(jnp.int32)
    places = place.reshape(1)
    row_count, features = ctx_hidden.shape[1:]
    head_size = key_weight.shape[2]
    heads = query_weight.shape[2] // head_size
    requests, width = new_tokens.shape
    slot_count = row_count * ctx_count // requests
    team = slot_count // row_count
    assert requests == 2 and slot_count % row_count == 0 and row_count % NORM_ROWS == 0
    assert head_size == LANES
    gains = norm_gain.reshape(ctx_count, 1, width)

    split = ctx_count == 8
    chip_bits = bits_below(ctx_count)[1:]
    rows = []
    squares, core, own_request, first_row = call(
        functools.partial(squares_kernel, team, row_count),
        "squares",
        [IN_SMEM, IN_VMEM],
        (shape((requests, LANES)),) + (shape((1, LANES), jnp.int32),) * 3,
    )(places, new_tokens)

    def beside(received, sent, parts):
        first = len(rows) * NORM_ROWS
        rows.extend(normalise(after(ctx_hidden[0], sent), gains, first, parts))
        return after(received, rows[-1])

    def sum_chips(value, first_parts=0, second_parts=0):
        received = by_core(value, 4, 2)
        if first_parts:
            received = beside(received, value, first_parts)
        told = swap(received, "ctx", 1)
        opposite = by_core(told, 4, 2)
        if second_parts:
            opposite = beside(opposite, told, second_parts)
        over_x = jnp.where(core == 0, told, received)
        over_y = jnp.where(core == 0, received, told)
        return (value + over_x) + (over_y + opposite), told, received

    key_partner = swap(key_weight[0], "ctx", 1)
    value_partner = swap(value_weight[0], "ctx", 1)
    key_near = [((0, 0), key_weight[0]), ((1, 1), key_partner)]
    value_near = [((0, 0), value_weight[0]), ((1, 1), value_partner)]
    key_far = send_first(key_weight[0], key_partner)

    squares = squares + swap(squares, "ctx", 1)
    squares = after(squares, key_partner, value_partner)
    if split:
        squares, told, _ = sum_chips(squares, 2, row_count // NORM_ROWS - 3)
        key_shared = share(key_far, told)
        own_values = value_weight[0]
        squares = after(squares, key_far[1][1])
    else:
        key_shared = share(key_far)
        own_values = value_weight[0]
        squares = beside(squares, squares, row_count // NORM_ROWS)
        squares = butterfly(squares, "ctx", chip_bits, jnp.add)
    key_last = send_last(key_weight[0], key_shared)

    parts = call(
        functools.partial(query_kernel, features),
        "query_products",
        [IN_SMEM] + [IN_VMEM] * 6,
        shape((requests, heads + 2, head_size)),
    )(places, squares, new_tokens, gains, query_weight[0], key_weight[0], value_weight[0])
    parts = parts + swap(parts, "ctx", 1)
    parts_sent = parts
    value_far = send_first(own_values, value_partner)
    if split:
        parts, _, parts_sent = sum_chips(parts, 1)
        summed = jnp.where(own_request == 0, parts[0], parts[1])
    else:
        own_part = jnp.where(own_request == 0, parts[0], parts[1])
        other_part = jnp.where(own_request == 0, parts[1], parts[0])
        summed = own_part + swap(other_part, "ctx", team)
        summed = butterfly(summed, "ctx", chip_bits[:-1], jnp.add)

    key_total = project(places, rows, key_near)
    key_total = project(places, rows, key_far + key_shared, key_total)
    key_mid = key_total
    key_total = project(places, rows, key_last + share(key_last, key_total), key_total)

    late_row, late_places = lax.optimization_barrier((first_row, positions, key_mid))[:2]
    within = late_row[0, :1] + jnp.arange(row_count, dtype=jnp.int32)
    cosine, sine_part = tables(within.astype(jnp.float32), head_size)
    new_cosine, new_sine = tables(late_places.astype(jnp.float32), head_size)
    masked, top, self_scores = call(
        functools.partial(score_kernel, team),
        "scores",
        [IN_SMEM] * 2 + [IN_VMEM] * 6,
        (shape((heads, row_count)), shape((heads, LANES)), shape((heads, LANES))),
    )(places, lengths, key_total, cosine, sine_part, new_cosine, new_sine, summed)
    value_first = share(value_far[:1], parts_sent)
    value_last = send_last(own_values, value_first)
    value_first += value_far[:1]
    top = butterfly(top, "ctx", [1], jnp.maximum)
    top = after(top, *[block for _, block in value_far[1:]])
    near_top = top
    value_total = project(after(places, near_top), rows, value_near + value_first)
    if split:
        received = jnp.maximum(top, after(by_core(top, 4, 2), value_last[0][1], value_total))
        top = jnp.where(core == 0, swap(received, "ctx", 1), received)
    else:
        top = butterfly(top, "ctx", bits_below(team)[1:], jnp.maximum)
        received = top

    value_second = value_far[1:] + share(value_far[1:], near_top)
    value_total = project(places, rows, value_second, value_total)

    blocks = share(value_last, received)
    value_total = project(places, rows, value_last, value_total)
    packed = call(
        functools.partial(weigh_kernel, [d for d, _ in blocks], len(rows), team),
        "weighted_values",
        [IN_SMEM] * 2 + [IN_VMEM] * (len(rows) + len(blocks) + 5),
        shape((heads, 2 * head_size)),
    )(
        places,
        lengths,
        *rows,
        *[block for _, block in blocks],
        value_total,
        masked,
        top,
        self_scores,
        summed,
    )
    packed = butterfly(packed, "ctx", bits_below(team), jnp.add)
    other = swap(packed, "ctx", team)
    update = call(
        functools.partial(output_kernel, team),
        "output_products",
        [IN_SMEM] + [IN_VMEM] * 3,
        shape((requests, out_weight.shape[2])),
    )(places, packed, other, out_weight[0])
    return new_tokens + butterfly(update, "kv", bits_below(kv_count), jnp.add)


def solution(mesh):
    in_specs = (
        P(None, "ctx"),
        P(None, "ctx", None),
        P(),
        P(None, "ctx", "kv"),
        P(None, "ctx", "kv"),
        P(None, "ctx", "kv"),
        P(None, "kv", "ctx"),
        P(),
        P(),
    )
    out_specs = P(None, "ctx")
    return jax.shard_map(shards, mesh=mesh, in_specs=in_specs, out_specs=out_specs, check_vma=False)
```

```python
import functools
import math

import jax
import jax.numpy as jnp
from jax import lax
from jax.experimental import pallas as pl
from jax.experimental.pallas import tpu as pltpu
from jax.sharding import PartitionSpec as P

ROPE_BASE = 500000.0
EPSILON = 1e-05
FLOOR = -1e30
LANES = 128
NORM_ROWS = 64
GROUP_ROWS = 16
VMEM_BYTES = 16 * 1024 * 1024
CHEAP = pl.CostEstimate(flops=1000, bytes_accessed=1000, transcendentals=0)
IN_VMEM = pl.BlockSpec(memory_space=pltpu.VMEM)
IN_SMEM = pl.BlockSpec(memory_space=pltpu.SMEM)
IN_HBM = pl.BlockSpec(memory_space=pltpu.HBM)


def call(kernel, name, in_specs, out_shape, scratch_shapes=()):
    return pl.pallas_call(
        kernel,
        in_specs=in_specs,
        out_specs=jax.tree.map(lambda _: IN_VMEM, out_shape),
        out_shape=out_shape,
        scratch_shapes=scratch_shapes,
        compiler_params=pltpu.CompilerParams(vmem_limit_bytes=VMEM_BYTES),
        cost_estimate=CHEAP,
        name=name,
    )


def shape(dims, dtype=jnp.float32):
    return jax.ShapeDtypeStruct(dims, dtype)


def swap(value, axis, distance):
    count = lax.axis_size(axis)
    return lax.ppermute(value, axis, [(i, i ^ distance) for i in range(count)])


def after(value, *others):
    return lax.optimization_barrier((value, *others))[0]


def bits_below(count):
    return [1 << b for b in range(count.bit_length() - 1)]


def butterfly(value, axis, bits, join):
    for bit in bits:
        value = join(value, swap(value, axis, bit))
    return value


def by_core(value, bit_0, bit_1):
    count = lax.axis_size("ctx")
    bits = (bit_0, bit_1)
    pairs = [(i, i ^ bits[i % 2]) for i in range(count) if bits[i % 2]]
    return lax.ppermute(value, "ctx", pairs)


def send_first(own, partner):
    count = lax.axis_size("ctx")
    if count != 8:
        return [((d, d), swap(own, "ctx", d)) for d in range(2, count // 2)]
    return [((2, 4), by_core(own, 2, 4)), ((3, 5), by_core(partner, 2, 4))]


def share(blocks, *before):
    count = lax.axis_size("ctx")
    if count != 8:
        return []
    return [
        ((odd ^ 1, even ^ 1), swap(after(block, *before) if before else block, "ctx", 1))
        for (even, odd), block in blocks
    ]


def send_last(own, received):
    count = lax.axis_size("ctx")
    if count != 8:
        return [((d, d), swap(own, "ctx", d)) for d in range(count // 2, count)]
    return [((7, 7), by_core(received[0][1], 2, 4))]


def tables(placed, head_size):
    half_size = head_size // 2
    frequency = jnp.exp(
        jnp.arange(half_size, dtype=jnp.float32) * (-2.0 * math.log(ROPE_BASE) / head_size)
    )
    angles = placed[..., None] * frequency
    return jnp.cos(angles), jnp.sin(angles)


def turn(values, cosine, sine_part):
    half_size = values.shape[-1] // 2
    leading = values[:, :half_size]
    trailing = values[:, half_size:]
    return jnp.concatenate(
        (leading * cosine - trailing * sine_part, trailing * cosine + leading * sine_part), axis=-1
    )


def squares_kernel(team, row_count, place_ref, tokens_ref, out_ref, core_ref, request_ref, row_ref):
    values = tokens_ref[...]
    total = jnp.sum(values * values, axis=-1, keepdims=True)
    out_ref[...] = jnp.broadcast_to(total, out_ref.shape)
    place = place_ref[0]
    core_ref[...] = jnp.full(core_ref.shape, lax.rem(place, 2))
    request_ref[...] = jnp.full(request_ref.shape, lax.div(place, team))
    row_ref[...] = jnp.full(row_ref.shape, lax.rem(place, team) * row_count)


def norm_kernel(first, x_ref, gain_ref, *refs):
    out_refs, (held_ref, sems) = refs[:-2], refs[-2:]
    blocks, rows, width = out_refs[0].shape
    features = blocks * width
    groups = len(out_refs) * rows // GROUP_ROWS
    tiles = width // LANES

    def copy(g):
        return pltpu.make_async_copy(
            x_ref.at[pl.ds(first + g * GROUP_ROWS, GROUP_ROWS), :], held_ref.at[g], sems.at[g]
        )

    def factor_of(g):
        totals = [jnp.zeros((GROUP_ROWS, LANES), jnp.float32) for _ in range(4)]
        for j in range(blocks * tiles):
            values = held_ref[g, :, j * LANES : (j + 1) * LANES].astype(jnp.float32)
            totals[j % 4] = totals[j % 4] + values * values
        total = (totals[0] + totals[1]) + (totals[2] + totals[3])
        mean = jnp.sum(total, axis=-1, keepdims=True) / features
        return jnp.broadcast_to(lax.rsqrt(mean + EPSILON), (GROUP_ROWS, LANES))

    def scale(g, factor, out_ref, row):
        part = pl.ds(pl.multiple_of(row, GROUP_ROWS), GROUP_ROWS)
        for b in range(blocks):
            for j in range(tiles):
                lanes = slice(j * LANES, (j + 1) * LANES)
                from_lane = b * width + j * LANES
                values = held_ref[g, :, from_lane : from_lane + LANES].astype(jnp.float32)
                out_ref[b, part, lanes] = (values * factor * gain_ref[b, :, lanes]).astype(
                    jnp.bfloat16
                )

    for g in range(groups):
        copy(g).start()
    copy(0).wait()

    factor = factor_of(0)
    for i, out_ref in enumerate(out_refs):
        start = i * rows // GROUP_ROWS
        stop = min(start + rows // GROUP_ROWS, groups - 1)

        def step(g, factor, out_ref=out_ref, start=start):
            copy(g + 1).wait()
            following = factor_of(g + 1)
            scale(g, factor, out_ref, (g - start) * GROUP_ROWS)
            return following

        factor = lax.fori_loop(start, stop, step, factor)
    scale(groups - 1, factor, out_refs[-1], rows - GROUP_ROWS)


def normalise(hidden, gains, first, parts):
    blocks, _, width = gains.shape
    groups = parts * NORM_ROWS // GROUP_ROWS
    return call(
        functools.partial(norm_kernel, first),
        "normalise",
        [IN_HBM, IN_VMEM],
        (shape((blocks, NORM_ROWS, width), jnp.bfloat16),) * parts,
        [
            pltpu.VMEM((groups, GROUP_ROWS, blocks * width), jnp.bfloat16),
            pltpu.SemaphoreType.DMA((groups,)),
        ],
    )(pltpu.with_memory_space_constraint(hidden, pltpu.HBM), gains)


def query_kernel(
    features, place_ref, squares_ref, tokens_ref, gains_ref, query_ref, key_ref, value_ref, out_ref
):
    requests = tokens_ref.shape[0]
    factor = lax.rsqrt(squares_ref[:, :1] / features + EPSILON)
    normed = (tokens_ref[...] * factor * gains_ref[place_ref[0]]).astype(jnp.bfloat16)
    row = 0
    for weight_ref in (query_ref, key_ref, value_ref):
        part = jnp.dot(normed, weight_ref[...], preferred_element_type=jnp.float32)
        for h in range(weight_ref.shape[1] // LANES):
            for r in range(requests):
                out_ref[r, row : row + 1, :] = part[r : r + 1, h * LANES : (h + 1) * LANES]
            row += 1


def blocks_dot(distances, place, row_refs, block_refs, total):
    for (even, odd), block_ref in zip(distances, block_refs):
        distance = jnp.where(lax.rem(place, 2) == 0, even, odd)
        rows = jnp.concatenate([ref[place ^ distance] for ref in row_refs], axis=0)
        part = jnp.dot(rows, block_ref[...], preferred_element_type=jnp.float32)
        total = part if total is None else total + part
    return total


def project_kernel(distances, row_count, has_total, place_ref, *refs):
    rows, refs = refs[:row_count], refs[row_count:]
    total = refs[len(distances)][...] if has_total else None
    refs[-1][...] = blocks_dot(distances, place_ref[0], rows, refs, total)


def project(place, rows, blocks, total=None):
    extra = [] if total is None else [total]
    row_count = sum(r.shape[1] for r in rows)
    return call(
        functools.partial(project_kernel, [d for d, _ in blocks], len(rows), total is not None),
        "project",
        [IN_SMEM] + [IN_VMEM] * (len(rows) + len(blocks) + len(extra)),
        shape((row_count, LANES)),
    )(place, *rows, *[block for _, block in blocks], *extra)


def live_rows(dims, team, place, lengths_ref):
    rows = dims[1]
    within = lax.rem(place, team) * rows + lax.broadcasted_iota(jnp.int32, dims, 1)
    return within < lengths_ref[lax.div(place, team)]


def score_kernel(team, place_ref, lengths_ref, *refs):
    keys_ref, cos_ref, sin_ref, new_cos_ref, new_sin_ref, summed_ref = refs[:6]
    masked_ref, top_ref, self_ref = refs[6:]
    place = place_ref[0]
    request = lax.div(place, team)
    heads = masked_ref.shape[0]
    scale = 1.0 / math.sqrt(LANES)
    turned = turn(
        summed_ref[...], new_cos_ref[pl.ds(request, 1), :], new_sin_ref[pl.ds(request, 1), :]
    ).astype(jnp.bfloat16)
    queries = turned[:heads]
    self_key = turned[heads : heads + 1].astype(jnp.float32)
    self_scores = (
        jnp.sum(queries.astype(jnp.float32) * self_key, axis=-1, keepdims=True) * scale
    )
    keys = turn(keys_ref[...], cos_ref[...], sin_ref[...]).astype(jnp.bfloat16)
    scores = (
        lax.dot_general(
            queries, keys, (((1,), (1,)), ((), ())), preferred_element_type=jnp.float32
        )
        * scale
    )
    masked = jnp.where(live_rows(scores.shape, team, place, lengths_ref), scores, FLOOR)
    masked_ref[...] = masked
    top = jnp.maximum(jnp.max(masked, axis=-1, keepdims=True), self_scores)
    top_ref[...] = jnp.broadcast_to(top, top_ref.shape)
    self_ref[...] = jnp.broadcast_to(self_scores, self_ref.shape)


def weigh_kernel(distances, row_count, team, place_ref, lengths_ref, *refs):
    rows, refs = refs[:row_count], refs[row_count:]
    blocks, refs = refs[: len(distances)], refs[len(distances) :]
    total_ref, masked_ref, top_ref, self_ref, summed_ref, out_ref = refs
    place = place_ref[0]
    heads = masked_ref.shape[0]
    masked = masked_ref[...]
    top = top_ref[:, :1]
    live = live_rows(masked.shape, team, place, lengths_ref)
    weights = jnp.where(live, jnp.exp(masked - top), 0.0).astype(jnp.bfloat16)
    self_weight = jnp.exp(self_ref[...] - top_ref[...]).astype(jnp.bfloat16).astype(jnp.float32)
    self_weight = jnp.where(lax.rem(place, team) == 0, self_weight, 0.0)
    self_value = summed_ref[heads + 1 : heads + 2, :].astype(jnp.bfloat16).astype(jnp.float32)
    mass = jnp.sum(weights.astype(jnp.float32), axis=-1, keepdims=True) + self_weight
    values = blocks_dot(distances, place, rows, blocks, total_ref[...]).astype(jnp.bfloat16)
    accum = jnp.dot(weights, values, preferred_element_type=jnp.float32)
    out_ref[:, :LANES] = accum + self_weight * self_value
    out_ref[:, LANES:] = mass


def output_kernel(team, place_ref, mine_ref, other_ref, weight_ref, out_ref):
    request = lax.div(place_ref[0], team)
    heads = mine_ref.shape[0]
    attended = []
    for ref in (mine_ref, other_ref):
        attended.append(ref[:, :LANES] / ref[:, LANES:])
    first = jnp.where(request == 0, attended[0], attended[1]).astype(jnp.bfloat16)
    second = jnp.where(request == 0, attended[1], attended[0]).astype(jnp.bfloat16)
    both = jnp.concatenate(
        [
            jnp.concatenate((first[h : h + 1], second[h : h + 1]), axis=0)
            for h in range(heads)
        ],
        axis=1,
    )
    out_ref[...] = jnp.dot(both, weight_ref[...], preferred_element_type=jnp.float32)


def shards(
    new_tokens,
    ctx_hidden,
    norm_gain,
    query_weight,
    key_weight,
    value_weight,
    out_weight,
    lengths,
    positions,
):
    ctx_count = lax.axis_size("ctx")
    kv_count = lax.axis_size("kv")
    place = lax.axis_index("ctx").astype(jnp.int32)
    places = place.reshape(1)
    row_count, features = ctx_hidden.shape[1:]
    head_size = key_weight.shape[2]
    heads = query_weight.shape[2] // head_size
    requests, width = new_tokens.shape
    slot_count = row_count * ctx_count // requests
    team = slot_count // row_count
    assert requests == 2 and slot_count % row_count == 0 and row_count % NORM_ROWS == 0
    assert head_size == LANES
    gains = norm_gain.reshape(ctx_count, 1, width)

    split = ctx_count == 8
    chip_bits = bits_below(ctx_count)[1:]
    rows = []
    squares, core, own_request, first_row = call(
        functools.partial(squares_kernel, team, row_count),
        "squares",
        [IN_SMEM, IN_VMEM],
        (shape((requests, LANES)),) + (shape((1, LANES), jnp.int32),) * 3,
    )(places, new_tokens)

    def beside(received, sent, parts):
        first = len(rows) * NORM_ROWS
        rows.extend(normalise(after(ctx_hidden[0], sent), gains, first, parts))
        return after(received, rows[-1])

    def sum_chips(value, first_parts=0, second_parts=0):
        received = by_core(value, 4, 2)
        if first_parts:
            received = beside(received, value, first_parts)
        told = swap(received, "ctx", 1)
        opposite = by_core(told, 4, 2)
        if second_parts:
            opposite = beside(opposite, told, second_parts)
        over_x = jnp.where(core == 0, told, received)
        over_y = jnp.where(core == 0, received, told)
        return (value + over_x) + (over_y + opposite), told, received

    key_partner = swap(key_weight[0], "ctx", 1)
    value_partner = swap(value_weight[0], "ctx", 1)
    key_near = [((0, 0), key_weight[0]), ((1, 1), key_partner)]
    value_near = [((0, 0), value_weight[0]), ((1, 1), value_partner)]
    key_far = send_first(key_weight[0], key_partner)

    squares = squares + swap(squares, "ctx", 1)
    squares = after(squares, key_partner, value_partner)
    if split:
        squares, told, _ = sum_chips(squares, 2, row_count // NORM_ROWS - 3)
        key_shared = share(key_far, told)
        own_values = value_weight[0]
        squares = after(squares, key_far[1][1])
    else:
        key_shared = share(key_far)
        own_values = value_weight[0]
        squares = beside(squares, squares, row_count // NORM_ROWS)
        squares = butterfly(squares, "ctx", chip_bits, jnp.add)
    key_last = send_last(key_weight[0], key_shared)

    parts = call(
        functools.partial(query_kernel, features),
        "query_products",
        [IN_SMEM] + [IN_VMEM] * 6,
        shape((requests, heads + 2, head_size)),
    )(places, squares, new_tokens, gains, query_weight[0], key_weight[0], value_weight[0])
    parts = parts + swap(parts, "ctx", 1)
    parts_sent = parts
    value_far = send_first(own_values, value_partner)
    if split:
        parts, _, parts_sent = sum_chips(parts, 1)
        summed = jnp.where(own_request == 0, parts[0], parts[1])
    else:
        own_part = jnp.where(own_request == 0, parts[0], parts[1])
        other_part = jnp.where(own_request == 0, parts[1], parts[0])
        summed = own_part + swap(other_part, "ctx", team)
        summed = butterfly(summed, "ctx", chip_bits[:-1], jnp.add)

    key_total = project(places, rows, key_near)
    key_mid = key_total
    key_total = project(places, rows, key_far + key_shared, key_total)
    key_total = project(places, rows, key_last + share(key_last, key_total), key_total)

    late_row, late_places = lax.optimization_barrier((first_row, positions, key_mid))[:2]
    within = late_row[0, :1] + jnp.arange(row_count, dtype=jnp.int32)
    cosine, sine_part = tables(within.astype(jnp.float32), head_size)
    new_cosine, new_sine = tables(positions.astype(jnp.float32), head_size)
    masked, top, self_scores = call(
        functools.partial(score_kernel, team),
        "scores",
        [IN_SMEM] * 2 + [IN_VMEM] * 6,
        (shape((heads, row_count)), shape((heads, LANES)), shape((heads, LANES))),
    )(places, lengths, key_total, cosine, sine_part, new_cosine, new_sine, summed)
    value_first = share(value_far[:1], parts_sent)
    value_last = send_last(own_values, value_first)
    value_first += value_far[:1]
    top = butterfly(top, "ctx", [1], jnp.maximum)
    top = after(top, *[block for _, block in value_far[1:]])
    near_top = top
    value_total = project(after(places, near_top), rows, value_near + value_first)
    if split:
        received = jnp.maximum(top, after(by_core(top, 4, 2), value_last[0][1], value_total))
        top = jnp.where(core == 0, swap(received, "ctx", 1), received)
    else:
        top = butterfly(top, "ctx", bits_below(team)[1:], jnp.maximum)
        received = top

    value_second = value_far[1:] + share(value_far[1:], near_top)
    value_total = project(places, rows, value_second, value_total)

    blocks = share(value_last, received)
    value_total = project(places, rows, value_last, value_total)
    packed = call(
        functools.partial(weigh_kernel, [d for d, _ in blocks], len(rows), team),
        "weighted_values",
        [IN_SMEM] * 2 + [IN_VMEM] * (len(rows) + len(blocks) + 5),
        shape((heads, 2 * head_size)),
    )(
        places,
        lengths,
        *rows,
        *[block for _, block in blocks],
        value_total,
        masked,
        top,
        self_scores,
        summed,
    )
    packed = butterfly(packed, "ctx", bits_below(team), jnp.add)
    other = swap(packed, "ctx", team)
    update = call(
        functools.partial(output_kernel, team),
        "output_products",
        [IN_SMEM] + [IN_VMEM] * 3,
        shape((requests, out_weight.shape[2])),
    )(places, packed, other, out_weight[0])
    return new_tokens + butterfly(update, "kv", bits_below(kv_count), jnp.add)


def solution(mesh):
    in_specs = (
        P(None, "ctx"),
        P(None, "ctx", None),
        P(),
        P(None, "ctx", "kv"),
        P(None, "ctx", "kv"),
        P(None, "ctx", "kv"),
        P(None, "kv", "ctx"),
        P(),
        P(),
    )
    out_specs = P(None, "ctx")
    return jax.shard_map(shards, mesh=mesh, in_specs=in_specs, out_specs=out_specs, check_vma=False)
```

```python
import functools
import math

import jax
import jax.numpy as jnp
from jax import lax
from jax.experimental import pallas as pl
from jax.experimental.pallas import tpu as pltpu
from jax.sharding import PartitionSpec as P

ROPE_BASE = 500000.0
EPSILON = 1e-05
FLOOR = -1e30
LANES = 128
NORM_ROWS = 64
GROUP_ROWS = 16
VMEM_BYTES = 16 * 1024 * 1024
CHEAP = pl.CostEstimate(flops=1000, bytes_accessed=1000, transcendentals=0)
IN_VMEM = pl.BlockSpec(memory_space=pltpu.VMEM)
IN_SMEM = pl.BlockSpec(memory_space=pltpu.SMEM)
IN_HBM = pl.BlockSpec(memory_space=pltpu.HBM)


def call(kernel, name, in_specs, out_shape, scratch_shapes=()):
    return pl.pallas_call(
        kernel,
        in_specs=in_specs,
        out_specs=jax.tree.map(lambda _: IN_VMEM, out_shape),
        out_shape=out_shape,
        scratch_shapes=scratch_shapes,
        compiler_params=pltpu.CompilerParams(vmem_limit_bytes=VMEM_BYTES),
        cost_estimate=CHEAP,
        name=name,
    )


def shape(dims, dtype=jnp.float32):
    return jax.ShapeDtypeStruct(dims, dtype)


def swap(value, axis, distance):
    count = lax.axis_size(axis)
    return lax.ppermute(value, axis, [(i, i ^ distance) for i in range(count)])


def after(value, *others):
    return lax.optimization_barrier((value, *others))[0]


def bits_below(count):
    return [1 << b for b in range(count.bit_length() - 1)]


def butterfly(value, axis, bits, join):
    for bit in bits:
        value = join(value, swap(value, axis, bit))
    return value


def by_core(value, bit_0, bit_1):
    count = lax.axis_size("ctx")
    bits = (bit_0, bit_1)
    pairs = [(i, i ^ bits[i % 2]) for i in range(count) if bits[i % 2]]
    return lax.ppermute(value, "ctx", pairs)


def send_first(own, partner):
    count = lax.axis_size("ctx")
    if count != 8:
        return [((d, d), swap(own, "ctx", d)) for d in range(2, count // 2)]
    return [((2, 4), by_core(own, 2, 4)), ((3, 5), by_core(partner, 2, 4))]


def share(blocks, *before):
    count = lax.axis_size("ctx")
    if count != 8:
        return []
    return [
        ((odd ^ 1, even ^ 1), swap(after(block, *before) if before else block, "ctx", 1))
        for (even, odd), block in blocks
    ]


def send_last(own, received):
    count = lax.axis_size("ctx")
    if count != 8:
        return [((d, d), swap(own, "ctx", d)) for d in range(count // 2, count)]
    return [((7, 7), by_core(received[0][1], 2, 4))]


def tables(placed, head_size):
    half_size = head_size // 2
    frequency = jnp.exp(
        jnp.arange(half_size, dtype=jnp.float32) * (-2.0 * math.log(ROPE_BASE) / head_size)
    )
    angles = placed[..., None] * frequency
    return jnp.cos(angles), jnp.sin(angles)


def turn(values, cosine, sine_part):
    half_size = values.shape[-1] // 2
    leading = values[:, :half_size]
    trailing = values[:, half_size:]
    return jnp.concatenate(
        (leading * cosine - trailing * sine_part, trailing * cosine + leading * sine_part), axis=-1
    )


def squares_kernel(team, row_count, place_ref, tokens_ref, out_ref, core_ref, request_ref, row_ref):
    values = tokens_ref[...]
    total = jnp.sum(values * values, axis=-1, keepdims=True)
    out_ref[...] = jnp.broadcast_to(total, out_ref.shape)
    place = place_ref[0]
    core_ref[...] = jnp.full(core_ref.shape, lax.rem(place, 2))
    request_ref[...] = jnp.full(request_ref.shape, lax.div(place, team))
    row_ref[...] = jnp.full(row_ref.shape, lax.rem(place, team) * row_count)


def norm_kernel(first, x_ref, gain_ref, *refs):
    out_refs, (held_ref, sems) = refs[:-2], refs[-2:]
    blocks, rows, width = out_refs[0].shape
    features = blocks * width
    groups = len(out_refs) * rows // GROUP_ROWS
    tiles = width // LANES

    def copy(g):
        return pltpu.make_async_copy(
            x_ref.at[pl.ds(first + g * GROUP_ROWS, GROUP_ROWS), :], held_ref.at[g], sems.at[g]
        )

    def factor_of(g):
        totals = [jnp.zeros((GROUP_ROWS, LANES), jnp.float32) for _ in range(4)]
        for j in range(blocks * tiles):
            values = held_ref[g, :, j * LANES : (j + 1) * LANES].astype(jnp.float32)
            totals[j % 4] = totals[j % 4] + values * values
        total = (totals[0] + totals[1]) + (totals[2] + totals[3])
        mean = jnp.sum(total, axis=-1, keepdims=True) / features
        return jnp.broadcast_to(lax.rsqrt(mean + EPSILON), (GROUP_ROWS, LANES))

    def scale(g, factor, out_ref, row):
        part = pl.ds(pl.multiple_of(row, GROUP_ROWS), GROUP_ROWS)
        for b in range(blocks):
            for j in range(tiles):
                lanes = slice(j * LANES, (j + 1) * LANES)
                from_lane = b * width + j * LANES
                values = held_ref[g, :, from_lane : from_lane + LANES].astype(jnp.float32)
                out_ref[b, part, lanes] = (values * factor * gain_ref[b, :, lanes]).astype(
                    jnp.bfloat16
                )

    for g in range(groups):
        copy(g).start()
    copy(0).wait()

    factor = factor_of(0)
    for i, out_ref in enumerate(out_refs):
        start = i * rows // GROUP_ROWS
        stop = min(start + rows // GROUP_ROWS, groups - 1)

        def step(g, factor, out_ref=out_ref, start=start):
            copy(g + 1).wait()
            following = factor_of(g + 1)
            scale(g, factor, out_ref, (g - start) * GROUP_ROWS)
            return following

        factor = lax.fori_loop(start, stop, step, factor)
    scale(groups - 1, factor, out_refs[-1], rows - GROUP_ROWS)


def normalise(hidden, gains, first, parts):
    blocks, _, width = gains.shape
    groups = parts * NORM_ROWS // GROUP_ROWS
    return call(
        functools.partial(norm_kernel, first),
        "normalise",
        [IN_HBM, IN_VMEM],
        (shape((blocks, NORM_ROWS, width), jnp.bfloat16),) * parts,
        [
            pltpu.VMEM((groups, GROUP_ROWS, blocks * width), jnp.bfloat16),
            pltpu.SemaphoreType.DMA((groups,)),
        ],
    )(pltpu.with_memory_space_constraint(hidden, pltpu.HBM), gains)


def query_kernel(
    features, place_ref, squares_ref, tokens_ref, gains_ref, query_ref, key_ref, value_ref, out_ref
):
    requests = tokens_ref.shape[0]
    factor = lax.rsqrt(squares_ref[:, :1] / features + EPSILON)
    normed = (tokens_ref[...] * factor * gains_ref[place_ref[0]]).astype(jnp.bfloat16)
    row = 0
    for weight_ref in (query_ref, key_ref, value_ref):
        part = jnp.dot(normed, weight_ref[...], preferred_element_type=jnp.float32)
        for h in range(weight_ref.shape[1] // LANES):
            for r in range(requests):
                out_ref[r, row : row + 1, :] = part[r : r + 1, h * LANES : (h + 1) * LANES]
            row += 1


def blocks_dot(distances, place, row_refs, block_refs, total):
    for (even, odd), block_ref in zip(distances, block_refs):
        distance = jnp.where(lax.rem(place, 2) == 0, even, odd)
        rows = jnp.concatenate([ref[place ^ distance] for ref in row_refs], axis=0)
        part = jnp.dot(rows, block_ref[...], preferred_element_type=jnp.float32)
        total = part if total is None else total + part
    return total


def project_kernel(distances, row_count, has_total, place_ref, *refs):
    rows, refs = refs[:row_count], refs[row_count:]
    total = refs[len(distances)][...] if has_total else None
    refs[-1][...] = blocks_dot(distances, place_ref[0], rows, refs, total)


def project(place, rows, blocks, total=None):
    extra = [] if total is None else [total]
    row_count = sum(r.shape[1] for r in rows)
    return call(
        functools.partial(project_kernel, [d for d, _ in blocks], len(rows), total is not None),
        "project",
        [IN_SMEM] + [IN_VMEM] * (len(rows) + len(blocks) + len(extra)),
        shape((row_count, LANES)),
    )(place, *rows, *[block for _, block in blocks], *extra)


def live_rows(dims, team, place, lengths_ref):
    rows = dims[1]
    within = lax.rem(place, team) * rows + lax.broadcasted_iota(jnp.int32, dims, 1)
    return within < lengths_ref[lax.div(place, team)]


def score_kernel(team, place_ref, lengths_ref, *refs):
    keys_ref, cos_ref, sin_ref, new_cos_ref, new_sin_ref, summed_ref = refs[:6]
    masked_ref, top_ref, self_ref = refs[6:]
    place = place_ref[0]
    request = lax.div(place, team)
    heads = masked_ref.shape[0]
    scale = 1.0 / math.sqrt(LANES)
    turned = turn(
        summed_ref[...], new_cos_ref[pl.ds(request, 1), :], new_sin_ref[pl.ds(request, 1), :]
    ).astype(jnp.bfloat16)
    queries = turned[:heads]
    self_key = turned[heads : heads + 1].astype(jnp.float32)
    self_scores = (
        jnp.sum(queries.astype(jnp.float32) * self_key, axis=-1, keepdims=True) * scale
    )
    keys = turn(keys_ref[...], cos_ref[...], sin_ref[...]).astype(jnp.bfloat16)
    scores = (
        lax.dot_general(
            queries, keys, (((1,), (1,)), ((), ())), preferred_element_type=jnp.float32
        )
        * scale
    )
    masked = jnp.where(live_rows(scores.shape, team, place, lengths_ref), scores, FLOOR)
    masked_ref[...] = masked
    top = jnp.maximum(jnp.max(masked, axis=-1, keepdims=True), self_scores)
    top_ref[...] = jnp.broadcast_to(top, top_ref.shape)
    self_ref[...] = jnp.broadcast_to(self_scores, self_ref.shape)


def weigh_kernel(distances, row_count, team, place_ref, lengths_ref, *refs):
    rows, refs = refs[:row_count], refs[row_count:]
    blocks, refs = refs[: len(distances)], refs[len(distances) :]
    total_ref, masked_ref, top_ref, self_ref, summed_ref, out_ref = refs
    place = place_ref[0]
    heads = masked_ref.shape[0]
    masked = masked_ref[...]
    top = top_ref[:, :1]
    live = live_rows(masked.shape, team, place, lengths_ref)
    weights = jnp.where(live, jnp.exp(masked - top), 0.0).astype(jnp.bfloat16)
    self_weight = jnp.exp(self_ref[...] - top_ref[...]).astype(jnp.bfloat16).astype(jnp.float32)
    self_weight = jnp.where(lax.rem(place, team) == 0, self_weight, 0.0)
    self_value = summed_ref[heads + 1 : heads + 2, :].astype(jnp.bfloat16).astype(jnp.float32)
    mass = jnp.sum(weights.astype(jnp.float32), axis=-1, keepdims=True) + self_weight
    values = blocks_dot(distances, place, rows, blocks, total_ref[...]).astype(jnp.bfloat16)
    accum = jnp.dot(weights, values, preferred_element_type=jnp.float32)
    out_ref[:, :LANES] = accum + self_weight * self_value
    out_ref[:, LANES:] = mass


def output_kernel(team, place_ref, mine_ref, other_ref, weight_ref, out_ref):
    request = lax.div(place_ref[0], team)
    heads = mine_ref.shape[0]
    attended = []
    for ref in (mine_ref, other_ref):
        attended.append(ref[:, :LANES] / ref[:, LANES:])
    first = jnp.where(request == 0, attended[0], attended[1]).astype(jnp.bfloat16)
    second = jnp.where(request == 0, attended[1], attended[0]).astype(jnp.bfloat16)
    both = jnp.concatenate(
        [
            jnp.concatenate((first[h : h + 1], second[h : h + 1]), axis=0)
            for h in range(heads)
        ],
        axis=1,
    )
    out_ref[...] = jnp.dot(both, weight_ref[...], preferred_element_type=jnp.float32)


def shards(
    new_tokens,
    ctx_hidden,
    norm_gain,
    query_weight,
    key_weight,
    value_weight,
    out_weight,
    lengths,
    positions,
):
    ctx_count = lax.axis_size("ctx")
    kv_count = lax.axis_size("kv")
    place = lax.axis_index("ctx").astype(jnp.int32)
    places = place.reshape(1)
    row_count, features = ctx_hidden.shape[1:]
    head_size = key_weight.shape[2]
    heads = query_weight.shape[2] // head_size
    requests, width = new_tokens.shape
    slot_count = row_count * ctx_count // requests
    team = slot_count // row_count
    assert requests == 2 and slot_count % row_count == 0 and row_count % NORM_ROWS == 0
    assert head_size == LANES
    gains = norm_gain.reshape(ctx_count, 1, width)

    split = ctx_count == 8
    chip_bits = bits_below(ctx_count)[1:]
    rows = []
    squares, core, own_request, first_row = call(
        functools.partial(squares_kernel, team, row_count),
        "squares",
        [IN_SMEM, IN_VMEM],
        (shape((requests, LANES)),) + (shape((1, LANES), jnp.int32),) * 3,
    )(places, new_tokens)

    def beside(received, sent, parts):
        first = len(rows) * NORM_ROWS
        rows.extend(normalise(after(ctx_hidden[0], sent), gains, first, parts))
        return after(received, rows[-1])

    def sum_chips(value, first_parts=0, second_parts=0):
        received = by_core(value, 4, 2)
        if first_parts:
            received = beside(received, value, first_parts)
        told = swap(received, "ctx", 1)
        opposite = by_core(told, 4, 2)
        if second_parts:
            opposite = beside(opposite, told, second_parts)
        over_x = jnp.where(core == 0, told, received)
        over_y = jnp.where(core == 0, received, told)
        return (value + over_x) + (over_y + opposite), told, received

    key_partner = swap(key_weight[0], "ctx", 1)
    value_partner = swap(value_weight[0], "ctx", 1)
    key_near = [((0, 0), key_weight[0]), ((1, 1), key_partner)]
    value_near = [((0, 0), value_weight[0]), ((1, 1), value_partner)]
    key_far = send_first(key_weight[0], key_partner)

    squares = squares + swap(squares, "ctx", 1)
    squares = after(squares, key_partner, value_partner)
    if split:
        squares, told, _ = sum_chips(squares, 2, row_count // NORM_ROWS - 3)
        key_shared = share(key_far, told)
        own_values = value_weight[0]
        squares = after(squares, key_far[1][1])
    else:
        key_shared = share(key_far)
        own_values = value_weight[0]
        squares = beside(squares, squares, row_count // NORM_ROWS)
        squares = butterfly(squares, "ctx", chip_bits, jnp.add)
    key_last = send_last(key_weight[0], key_shared)

    parts = call(
        functools.partial(query_kernel, features),
        "query_products",
        [IN_SMEM] + [IN_VMEM] * 6,
        shape((requests, heads + 2, head_size)),
    )(places, squares, new_tokens, gains, query_weight[0], key_weight[0], value_weight[0])
    parts = parts + swap(parts, "ctx", 1)
    parts_sent = parts
    value_far = send_first(own_values, value_partner)
    if split:
        parts, _, parts_sent = sum_chips(parts, 1)
        summed = jnp.where(own_request == 0, parts[0], parts[1])
    else:
        own_part = jnp.where(own_request == 0, parts[0], parts[1])
        other_part = jnp.where(own_request == 0, parts[1], parts[0])
        summed = own_part + swap(other_part, "ctx", team)
        summed = butterfly(summed, "ctx", chip_bits[:-1], jnp.add)

    key_total = project(places, rows, key_near)
    key_mid = key_total
    key_total = project(places, rows, key_far + key_shared, key_total)
    key_total = project(places, rows, key_last + share(key_last, key_total), key_total)

    late_row, late_places = lax.optimization_barrier((first_row, positions, key_mid))[:2]
    within = late_row[0, :1] + jnp.arange(row_count, dtype=jnp.int32)
    cosine, sine_part = tables(within.astype(jnp.float32), head_size)
    new_cosine, new_sine = tables(positions.astype(jnp.float32), head_size)
    masked, top, self_scores = call(
        functools.partial(score_kernel, team),
        "scores",
        [IN_SMEM] * 2 + [IN_VMEM] * 6,
        (shape((heads, row_count)), shape((heads, LANES)), shape((heads, LANES))),
    )(places, lengths, key_total, cosine, sine_part, new_cosine, new_sine, summed)
    value_first = share(value_far[:1], parts_sent)
    value_last = send_last(own_values, value_first)
    value_first += value_far[:1]
    top = butterfly(top, "ctx", [1], jnp.maximum)
    top = after(top, *[block for _, block in value_far[1:]])
    near_top = top
    value_total = project(after(places, near_top), rows, value_near + value_first)
    if split:
        received = jnp.maximum(top, after(by_core(top, 4, 2), value_last[0][1], value_total))
        told = swap(received, "ctx", 1)
    else:
        top = butterfly(top, "ctx", bits_below(team)[1:], jnp.maximum)
        received = top

    value_second = value_far[1:] + share(value_far[1:], near_top)
    value_total = project(places, rows, value_second, value_total)

    blocks = share(value_last, received)
    value_total = project(places, rows, value_last, value_total)
    if split:
        top = jnp.where(core == 0, after(told, value_total), received)
    packed = call(
        functools.partial(weigh_kernel, [d for d, _ in blocks], len(rows), team),
        "weighted_values",
        [IN_SMEM] * 2 + [IN_VMEM] * (len(rows) + len(blocks) + 5),
        shape((heads, 2 * head_size)),
    )(
        places,
        lengths,
        *rows,
        *[block for _, block in blocks],
        value_total,
        masked,
        top,
        self_scores,
        summed,
    )
    packed = butterfly(packed, "ctx", bits_below(team), jnp.add)
    other = swap(packed, "ctx", team)
    update = call(
        functools.partial(output_kernel, team),
        "output_products",
        [IN_SMEM] + [IN_VMEM] * 3,
        shape((requests, out_weight.shape[2])),
    )(places, packed, other, out_weight[0])
    return new_tokens + butterfly(update, "kv", bits_below(kv_count), jnp.add)


def solution(mesh):
    in_specs = (
        P(None, "ctx"),
        P(None, "ctx", None),
        P(),
        P(None, "ctx", "kv"),
        P(None, "ctx", "kv"),
        P(None, "ctx", "kv"),
        P(None, "kv", "ctx"),
        P(),
        P(),
    )
    out_specs = P(None, "ctx")
    return jax.shard_map(shards, mesh=mesh, in_specs=in_specs, out_specs=out_specs, check_vma=False)
```
